512 devices in a mesh: dom: 128 (over y, z, core), rep: 4 (over x).
Axes of the slice: x: 4, y: 8, z: 8, core: 2. Of those that a mesh axis runs over, the one named last changes fastest.
Arguments:
- events: bfloat16 [4, 32768, 128], P('rep', 'dom'), may hold values from -6 to 6
- perm: int32 [4, 32768], P('rep', 'dom'), may hold values from 0 to 32767, as said below
- w_enc: bfloat16 [128, 256], replicated, may hold values from -0.5 to 0.5
- w_one: bfloat16 [256, 256], replicated, may hold values from -0.375 to 0.375
- w_two: bfloat16 [256, 256], replicated, may hold values from -0.375 to 0.375
- slot_blocks: int32 [4, 1280, 2], P('rep', 'dom'), may hold values from 0 to 255, as said below
- live_count: int32 [4, 128], P('rep', 'dom'), may hold values from 1 to 10, as said below
- block_counts: int32 [4, 1280, 128, 128], P('rep', 'dom'), may hold values from 0 to 3
- out_grad: bfloat16 [4, 32768, 256], P('rep', 'dom'), may hold values from -6 to 6
Outputs:
- embed: bfloat16 [4, 32768, 256], P('rep', 'dom')
- grad_enc: float32 [128, 256], replicated
- grad_one: float32 [256, 256], replicated
- grad_two: float32 [256, 256], replicated
The draws below stay inside these ranges and needn't reach their ends.
Inputs may be any that keep to these rules, and one draw needn't show every extreme that they name: Within each batch perm names every account once, and the 256 time rows of each device hold exactly 256 // 128 accounts of each partition; account a belongs to partition a // 256. `slot_blocks`: slot s belongs to partition p = s // 10; its row block is one of p's 2 blocks; its column block is one of p's blocks, or the last block of partition p - 1, or the first block of partition p + 1, cyclically over partitions. Two slots may name the same pair; their counts add. `live_count`: in every batch some partition uses all 10 slots.
All inputs are finite; a program needn't handle non-finite values.
Results may differ from the reference program's by a relative error of at most 0.0075.
Values may be sent and summed in bfloat16 or wider, within the bound.
A program may use at most 64 MiB of HBM per device.

```python
import math
import jax
import jax.numpy as jnp
from jax import lax

BLOCK = 128
FE = 128
H = 256
BLK_DEV = 2
NB_DEV = 10
ACC_DEV = 256
ACCOUNTS = 32768
N_DOM = 128
N_REP = 4


def draw_perm(key, part):
    key = jax.random.fold_in(key, 11)
    per_group = ACC_DEV // N_DOM

    def one_batch(batch_key):
        first_key, second_key = jax.random.split(batch_key)
        local = jax.vmap(lambda item_key: jax.random.permutation(item_key, ACC_DEV))(jax.random.split(first_key, N_DOM))
        global_ids = local + (jnp.arange(N_DOM, dtype=jnp.int32) * ACC_DEV)[:, None]
        grouped = global_ids.reshape(N_DOM, N_DOM, per_group).transpose(1, 0, 2).reshape(N_DOM, ACC_DEV)
        shuffled = jax.vmap(lambda item_key, row: jax.random.permutation(item_key, row))(jax.random.split(second_key, N_DOM), grouped)
        return shuffled.reshape(-1)
    return jax.vmap(one_batch)(jax.random.split(key, N_REP)).astype(jnp.int32)


def draw_slot_blocks(key, part):
    key = jax.random.fold_in(key, 12)
    key_row, key_kind, key_inner = jax.random.split(key, 3)
    shape = (N_REP, NB_DEV * N_DOM)
    owner = (jnp.arange(NB_DEV * N_DOM, dtype=jnp.int32) // NB_DEV)[None, :]
    row_block = owner * BLK_DEV + jax.random.randint(key_row, shape, 0, BLK_DEV)
    kind = jax.random.randint(key_kind, shape, 0, 4)
    inner = jax.random.randint(key_inner, shape, 0, BLK_DEV)
    own_block = owner * BLK_DEV + inner
    prev_block = (owner - 1) % N_DOM * BLK_DEV + BLK_DEV - 1
    next_block = (owner + 1) % N_DOM * BLK_DEV
    col_block = jnp.where(kind < 2, own_block, jnp.where(kind == 2, prev_block, next_block))
    return jnp.stack([row_block, col_block], axis=-1).astype(jnp.int32)


def draw_live_count(key, part):
    key = jax.random.fold_in(key, 13)
    key_level, key_full = jax.random.split(key)
    levels = jax.random.randint(key_level, (N_REP, N_DOM), 0, 4)
    full_at = jax.random.randint(key_full, (N_REP, 1), 0, N_DOM)
    levels = jnp.where(jnp.arange(N_DOM, dtype=jnp.int32)[None, :] == full_at, 0, levels)
    counted = jnp.right_shift(jnp.full((N_REP, N_DOM), NB_DEV, jnp.int32), levels)
    return jnp.maximum(1, counted).astype(jnp.int32)


def draw_block_counts(key, part):
    key = jax.random.fold_in(key, 14)
    key_where, key_value = jax.random.split(key)
    shape = (N_REP, NB_DEV * N_DOM, BLOCK, BLOCK)
    present = jax.random.randint(key_where, shape, 0, 16) == 0
    values = jax.random.randint(key_value, shape, 1, 4)
    return jnp.where(present, values, 0).astype(jnp.int32)


def level_of(stream_key, shape, pieces, low, high):
    loudness = 1.0
    for dim, parts in pieces:
        steps = jax.random.uniform(jax.random.fold_in(jax.random.fold_in(stream_key, 6), dim), (parts,), jnp.float32, low / len(pieces), high / len(pieces))
        loudness = loudness * jnp.repeat(jnp.exp(steps), shape[dim] // parts).reshape((-1,) + (1,) * (len(shape) - 1 - dim))
    return loudness


def normal_values(rng, dims, width, bound, cuts=(), held_as=jnp.bfloat16):
    gain = level_of(rng, dims, cuts, -0.22, 0.18) if cuts else 1.0
    drawn = jax.random.normal(rng, dims, jnp.float32) * width * gain
    return jnp.minimum(jnp.maximum(drawn, -bound), bound).astype(held_as)


def setup_inputs(seed: int = 0) -> dict:
    seeds = jax.random.split(jax.random.key(seed), 10)
    events = normal_values(seeds[0], (N_REP, ACCOUNTS, FE), 1.0, 6.0, ((0, 4), (1, 128)))
    perm = draw_perm(jax.random.fold_in(seeds[9], 71), 0)
    w_enc = normal_values(seeds[2], (FE, H), FE ** -0.5, 0.5)
    w_one = normal_values(seeds[3], (H, H), H ** -0.5, 0.375)
    w_two = normal_values(seeds[4], (H, H), H ** -0.5, 0.375)
    slot_blocks = draw_slot_blocks(jax.random.fold_in(seeds[9], 71), 0)
    live_count = draw_live_count(jax.random.fold_in(seeds[9], 71), 0)
    block_counts = draw_block_counts(jax.random.fold_in(seeds[9], 71), 0)
    out_grad = normal_values(seeds[8], (N_REP, ACCOUNTS, H), 1.0, 6.0, ((0, 4), (1, 128)))
    return dict(events=events, perm=perm, w_enc=w_enc, w_one=w_one, w_two=w_two, slot_blocks=slot_blocks, live_count=live_count, block_counts=block_counts, out_grad=out_grad)


loop_weight = 4.0

def silu_slope(value):
    sig = jax.nn.sigmoid(value)
    return sig * (1.0 + value * (1.0 - sig))

def reference(events, perm, w_enc, w_one, w_two, slot_blocks, live_count, block_counts, out_grad):
    accounts = ACC_DEV * N_DOM
    nblocks = BLK_DEV * N_DOM
    scale_loss = 1.0 / math.sqrt(N_REP * accounts)
    grad_enc = jnp.zeros((FE, H), jnp.float32)
    grad_one = jnp.zeros((H, H), jnp.float32)
    grad_two = jnp.zeros((H, H), jnp.float32)
    outputs = []
    for batch in range(N_REP):
        counts = block_counts[batch].reshape(N_DOM, NB_DEV, BLOCK, BLOCK)
        rowblk = slot_blocks[batch, :, 0].reshape(N_DOM, NB_DEV).astype(jnp.int32)
        colblk = slot_blocks[batch, :, 1].reshape(N_DOM, NB_DEV).astype(jnp.int32)
        live_mask = (jnp.arange(NB_DEV, dtype=jnp.int32)[None, :] < live_count[batch][:, None]).astype(jnp.float32)
        first_block = (jnp.arange(N_DOM, dtype=jnp.int32) * BLK_DEV)[:, None, None]
        row_onehot = (rowblk[:, :, None] - first_block == jnp.arange(BLK_DEV, dtype=jnp.int32)[None, None, :]).astype(jnp.float32)
        row_onehot = row_onehot * live_mask[:, :, None]
        row_sums = lax.optimization_barrier(jnp.sum(counts, axis=3)).astype(jnp.float32)
        degree = loop_weight + jnp.einsum('psb,psi->pbi', row_onehot, row_sums, precision=lax.Precision.HIGHEST).reshape(accounts)

        def propagate(field):
            blocked = field.reshape(nblocks, BLOCK, H)

            def one_part(items):
                part_counts, part_cols, part_hot = items
                taken = blocked[part_cols].astype(jnp.float32)
                product = jnp.einsum('sij,sjh->sih', part_counts.astype(jnp.float32), taken, precision=lax.Precision.HIGHEST)
                return jnp.einsum('sb,sih->bih', part_hot, product, precision=lax.Precision.HIGHEST)
            summed = lax.map(one_part, (counts, colblk, row_onehot)).reshape(accounts, H)
            return (loop_weight * field.astype(jnp.float32) + summed) / degree[:, None]

        def transpose(field):
            blocked = field.reshape(nblocks, BLOCK, H)

            def one_part(carry, items):
                part_counts, part_rows, part_cols, part_mask = items
                taken = blocked[part_rows].astype(jnp.float32)
                weighted = part_counts.astype(jnp.float32) * part_mask[:, None, None]
                product = jnp.einsum('sij,sih->sjh', weighted, taken, precision=lax.Precision.HIGHEST)
                return (carry.at[part_cols].add(product), None)
            summed, _ = lax.scan(one_part, jnp.zeros((nblocks, BLOCK, H), jnp.float32), (counts, rowblk, colblk, live_mask))
            return loop_weight * field.astype(jnp.float32) + summed.reshape(accounts, H)
        rows_time = events[batch]
        pre = jnp.dot(rows_time, w_enc, preferred_element_type=jnp.float32)
        encoded = jax.nn.silu(pre).astype(jnp.bfloat16)
        account_ids = perm[batch].astype(jnp.int32)
        h_zero = jnp.zeros((accounts, H), jnp.bfloat16).at[account_ids].set(encoded)
        z_one = jnp.dot(h_zero, w_one, preferred_element_type=jnp.float32).astype(jnp.bfloat16)
        agg_one = propagate(z_one)
        h_one = jax.nn.silu(agg_one).astype(jnp.bfloat16)
        z_two = jnp.dot(h_one, w_two, preferred_element_type=jnp.float32).astype(jnp.bfloat16)
        outputs.append(propagate(z_two).astype(jnp.bfloat16))
        gs_two = (out_grad[batch].astype(jnp.float32) * scale_loss / degree[:, None]).astype(jnp.bfloat16)
        gz_two = transpose(gs_two).astype(jnp.bfloat16)
        grad_two = grad_two + jnp.dot(h_one.T, gz_two, preferred_element_type=jnp.float32)
        gh_one = jnp.dot(gz_two, w_two.T, preferred_element_type=jnp.float32)
        gs_one = (gh_one * silu_slope(agg_one) / degree[:, None]).astype(jnp.bfloat16)
        gz_one = transpose(gs_one).astype(jnp.bfloat16)
        grad_one = grad_one + jnp.dot(h_zero.T, gz_one, preferred_element_type=jnp.float32)
        gh_zero = lax.optimization_barrier(jnp.dot(gz_one, w_one.T, preferred_element_type=jnp.float32).astype(jnp.bfloat16))
        g_time = gh_zero[account_ids]
        g_encoded = (g_time.astype(jnp.float32) * silu_slope(pre)).astype(jnp.bfloat16)
        grad_enc = grad_enc + jnp.dot(rows_time.T, g_encoded, preferred_element_type=jnp.float32)
    return (jnp.stack(outputs), grad_enc, grad_one, grad_two)
```

```python
import functools
import math

import jax
import jax.numpy as jnp
from jax import lax
from jax.experimental import pallas as pl
from jax.experimental.pallas import tpu as pltpu
from jax.sharding import PartitionSpec as P

loop_weight = 4.0
NY = 8
NZ = 16
NX = 4
F32 = jnp.float32
BF16 = jnp.bfloat16


def dot(a, b):
    return jnp.dot(a, b, preferred_element_type=F32)


def dot_nt(a, b):
    return lax.dot_general(a, b, (((1,), (1,)), ((), ())), preferred_element_type=F32)


def dot_tn(a, b):
    return lax.dot_general(a, b, (((0,), (0,)), ((), ())), preferred_element_type=F32)


def sigmoid(value):
    return 1.0 / (1.0 + jnp.exp(-value))


def wait_for(ref, sem):
    pltpu.make_async_copy(ref, ref, sem).wait()


def step_kernel(
    scale_loss,
    events, perm, w_enc, w_one, w_two, slots, live, counts, out_grad,
    embed, grad_enc, grad_one, grad_two,
    adj_f, adj, adj_t, inv_deg, mid, ev_win, z_one, z_two, gs_ref, gz_ref, gh_ref,
    a_src, a_dst, b_src, b_dst, qa_src, qa_dst, qb_src, qb_dst,
    rs_src, rs_dst, y_dst, x_dst, ag_dst,
    send_sem, recv_sem,
):
    me = lax.axis_index("dom")
    rep = lax.axis_index("rep")
    ndom = NY * NZ
    my_y = me // NZ
    my_z = me % NZ
    left = (me + ndom - 1) % ndom
    right = (me + 1) % ndom

    def in_y(j):
        return (my_y + j) % NY

    def in_z(j):
        return (my_z + j) % NZ

    def in_x(j):
        return (rep + j) % NX

    barrier = pltpu.get_barrier_semaphore()

    def hello(device):
        pl.semaphore_signal(barrier, inc=1, device_id=device, device_id_type=pl.DeviceIdType.MESH)

    for j in range(1, NY):
        hello({"dom": in_y(j) * NZ + my_z})
    for j in range(1, NZ):
        hello({"dom": my_y * NZ + in_z(j)})
    for j in range(1, NX):
        hello({"rep": in_x(j)})
    hello({"dom": left})
    hello({"dom": right})

    def send(src, dst, step, device):
        pltpu.make_async_remote_copy(
            src_ref=src, dst_ref=dst, send_sem=send_sem.at[step], recv_sem=recv_sem.at[step],
            device_id=device, device_id_type=pl.DeviceIdType.MESH,
        ).start()

    rows = lax.broadcasted_iota(jnp.int32, (256, 256), 0)
    cols = lax.broadcasted_iota(jnp.int32, (256, 256), 1)
    ids = perm[...]
    ids_row = ids.astype(F32)
    ids_col = jnp.sum(jnp.where(rows == cols, ids_row, 0.0), axis=1, keepdims=True)
    place = jnp.sum(jnp.where(ids_col < ids_row, 1.0, 0.0), axis=0, keepdims=True)
    sorting = jnp.where(rows.astype(F32) == place, 1.0, 0.0).astype(BF16)
    local_col = (ids_col.astype(jnp.int32) & 255).astype(F32)
    local_rep = jnp.broadcast_to(local_col, (256, 128)).astype(BF16)
    a_src[:, :, 0:128] = dot(sorting, events[0]).astype(BF16).reshape(NY, 32, 128)
    a_src[:, :, 128:256] = dot(sorting, local_rep).astype(BF16).reshape(NY, 32, 128)

    pl.semaphore_wait(barrier, NY - 1 + NZ - 1 + NX - 1 + 2)

    for j in range(1, NY):
        to = in_y(j)
        send(a_src.at[to], a_dst.at[my_y], 0, {"dom": to * NZ + my_z})
    a_dst[my_y] = a_src[my_y]

    weights = []
    for s in range(10):
        row = slots[0, s, 0] - 2 * me
        col = (slots[0, s, 1] - 2 * me + 1 + 2 * ndom) % (2 * ndom)
        used = s < live[0, 0]
        weights.append(
            [[jnp.where(used & (row == r) & (col == c), 1.0, 0.0) for c in range(4)] for r in range(2)]
        )
    for part in range(4):
        here = slice(part * 32, part * 32 + 32)
        sums = [[None] * 4 for _ in range(2)]
        for s in range(10):
            cell = counts[0, s, here, :].astype(F32)
            for r in range(2):
                for c in range(4):
                    term = cell * weights[s][r][c]
                    sums[r][c] = term if s == 0 else sums[r][c] + term
        diag = (
            lax.broadcasted_iota(jnp.int32, (32, 128), 0) + part * 32
            == lax.broadcasted_iota(jnp.int32, (32, 128), 1)
        )
        for r in range(2):
            sums[r][r + 1] = sums[r][r + 1] + jnp.where(diag, loop_weight, 0.0)
            for c in range(4):
                adj_f[r * 128 + part * 32 : r * 128 + part * 32 + 32, c * 128 : c * 128 + 128] = sums[r][c]
    adj[...] = adj_f[...].astype(BF16)
    for r in range(2):
        for c in range(4):
            adj_t[c * 128 : c * 128 + 128, r * 128 : r * 128 + 128] = (
                adj_f[r * 128 : r * 128 + 128, c * 128 : c * 128 + 128].T.astype(BF16)
            )
    inverse = 1.0 / dot(adj[...], jnp.ones((512, 128), BF16))
    inv_deg[:, 0:128] = inverse
    inv_deg[:, 128:256] = inverse

    gs_two = (out_grad[0].astype(F32) * scale_loss * inv_deg[...]).astype(BF16)
    qa_src[0] = dot(adj_t[0:128], gs_two).astype(BF16)
    qa_src[1] = dot(adj_t[384:512], gs_two).astype(BF16)
    send(qa_src.at[0], qa_dst.at[1], 1, {"dom": left})
    send(qa_src.at[1], qa_dst.at[0], 2, {"dom": right})
    gz_ref[...] = dot(adj_t[128:384], gs_two)

    source = ((rows >> 1) & (NY - 1)) * 32 + (rows >> 4) * 2 + (rows & 1)
    mid[...] = jnp.where(cols == source, 1.0, 0.0).astype(BF16)

    wait_for(a_dst.at[pl.ds(0, NY - 1)], recv_sem.at[0])
    b_src[...] = dot(mid[...], a_dst[...].reshape(256, 256)).astype(BF16).reshape(NZ, 16, 256)
    for j in range(1, NZ):
        to = in_z(j)
        send(b_src.at[to], b_dst.at[my_z], 3, {"dom": my_y * NZ + to})
    b_dst[my_z] = b_src[my_z]

    wait_for(qa_dst.at[1], recv_sem.at[1])
    wait_for(qa_dst.at[0], recv_sem.at[2])
    gz_two = (gz_ref[...] + qa_dst[...].astype(F32).reshape(256, 256)).astype(BF16)
    gh_ref[...] = dot_nt(gz_two, w_two[...]) * inv_deg[...]

    wait_for(b_dst.at[pl.ds(0, NZ - 1)], recv_sem.at[3])
    got = b_dst[...].reshape(256, 256)
    got_ids = got[:, 128:256].astype(F32)
    lane = cols[:, 0:128].astype(F32)
    placing = jnp.concatenate(
        [jnp.where(got_ids == lane, 1.0, 0.0), jnp.where(got_ids == lane + 128.0, 1.0, 0.0)], axis=1
    ).astype(BF16)
    ev_win[128:384] = dot_tn(placing, got[:, 0:128]).astype(BF16)
    send(ev_win.at[pl.ds(128, 128)], ev_win.at[pl.ds(384, 128)], 4, {"dom": left})
    send(ev_win.at[pl.ds(256, 128)], ev_win.at[pl.ds(0, 128)], 5, {"dom": right})

    def encoded(rows_in):
        pre_rows = dot(rows_in, w_enc[...])
        return pre_rows, (pre_rows * sigmoid(pre_rows)).astype(BF16)

    ev_own = ev_win[128:384]
    pre, h_zero = encoded(ev_own)
    z_own = dot(h_zero, w_one[...]).astype(BF16)
    total = dot(adj[:, 128:384], z_own)
    wait_for(ev_win.at[pl.ds(384, 128)], recv_sem.at[4])
    wait_for(ev_win.at[pl.ds(0, 128)], recv_sem.at[5])
    for where in (0, 384):
        z_side = dot(encoded(ev_win[where : where + 128])[1], w_one[...]).astype(BF16)
        total = total + dot(adj[:, where : where + 128], z_side)
    agg_one = total * inv_deg[...]
    sig = sigmoid(agg_one)
    h_one = (agg_one * sig).astype(BF16)
    z_two[128:384] = dot(h_one, w_two[...]).astype(BF16)
    send(z_two.at[pl.ds(128, 128)], z_two.at[pl.ds(384, 128)], 6, {"dom": left})
    send(z_two.at[pl.ds(256, 128)], z_two.at[pl.ds(0, 128)], 7, {"dom": right})
    gs_one = (gh_ref[...] * (sig * (1.0 + agg_one * (1.0 - sig)))).astype(BF16)
    qb_src[0] = dot(adj_t[0:128], gs_one).astype(BF16)
    qb_src[1] = dot(adj_t[384:512], gs_one).astype(BF16)
    send(qb_src.at[0], qb_dst.at[1], 8, {"dom": left})
    send(qb_src.at[1], qb_dst.at[0], 9, {"dom": right})
    gz_own = dot(adj_t[128:384], gs_one)
    rs_src[:, :, 0:256] = dot_tn(h_one, gz_two).astype(BF16).reshape(NZ, 16, 256)

    wait_for(qb_dst.at[1], recv_sem.at[8])
    wait_for(qb_dst.at[0], recv_sem.at[9])
    gz_one = (gz_own + qb_dst[...].astype(F32).reshape(256, 256)).astype(BF16)
    rs_src[:, :, 256:512] = dot_tn(h_zero, gz_one).astype(BF16).reshape(NZ, 16, 256)
    gh_zero = dot_nt(gz_one, w_one[...]).astype(BF16)
    sig = sigmoid(pre)
    g_enc = (gh_zero.astype(F32) * (sig * (1.0 + pre * (1.0 - sig)))).astype(BF16)
    l_enc = dot_tn(ev_own, g_enc).astype(BF16)
    for k in range(NZ):
        r, c = 16 * (k // 2), 128 * (k % 2)
        rs_src[k, :, 512:640] = l_enc[r : r + 16, c : c + 128]

    for j in range(1, NZ):
        to = in_z(j)
        send(rs_src.at[to], rs_dst.at[my_z], 10, {"dom": my_y * NZ + to})
    rs_dst[my_z] = rs_src[my_z]

    wait_for(z_two.at[pl.ds(384, 128)], recv_sem.at[6])
    wait_for(z_two.at[pl.ds(0, 128)], recv_sem.at[7])
    embed[0] = (dot(adj[...], z_two[...]) * inv_deg[...]).astype(BF16)

    wait_for(rs_dst.at[pl.ds(0, NZ - 1)], recv_sem.at[10])
    y_dst[my_y] = jnp.sum(rs_dst[...].astype(F32), axis=0).astype(BF16)
    for j in range(1, NY):
        send(y_dst.at[my_y], y_dst.at[my_y], 11, {"dom": in_y(j) * NZ + my_z})
    wait_for(y_dst.at[pl.ds(0, NY - 1)], recv_sem.at[11])
    x_dst[rep] = jnp.sum(y_dst[...].astype(F32), axis=0).astype(BF16)
    for j in range(1, NX):
        send(x_dst.at[rep], x_dst.at[rep], 12, {"rep": in_x(j)})
    wait_for(x_dst.at[pl.ds(0, NX - 1)], recv_sem.at[12])
    ag_dst[my_z] = jnp.sum(x_dst[...].astype(F32), axis=0).astype(BF16)
    for j in range(1, NZ):
        send(ag_dst.at[my_z], ag_dst.at[my_z], 13, {"dom": my_y * NZ + in_z(j)})
    wait_for(ag_dst.at[pl.ds(0, NZ - 1)], recv_sem.at[13])
    grad_two[...] = ag_dst[:, :, 0:256].astype(F32).reshape(256, 256)
    grad_one[...] = ag_dst[:, :, 256:512].astype(F32).reshape(256, 256)
    for k in range(NZ):
        r, c = 16 * (k // 2), 128 * (k % 2)
        grad_enc[r : r + 16, c : c + 128] = ag_dst[k, :, 512:640].astype(F32)

    wait_for(a_src.at[pl.ds(0, NY - 1)], send_sem.at[0])
    wait_for(qa_src.at[0], send_sem.at[1])
    wait_for(qa_src.at[1], send_sem.at[2])
    wait_for(b_src.at[pl.ds(0, NZ - 1)], send_sem.at[3])
    for step, ref in ((4, ev_win), (5, ev_win), (6, z_two), (7, z_two)):
        wait_for(ref.at[pl.ds(0, 128)], send_sem.at[step])
    wait_for(qb_src.at[0], send_sem.at[8])
    wait_for(qb_src.at[1], send_sem.at[9])
    wait_for(rs_src.at[pl.ds(0, NZ - 1)], send_sem.at[10])
    wait_for(y_dst.at[pl.ds(0, NY - 1)], send_sem.at[11])
    wait_for(x_dst.at[pl.ds(0, NX - 1)], send_sem.at[12])
    wait_for(ag_dst.at[pl.ds(0, NZ - 1)], send_sem.at[13])


def body(events, perm, w_enc, w_one, w_two, slot_blocks, live_count, block_counts, out_grad):
    scale_loss = 1.0 / math.sqrt(lax.axis_size("rep") * lax.axis_size("dom") * events.shape[1])
    vmem = pl.BlockSpec(memory_space=pltpu.VMEM)
    smem = pl.BlockSpec(memory_space=pltpu.SMEM)
    return pl.pallas_call(
        functools.partial(step_kernel, scale_loss),
        out_shape=(
            jax.ShapeDtypeStruct((1, 256, 256), BF16),
            jax.ShapeDtypeStruct((128, 256), F32),
            jax.ShapeDtypeStruct((256, 256), F32),
            jax.ShapeDtypeStruct((256, 256), F32),
        ),
        in_specs=[vmem, vmem, vmem, vmem, vmem, smem, smem, vmem, vmem],
        out_specs=(vmem, vmem, vmem, vmem),
        scratch_shapes=[
            pltpu.VMEM((256, 512), F32),
            pltpu.VMEM((256, 512), BF16),
            pltpu.VMEM((512, 256), BF16),
            pltpu.VMEM((256, 256), F32),
            pltpu.VMEM((256, 256), BF16),
            pltpu.VMEM((512, 128), BF16),
            pltpu.VMEM((512, 256), BF16),
            pltpu.VMEM((512, 256), BF16),
            pltpu.VMEM((256, 256), BF16),
            pltpu.VMEM((256, 256), F32),
            pltpu.VMEM((256, 256), F32),
            pltpu.VMEM((NY, 32, 256), BF16),
            pltpu.VMEM((NY, 32, 256), BF16),
            pltpu.VMEM((NZ, 16, 256), BF16),
            pltpu.VMEM((NZ, 16, 256), BF16),
            pltpu.VMEM((2, 128, 256), BF16),
            pltpu.VMEM((2, 128, 256), BF16),
            pltpu.VMEM((2, 128, 256), BF16),
            pltpu.VMEM((2, 128, 256), BF16),
            pltpu.VMEM((NZ, 16, 640), BF16),
            pltpu.VMEM((NZ, 16, 640), BF16),
            pltpu.VMEM((NY, 16, 640), BF16),
            pltpu.VMEM((NX, 16, 640), BF16),
            pltpu.VMEM((NZ, 16, 640), BF16),
            pltpu.SemaphoreType.DMA((14,)),
            pltpu.SemaphoreType.DMA((14,)),
        ],
        compiler_params=pltpu.CompilerParams(
            collective_id=0, has_side_effects=True, vmem_limit_bytes=32 * 1024 * 1024
        ),
    )(events, perm, w_enc, w_one, w_two, slot_blocks, live_count, block_counts, out_grad)


def solution(mesh):
    return jax.shard_map(
        body,
        mesh=mesh,
        in_specs=(
            P("rep", "dom", None),
            P("rep", "dom"),
            P(),
            P(),
            P(),
            P("rep", "dom", None),
            P("rep", "dom"),
            P("rep", "dom", None, None),
            P("rep", "dom", None),
        ),
        out_specs=(P("rep", "dom", None), P(), P(), P()),
        check_vma=False,
    )
```

```python
import functools
import math

import jax
import jax.numpy as jnp
from jax import lax
from jax.experimental import pallas as pl
from jax.experimental.pallas import tpu as pltpu
from jax.sharding import PartitionSpec as P

loop_weight = 4.0
NY = 8
NZ = 16
NX = 4
F32 = jnp.float32
BF16 = jnp.bfloat16


def dot(a, b):
    return jnp.dot(a, b, preferred_element_type=F32)


def dot_nt(a, b):
    return lax.dot_general(a, b, (((1,), (1,)), ((), ())), preferred_element_type=F32)


def dot_tn(a, b):
    return lax.dot_general(a, b, (((0,), (0,)), ((), ())), preferred_element_type=F32)


def sigmoid(value):
    return 1.0 / (1.0 + jnp.exp(-value))


def wait_for(ref, sem):
    pltpu.make_async_copy(ref, ref, sem).wait()


def step_kernel(
    scale_loss,
    events_in, perm_in, w_enc_in, w_one_in, w_two_in, slots, live, counts_in, out_grad_in,
    embed, grad_enc, grad_one, grad_two,
    events, perm, w_enc, w_one, w_two, counts, out_grad,
    adj_f, adj, adj_t, inv_deg, mid, ev_win, z_two, gz_ref, gh_ref,
    a_src, a_dst, b_src, b_dst, qa_src, qa_dst, qb_src, qb_dst,
    rs_src, rs_dst, y_dst, x_dst, ag_dst,
    load_sem, send_sem, recv_sem,
):
    me = lax.axis_index("dom")
    rep = lax.axis_index("rep")
    ndom = NY * NZ
    my_y = me // NZ
    my_z = me % NZ
    left = (me + ndom - 1) % ndom
    right = (me + 1) % ndom

    def in_y(j):
        return (my_y + j) % NY

    def in_z(j):
        return (my_z + j) % NZ

    def in_x(j):
        return (rep + j) % NX

    loads = [
        pltpu.make_async_copy(src, dst, load_sem.at[i])
        for i, (src, dst) in enumerate(
            (
                (perm_in, perm), (events_in, events), (counts_in, counts), (out_grad_in, out_grad),
                (w_two_in, w_two), (w_enc_in, w_enc), (w_one_in, w_one),
            )
        )
    ]
    for load in loads:
        load.start()

    barrier = pltpu.get_barrier_semaphore()

    def hello(device):
        pl.semaphore_signal(barrier, inc=1, device_id=device, device_id_type=pl.DeviceIdType.MESH)

    for j in range(1, NY):
        hello({"dom": in_y(j) * NZ + my_z})
    for j in range(1, NZ):
        hello({"dom": my_y * NZ + in_z(j)})
    for j in range(1, NX):
        hello({"rep": in_x(j)})
    hello({"dom": left})
    hello({"dom": right})

    def send(src, dst, step, device):
        pltpu.make_async_remote_copy(
            src_ref=src, dst_ref=dst, send_sem=send_sem.at[step], recv_sem=recv_sem.at[step],
            device_id=device, device_id_type=pl.DeviceIdType.MESH,
        ).start()

    rows = lax.broadcasted_iota(jnp.int32, (256, 256), 0)
    cols = lax.broadcasted_iota(jnp.int32, (256, 256), 1)
    loads[0].wait()
    ids = perm[...]
    ids_row = ids.astype(F32)
    ids_col = jnp.sum(jnp.where(rows == cols, ids_row, 0.0), axis=1, keepdims=True)
    place = jnp.sum(jnp.where(ids_col < ids_row, 1.0, 0.0), axis=0, keepdims=True)
    sorting = jnp.where(rows.astype(F32) == place, 1.0, 0.0).astype(BF16)
    local_col = (ids_col.astype(jnp.int32) & 255).astype(F32)
    local_rep = jnp.broadcast_to(local_col, (256, 128)).astype(BF16)
    loads[1].wait()
    a_src[:, :, 0:128] = dot(sorting, events[0]).astype(BF16).reshape(NY, 32, 128)
    a_src[:, :, 128:256] = dot(sorting, local_rep).astype(BF16).reshape(NY, 32, 128)

    pl.semaphore_wait(barrier, NY - 1 + NZ - 1 + NX - 1 + 2)

    for j in range(1, NY):
        to = in_y(j)
        send(a_src.at[to], a_dst.at[my_y], 0, {"dom": to * NZ + my_z})
    a_dst[my_y] = a_src[my_y]

    loads[2].wait()
    weights = []
    for s in range(10):
        row = slots[0, s, 0] - 2 * me
        col = (slots[0, s, 1] - 2 * me + 1 + 2 * ndom) % (2 * ndom)
        used = s < live[0, 0]
        weights.append(
            [[jnp.where(used & (row == r) & (col == c), 1.0, 0.0) for c in range(4)] for r in range(2)]
        )
    for part in range(4):
        here = slice(part * 32, part * 32 + 32)
        sums = [[None] * 4 for _ in range(2)]
        for s in range(10):
            cell = counts[0, s, here, :].astype(F32)
            for r in range(2):
                for c in range(4):
                    term = cell * weights[s][r][c]
                    sums[r][c] = term if s == 0 else sums[r][c] + term
        diag = (
            lax.broadcasted_iota(jnp.int32, (32, 128), 0) + part * 32
            == lax.broadcasted_iota(jnp.int32, (32, 128), 1)
        )
        for r in range(2):
            sums[r][r + 1] = sums[r][r + 1] + jnp.where(diag, loop_weight, 0.0)
            for c in range(4):
                adj_f[r * 128 + part * 32 : r * 128 + part * 32 + 32, c * 128 : c * 128 + 128] = sums[r][c]
    adj[...] = adj_f[...].astype(BF16)
    for r in range(2):
        for c in range(4):
            adj_t[c * 128 : c * 128 + 128, r * 128 : r * 128 + 128] = (
                adj_f[r * 128 : r * 128 + 128, c * 128 : c * 128 + 128].T.astype(BF16)
            )
    inverse = 1.0 / dot(adj[...], jnp.ones((512, 128), BF16))
    inv_deg[:, 0:128] = inverse
    inv_deg[:, 128:256] = inverse

    loads[3].wait()
    gs_two = (out_grad[0].astype(F32) * scale_loss * inv_deg[...]).astype(BF16)
    qa_src[0] = dot(adj_t[0:128], gs_two).astype(BF16)
    qa_src[1] = dot(adj_t[384:512], gs_two).astype(BF16)
    send(qa_src.at[0], qa_dst.at[1], 1, {"dom": left})
    send(qa_src.at[1], qa_dst.at[0], 2, {"dom": right})
    gz_ref[...] = dot(adj_t[128:384], gs_two)

    source = ((rows >> 1) & (NY - 1)) * 32 + (rows >> 4) * 2 + (rows & 1)
    mid[...] = jnp.where(cols == source, 1.0, 0.0).astype(BF16)

    wait_for(a_dst.at[pl.ds(0, NY - 1)], recv_sem.at[0])
    b_src[...] = dot(mid[...], a_dst[...].reshape(256, 256)).astype(BF16).reshape(NZ, 16, 256)
    for j in range(1, NZ):
        to = in_z(j)
        send(b_src.at[to], b_dst.at[my_z], 3, {"dom": my_y * NZ + to})
    b_dst[my_z] = b_src[my_z]

    wait_for(qa_dst.at[1], recv_sem.at[1])
    wait_for(qa_dst.at[0], recv_sem.at[2])
    loads[4].wait()
    gz_two = (gz_ref[...] + qa_dst[...].astype(F32).reshape(256, 256)).astype(BF16)
    gh_ref[...] = dot_nt(gz_two, w_two[...]) * inv_deg[...]

    wait_for(b_dst.at[pl.ds(0, NZ - 1)], recv_sem.at[3])
    got = b_dst[...].reshape(256, 256)
    got_ids = got[:, 128:256].astype(F32)
    lane = cols[:, 0:128].astype(F32)
    placing = jnp.concatenate(
        [jnp.where(got_ids == lane, 1.0, 0.0), jnp.where(got_ids == lane + 128.0, 1.0, 0.0)], axis=1
    ).astype(BF16)
    ev_win[128:384] = dot_tn(placing, got[:, 0:128]).astype(BF16)
    send(ev_win.at[pl.ds(128, 128)], ev_win.at[pl.ds(384, 128)], 4, {"dom": left})
    send(ev_win.at[pl.ds(256, 128)], ev_win.at[pl.ds(0, 128)], 5, {"dom": right})

    loads[5].wait()
    loads[6].wait()

    def encoded(rows_in):
        pre_rows = dot(rows_in, w_enc[...])
        return pre_rows, (pre_rows * sigmoid(pre_rows)).astype(BF16)

    ev_own = ev_win[128:384]
    pre, h_zero = encoded(ev_own)
    z_own = dot(h_zero, w_one[...]).astype(BF16)
    total = dot(adj[:, 128:384], z_own)
    wait_for(ev_win.at[pl.ds(384, 128)], recv_sem.at[4])
    wait_for(ev_win.at[pl.ds(0, 128)], recv_sem.at[5])
    for where in (0, 384):
        z_side = dot(encoded(ev_win[where : where + 128])[1], w_one[...]).astype(BF16)
        total = total + dot(adj[:, where : where + 128], z_side)
    agg_one = total * inv_deg[...]
    sig = sigmoid(agg_one)
    h_one = (agg_one * sig).astype(BF16)
    z_two[128:384] = dot(h_one, w_two[...]).astype(BF16)
    send(z_two.at[pl.ds(128, 128)], z_two.at[pl.ds(384, 128)], 6, {"dom": left})
    send(z_two.at[pl.ds(256, 128)], z_two.at[pl.ds(0, 128)], 7, {"dom": right})
    gs_one = (gh_ref[...] * (sig * (1.0 + agg_one * (1.0 - sig)))).astype(BF16)
    qb_src[0] = dot(adj_t[0:128], gs_one).astype(BF16)
    qb_src[1] = dot(adj_t[384:512], gs_one).astype(BF16)
    send(qb_src.at[0], qb_dst.at[1], 8, {"dom": left})
    send(qb_src.at[1], qb_dst.at[0], 9, {"dom": right})
    gz_own = dot(adj_t[128:384], gs_one)
    rs_src[:, :, 0:256] = dot_tn(h_one, gz_two).astype(BF16).reshape(NZ, 16, 256)

    wait_for(qb_dst.at[1], recv_sem.at[8])
    wait_for(qb_dst.at[0], recv_sem.at[9])
    gz_one = (gz_own + qb_dst[...].astype(F32).reshape(256, 256)).astype(BF16)
    rs_src[:, :, 256:512] = dot_tn(h_zero, gz_one).astype(BF16).reshape(NZ, 16, 256)
    gh_zero = dot_nt(gz_one, w_one[...]).astype(BF16)
    sig = sigmoid(pre)
    g_enc = (gh_zero.astype(F32) * (sig * (1.0 + pre * (1.0 - sig)))).astype(BF16)
    l_enc = dot_tn(ev_own, g_enc).astype(BF16)
    for k in range(NZ):
        r, c = 16 * (k // 2), 128 * (k % 2)
        rs_src[k, :, 512:640] = l_enc[r : r + 16, c : c + 128]

    for j in range(1, NZ):
        to = in_z(j)
        send(rs_src.at[to], rs_dst.at[my_z], 10, {"dom": my_y * NZ + to})
    rs_dst[my_z] = rs_src[my_z]

    wait_for(z_two.at[pl.ds(384, 128)], recv_sem.at[6])
    wait_for(z_two.at[pl.ds(0, 128)], recv_sem.at[7])
    embed[0] = (dot(adj[...], z_two[...]) * inv_deg[...]).astype(BF16)

    wait_for(rs_dst.at[pl.ds(0, NZ - 1)], recv_sem.at[10])
    y_dst[my_y] = jnp.sum(rs_dst[...].astype(F32), axis=0).astype(BF16)
    for j in range(1, NY):
        send(y_dst.at[my_y], y_dst.at[my_y], 11, {"dom": in_y(j) * NZ + my_z})
    wait_for(y_dst.at[pl.ds(0, NY - 1)], recv_sem.at[11])
    x_dst[rep] = jnp.sum(y_dst[...].astype(F32), axis=0).astype(BF16)
    for j in range(1, NX):
        send(x_dst.at[rep], x_dst.at[rep], 12, {"rep": in_x(j)})
    wait_for(x_dst.at[pl.ds(0, NX - 1)], recv_sem.at[12])
    ag_dst[my_z] = jnp.sum(x_dst[...].astype(F32), axis=0).astype(BF16)
    for j in range(1, NZ):
        send(ag_dst.at[my_z], ag_dst.at[my_z], 13, {"dom": my_y * NZ + in_z(j)})
    wait_for(ag_dst.at[pl.ds(0, NZ - 1)], recv_sem.at[13])
    grad_two[...] = ag_dst[:, :, 0:256].astype(F32).reshape(256, 256)
    grad_one[...] = ag_dst[:, :, 256:512].astype(F32).reshape(256, 256)
    for k in range(NZ):
        r, c = 16 * (k // 2), 128 * (k % 2)
        grad_enc[r : r + 16, c : c + 128] = ag_dst[k, :, 512:640].astype(F32)

    wait_for(a_src.at[pl.ds(0, NY - 1)], send_sem.at[0])
    wait_for(qa_src.at[0], send_sem.at[1])
    wait_for(qa_src.at[1], send_sem.at[2])
    wait_for(b_src.at[pl.ds(0, NZ - 1)], send_sem.at[3])
    for step, ref in ((4, ev_win), (5, ev_win), (6, z_two), (7, z_two)):
        wait_for(ref.at[pl.ds(0, 128)], send_sem.at[step])
    wait_for(qb_src.at[0], send_sem.at[8])
    wait_for(qb_src.at[1], send_sem.at[9])
    wait_for(rs_src.at[pl.ds(0, NZ - 1)], send_sem.at[10])
    wait_for(y_dst.at[pl.ds(0, NY - 1)], send_sem.at[11])
    wait_for(x_dst.at[pl.ds(0, NX - 1)], send_sem.at[12])
    wait_for(ag_dst.at[pl.ds(0, NZ - 1)], send_sem.at[13])


def body(events, perm, w_enc, w_one, w_two, slot_blocks, live_count, block_counts, out_grad):
    scale_loss = 1.0 / math.sqrt(lax.axis_size("rep") * lax.axis_size("dom") * events.shape[1])
    vmem = pl.BlockSpec(memory_space=pltpu.VMEM)
    hbm = pl.BlockSpec(memory_space=pltpu.HBM)
    smem = pl.BlockSpec(memory_space=pltpu.SMEM)
    args = [
        pltpu.with_memory_space_constraint(x, pltpu.HBM)
        for x in (events, perm, w_enc, w_one, w_two, block_counts, out_grad)
    ]
    return pl.pallas_call(
        functools.partial(step_kernel, scale_loss),
        out_shape=(
            jax.ShapeDtypeStruct((1, 256, 256), BF16),
            jax.ShapeDtypeStruct((128, 256), F32),
            jax.ShapeDtypeStruct((256, 256), F32),
            jax.ShapeDtypeStruct((256, 256), F32),
        ),
        in_specs=[hbm, hbm, hbm, hbm, hbm, smem, smem, hbm, hbm],
        out_specs=(vmem, vmem, vmem, vmem),
        scratch_shapes=[
            pltpu.VMEM((1, 256, 128), BF16),
            pltpu.VMEM((1, 256), jnp.int32),
            pltpu.VMEM((128, 256), BF16),
            pltpu.VMEM((256, 256), BF16),
            pltpu.VMEM((256, 256), BF16),
            pltpu.VMEM((1, 10, 128, 128), jnp.int32),
            pltpu.VMEM((1, 256, 256), BF16),
            pltpu.VMEM((256, 512), F32),
            pltpu.VMEM((256, 512), BF16),
            pltpu.VMEM((512, 256), BF16),
            pltpu.VMEM((256, 256), F32),
            pltpu.VMEM((256, 256), BF16),
            pltpu.VMEM((512, 128), BF16),
            pltpu.VMEM((512, 256), BF16),
            pltpu.VMEM((256, 256), F32),
            pltpu.VMEM((256, 256), F32),
            pltpu.VMEM((NY, 32, 256), BF16),
            pltpu.VMEM((NY, 32, 256), BF16),
            pltpu.VMEM((NZ, 16, 256), BF16),
            pltpu.VMEM((NZ, 16, 256), BF16),
            pltpu.VMEM((2, 128, 256), BF16),
            pltpu.VMEM((2, 128, 256), BF16),
            pltpu.VMEM((2, 128, 256), BF16),
            pltpu.VMEM((2, 128, 256), BF16),
            pltpu.VMEM((NZ, 16, 640), BF16),
            pltpu.VMEM((NZ, 16, 640), BF16),
            pltpu.VMEM((NY, 16, 640), BF16),
            pltpu.VMEM((NX, 16, 640), BF16),
            pltpu.VMEM((NZ, 16, 640), BF16),
            pltpu.SemaphoreType.DMA((7,)),
            pltpu.SemaphoreType.DMA((14,)),
            pltpu.SemaphoreType.DMA((14,)),
        ],
        compiler_params=pltpu.CompilerParams(
            collective_id=0, has_side_effects=True, vmem_limit_bytes=16 * 1024 * 1024
        ),
    )(*args[:5], slot_blocks, live_count, *args[5:])


def solution(mesh):
    return jax.shard_map(
        body,
        mesh=mesh,
        in_specs=(
            P("rep", "dom", None),
            P("rep", "dom"),
            P(),
            P(),
            P(),
            P("rep", "dom", None),
            P("rep", "dom"),
            P("rep", "dom", None, None),
            P("rep", "dom", None),
        ),
        out_specs=(P("rep", "dom", None), P(), P(), P()),
        check_vma=False,
    )
```

```python
import functools
import math

import jax
import jax.numpy as jnp
from jax import lax
from jax.experimental import pallas as pl
from jax.experimental.pallas import tpu as pltpu
from jax.sharding import PartitionSpec as P

loop_weight = 4.0
NY = 8
NZ = 16
NX = 4
F32 = jnp.float32
BF16 = jnp.bfloat16


def dot(a, b):
    return jnp.dot(a, b, preferred_element_type=F32)


def dot_nt(a, b):
    return lax.dot_general(a, b, (((1,), (1,)), ((), ())), preferred_element_type=F32)


def dot_tn(a, b):
    return lax.dot_general(a, b, (((0,), (0,)), ((), ())), preferred_element_type=F32)


def sigmoid(value):
    return 1.0 / (1.0 + jnp.exp(-value))


def wait_for(ref, sem):
    pltpu.make_async_copy(ref, ref, sem).wait()


def tile(k):
    return 16 * (k // 2), 128 * (k % 2)


def step_kernel(
    scale_loss,
    events_in, perm_in, w_enc_in, w_one_in, w_two_in, slots, live, counts_in, out_grad_in,
    embed, grad_enc, grad_one, grad_two,
    events, perm, w_enc, w_one, w_two, counts, out_grad,
    adj_f, adj, adj_t, inv_deg, mid, ev_win, z_two, gz_ref, gh_ref,
    a_src, a_dst, b_src, b_dst, qa_src, qa_dst, qb_src, qb_dst,
    two_src, two_dst, lo_src, lo_dst, lo_mid, lo_all, hi_src, hi_dst, hi_mid, hi_all, x_dst,
    load_sem, send_sem, recv_sem,
):
    me = lax.axis_index("dom")
    rep = lax.axis_index("rep")
    ndom = NY * NZ
    my_y = me // NZ
    my_z = me % NZ
    left = (me + ndom - 1) % ndom
    right = (me + 1) % ndom

    def in_y(j):
        return (my_y + j) % NY

    def in_z(j):
        return (my_z + j) % NZ

    def in_x(j):
        return (rep + j) % NX

    core = me % 2
    my_yc = my_y * 2 + core
    my_zc = my_z // 2

    def at_yc(k):
        return {"dom": (k // 2) * NZ + my_zc * 2 + k % 2}

    def at_zc(k):
        return {"dom": my_y * NZ + k}

    def at_y(k):
        return {"dom": k * NZ + my_z}

    def at_z(k):
        return {"dom": my_y * NZ + k * 2 + core}

    loads = [
        pltpu.make_async_copy(src, dst, load_sem.at[i])
        for i, (src, dst) in enumerate(
            (
                (perm_in, perm), (events_in, events), (counts_in, counts), (out_grad_in, out_grad),
                (w_two_in, w_two), (w_enc_in, w_enc), (w_one_in, w_one),
            )
        )
    ]
    for load in loads:
        load.start()

    barrier = pltpu.get_barrier_semaphore()

    def hello(device):
        pl.semaphore_signal(barrier, inc=1, device_id=device, device_id_type=pl.DeviceIdType.MESH)

    for j in range(1, NY):
        hello({"dom": in_y(j) * NZ + my_z})
        hello({"dom": in_y(j) * NZ + my_zc * 2 + 1 - core})
    for j in range(1, NZ):
        hello({"dom": my_y * NZ + in_z(j)})
    for j in range(1, NX):
        hello({"rep": in_x(j)})
    hello({"dom": left})
    hello({"dom": right})

    def send(src, dst, step, device):
        pltpu.make_async_remote_copy(
            src_ref=src, dst_ref=dst, send_sem=send_sem.at[step], recv_sem=recv_sem.at[step],
            device_id=device, device_id_type=pl.DeviceIdType.MESH,
        ).start()

    rows = lax.broadcasted_iota(jnp.int32, (256, 256), 0)
    cols = lax.broadcasted_iota(jnp.int32, (256, 256), 1)
    loads[0].wait()
    ids = perm[...]
    ids_row = ids.astype(F32)
    ids_col = jnp.sum(jnp.where(rows == cols, ids_row, 0.0), axis=1, keepdims=True)
    place = jnp.sum(jnp.where(ids_col < ids_row, 1.0, 0.0), axis=0, keepdims=True)
    sorting = jnp.where(rows.astype(F32) == place, 1.0, 0.0).astype(BF16)
    local_col = (ids_col.astype(jnp.int32) & 255).astype(F32)
    local_rep = jnp.broadcast_to(local_col, (256, 128)).astype(BF16)
    loads[1].wait()
    a_src[:, :, 0:128] = dot(sorting, events[0]).astype(BF16).reshape(NY, 32, 128)
    a_src[:, :, 128:256] = dot(sorting, local_rep).astype(BF16).reshape(NY, 32, 128)

    pl.semaphore_wait(barrier, 2 * (NY - 1) + NZ - 1 + NX - 1 + 2)

    for j in range(1, NY):
        to = in_y(j)
        send(a_src.at[to], a_dst.at[my_y], 0, {"dom": to * NZ + my_z})
    a_dst[my_y] = a_src[my_y]

    loads[2].wait()
    weights = []
    for s in range(10):
        row = slots[0, s, 0] - 2 * me
        col = (slots[0, s, 1] - 2 * me + 1 + 2 * ndom) % (2 * ndom)
        used = s < live[0, 0]
        weights.append(
            [[jnp.where(used & (row == r) & (col == c), 1.0, 0.0) for c in range(4)] for r in range(2)]
        )
    for part in range(4):
        here = slice(part * 32, part * 32 + 32)
        sums = [[None] * 4 for _ in range(2)]
        for s in range(10):
            cell = counts[0, s, here, :].astype(F32)
            for r in range(2):
                for c in range(4):
                    term = cell * weights[s][r][c]
                    sums[r][c] = term if s == 0 else sums[r][c] + term
        diag = (
            lax.broadcasted_iota(jnp.int32, (32, 128), 0) + part * 32
            == lax.broadcasted_iota(jnp.int32, (32, 128), 1)
        )
        for r in range(2):
            sums[r][r + 1] = sums[r][r + 1] + jnp.where(diag, loop_weight, 0.0)
            for c in range(4):
                adj_f[r * 128 + part * 32 : r * 128 + part * 32 + 32, c * 128 : c * 128 + 128] = sums[r][c]
    adj[...] = adj_f[...].astype(BF16)
    for r in range(2):
        for c in range(4):
            adj_t[c * 128 : c * 128 + 128, r * 128 : r * 128 + 128] = (
                adj_f[r * 128 : r * 128 + 128, c * 128 : c * 128 + 128].T.astype(BF16)
            )
    inverse = 1.0 / dot(adj[...], jnp.ones((512, 128), BF16))
    inv_deg[:, 0:128] = inverse
    inv_deg[:, 128:256] = inverse

    loads[3].wait()
    gs_two = (out_grad[0].astype(F32) * scale_loss * inv_deg[...]).astype(BF16)
    qa_src[0] = dot(adj_t[0:128], gs_two).astype(BF16)
    qa_src[1] = dot(adj_t[384:512], gs_two).astype(BF16)
    send(qa_src.at[0], qa_dst.at[1], 1, {"dom": left})
    send(qa_src.at[1], qa_dst.at[0], 2, {"dom": right})
    gz_ref[...] = dot(adj_t[128:384], gs_two)

    source = ((rows >> 1) & (NY - 1)) * 32 + (rows >> 4) * 2 + (rows & 1)
    mid[...] = jnp.where(cols == source, 1.0, 0.0).astype(BF16)

    wait_for(a_dst.at[pl.ds(0, NY - 1)], recv_sem.at[0])
    b_src[...] = dot(mid[...], a_dst[...].reshape(256, 256)).astype(BF16).reshape(NZ, 16, 256)
    for j in range(1, NZ):
        to = in_z(j)
        send(b_src.at[to], b_dst.at[my_z], 3, {"dom": my_y * NZ + to})
    b_dst[my_z] = b_src[my_z]

    wait_for(qa_dst.at[1], recv_sem.at[1])
    wait_for(qa_dst.at[0], recv_sem.at[2])
    loads[4].wait()
    gz_two = (gz_ref[...] + qa_dst[...].astype(F32).reshape(256, 256)).astype(BF16)
    gh_ref[...] = dot_nt(gz_two, w_two[...]) * inv_deg[...]

    wait_for(b_dst.at[pl.ds(0, NZ - 1)], recv_sem.at[3])
    got = b_dst[...].reshape(256, 256)
    got_ids = got[:, 128:256].astype(F32)
    lane = cols[:, 0:128].astype(F32)
    placing = jnp.concatenate(
        [jnp.where(got_ids == lane, 1.0, 0.0), jnp.where(got_ids == lane + 128.0, 1.0, 0.0)], axis=1
    ).astype(BF16)
    ev_win[128:384] = dot_tn(placing, got[:, 0:128]).astype(BF16)
    send(ev_win.at[pl.ds(128, 128)], ev_win.at[pl.ds(384, 128)], 4, {"dom": left})
    send(ev_win.at[pl.ds(256, 128)], ev_win.at[pl.ds(0, 128)], 5, {"dom": right})

    loads[5].wait()
    loads[6].wait()

    def encoded(rows_in):
        pre_rows = dot(rows_in, w_enc[...])
        return pre_rows, (pre_rows * sigmoid(pre_rows)).astype(BF16)

    ev_own = ev_win[128:384]
    pre, h_zero = encoded(ev_own)
    z_own = dot(h_zero, w_one[...]).astype(BF16)
    total = dot(adj[:, 128:384], z_own)
    wait_for(ev_win.at[pl.ds(384, 128)], recv_sem.at[4])
    wait_for(ev_win.at[pl.ds(0, 128)], recv_sem.at[5])
    for where in (0, 384):
        z_side = dot(encoded(ev_win[where : where + 128])[1], w_one[...]).astype(BF16)
        total = total + dot(adj[:, where : where + 128], z_side)
    agg_one = total * inv_deg[...]
    sig = sigmoid(agg_one)
    h_one = (agg_one * sig).astype(BF16)
    z_two[128:384] = dot(h_one, w_two[...]).astype(BF16)
    send(z_two.at[pl.ds(128, 128)], z_two.at[pl.ds(384, 128)], 6, {"dom": left})
    send(z_two.at[pl.ds(256, 128)], z_two.at[pl.ds(0, 128)], 7, {"dom": right})
    gs_one = (gh_ref[...] * (sig * (1.0 + agg_one * (1.0 - sig)))).astype(BF16)
    qb_src[0] = dot(adj_t[0:128], gs_one).astype(BF16)
    qb_src[1] = dot(adj_t[384:512], gs_one).astype(BF16)
    send(qb_src.at[0], qb_dst.at[1], 8, {"dom": left})
    send(qb_src.at[1], qb_dst.at[0], 9, {"dom": right})
    gz_own = dot(adj_t[128:384], gs_one)
    two_src[...] = dot_tn(h_one, gz_two).astype(BF16).reshape(NZ, 16, 256)
    for j in range(1, NZ):
        to = (my_yc + j) % NZ
        send(two_src.at[to], two_dst.at[my_yc], 10, at_yc(to))
    two_dst[my_yc] = two_src[my_yc]

    wait_for(qb_dst.at[1], recv_sem.at[8])
    wait_for(qb_dst.at[0], recv_sem.at[9])
    gz_one = (gz_own + qb_dst[...].astype(F32).reshape(256, 256)).astype(BF16)
    l_one = dot_tn(h_zero, gz_one).astype(BF16)
    for k in range(NZ):
        r, c = tile(k)
        lo_src[k] = l_one[r : r + 16, c : c + 128]
        hi_src[k, :, 0:128] = l_one[128 + r : 144 + r, c : c + 128]
    for j in range(1, NZ):
        to = (my_yc + j) % NZ
        send(lo_src.at[to], lo_dst.at[my_yc], 11, at_yc(to))
    lo_dst[my_yc] = lo_src[my_yc]
    gh_zero = dot_nt(gz_one, w_one[...]).astype(BF16)
    sig = sigmoid(pre)
    g_enc = (gh_zero.astype(F32) * (sig * (1.0 + pre * (1.0 - sig)))).astype(BF16)
    l_enc = dot_tn(ev_own, g_enc).astype(BF16)
    for k in range(NZ):
        r, c = tile(k)
        hi_src[k, :, 128:256] = l_enc[r : r + 16, c : c + 128]
    for j in range(1, NZ):
        to = in_z(j)
        send(hi_src.at[to], hi_dst.at[my_z], 12, at_zc(to))
    hi_dst[my_z] = hi_src[my_z]

    wait_for(z_two.at[pl.ds(384, 128)], recv_sem.at[6])
    wait_for(z_two.at[pl.ds(0, 128)], recv_sem.at[7])
    embed[0] = (dot(adj[...], z_two[...]) * inv_deg[...]).astype(BF16)

    wait_for(two_dst.at[pl.ds(0, NZ - 1)], recv_sem.at[10])
    wait_for(lo_dst.at[pl.ds(0, NZ - 1)], recv_sem.at[11])
    lo_mid[my_zc, :, 0:256] = jnp.sum(two_dst[...].astype(F32), axis=0).astype(BF16)
    lo_mid[my_zc, :, 256:384] = jnp.sum(lo_dst[...].astype(F32), axis=0).astype(BF16)
    for j in range(1, NY):
        send(lo_mid.at[my_zc], lo_mid.at[my_zc], 13, at_z((my_zc + j) % NY))
    wait_for(hi_dst.at[pl.ds(0, NZ - 1)], recv_sem.at[12])
    hi_mid[my_y] = jnp.sum(hi_dst[...].astype(F32), axis=0).astype(BF16)
    for j in range(1, NY):
        send(hi_mid.at[my_y], hi_mid.at[my_y], 14, at_y((my_y + j) % NY))
    wait_for(lo_mid.at[pl.ds(0, NY - 1)], recv_sem.at[13])
    x_dst[rep, :, 0:384] = jnp.sum(lo_mid[...].astype(F32), axis=0).astype(BF16)
    wait_for(hi_mid.at[pl.ds(0, NY - 1)], recv_sem.at[14])
    x_dst[rep, :, 384:640] = jnp.sum(hi_mid[...].astype(F32), axis=0).astype(BF16)
    for j in range(1, NX):
        send(x_dst.at[rep], x_dst.at[rep], 15, {"rep": in_x(j)})
    wait_for(x_dst.at[pl.ds(0, NX - 1)], recv_sem.at[15])
    summed = jnp.sum(x_dst[...].astype(F32), axis=0).astype(BF16)
    lo_all[my_yc] = summed[:, 0:384]
    hi_all[my_z] = summed[:, 384:640]
    for j in range(1, NZ):
        send(lo_all.at[my_yc], lo_all.at[my_yc], 16, at_yc((my_yc + j) % NZ))
        send(hi_all.at[my_z], hi_all.at[my_z], 17, at_zc(in_z(j)))
    wait_for(hi_all.at[pl.ds(0, NZ - 1)], recv_sem.at[17])
    for k in range(NZ):
        r, c = tile(k)
        grad_one[128 + r : 144 + r, c : c + 128] = hi_all[k, :, 0:128].astype(F32)
        grad_enc[r : r + 16, c : c + 128] = hi_all[k, :, 128:256].astype(F32)
    wait_for(lo_all.at[pl.ds(0, NZ - 1)], recv_sem.at[16])
    grad_two[...] = lo_all[:, :, 0:256].astype(F32).reshape(256, 256)
    for k in range(NZ):
        r, c = tile(k)
        grad_one[r : r + 16, c : c + 128] = lo_all[k, :, 256:384].astype(F32)

    wait_for(a_src.at[pl.ds(0, NY - 1)], send_sem.at[0])
    wait_for(qa_src.at[0], send_sem.at[1])
    wait_for(qa_src.at[1], send_sem.at[2])
    wait_for(b_src.at[pl.ds(0, NZ - 1)], send_sem.at[3])
    for step, ref in ((4, ev_win), (5, ev_win), (6, z_two), (7, z_two)):
        wait_for(ref.at[pl.ds(0, 128)], send_sem.at[step])
    wait_for(qb_src.at[0], send_sem.at[8])
    wait_for(qb_src.at[1], send_sem.at[9])
    wait_for(two_src.at[pl.ds(0, NZ - 1)], send_sem.at[10])
    wait_for(lo_src.at[pl.ds(0, NZ - 1)], send_sem.at[11])
    wait_for(hi_src.at[pl.ds(0, NZ - 1)], send_sem.at[12])
    wait_for(lo_mid.at[pl.ds(0, NY - 1)], send_sem.at[13])
    wait_for(hi_mid.at[pl.ds(0, NY - 1)], send_sem.at[14])
    wait_for(x_dst.at[pl.ds(0, NX - 1)], send_sem.at[15])
    wait_for(lo_all.at[pl.ds(0, NZ - 1)], send_sem.at[16])
    wait_for(hi_all.at[pl.ds(0, NZ - 1)], send_sem.at[17])


def body(events, perm, w_enc, w_one, w_two, slot_blocks, live_count, block_counts, out_grad):
    scale_loss = 1.0 / math.sqrt(lax.axis_size("rep") * lax.axis_size("dom") * events.shape[1])
    vmem = pl.BlockSpec(memory_space=pltpu.VMEM)
    hbm = pl.BlockSpec(memory_space=pltpu.HBM)
    smem = pl.BlockSpec(memory_space=pltpu.SMEM)
    args = [
        pltpu.with_memory_space_constraint(x, pltpu.HBM)
        for x in (events, perm, w_enc, w_one, w_two, block_counts, out_grad)
    ]
    return pl.pallas_call(
        functools.partial(step_kernel, scale_loss),
        out_shape=(
            jax.ShapeDtypeStruct((1, 256, 256), BF16),
            jax.ShapeDtypeStruct((128, 256), F32),
            jax.ShapeDtypeStruct((256, 256), F32),
            jax.ShapeDtypeStruct((256, 256), F32),
        ),
        in_specs=[hbm, hbm, hbm, hbm, hbm, smem, smem, hbm, hbm],
        out_specs=(vmem, vmem, vmem, vmem),
        scratch_shapes=[
            pltpu.VMEM((1, 256, 128), BF16),
            pltpu.VMEM((1, 256), jnp.int32),
            pltpu.VMEM((128, 256), BF16),
            pltpu.VMEM((256, 256), BF16),
            pltpu.VMEM((256, 256), BF16),
            pltpu.VMEM((1, 10, 128, 128), jnp.int32),
            pltpu.VMEM((1, 256, 256), BF16),
            pltpu.VMEM((256, 512), F32),
            pltpu.VMEM((256, 512), BF16),
            pltpu.VMEM((512, 256), BF16),
            pltpu.VMEM((256, 256), F32),
            pltpu.VMEM((256, 256), BF16),
            pltpu.VMEM((512, 128), BF16),
            pltpu.VMEM((512, 256), BF16),
            pltpu.VMEM((256, 256), F32),
            pltpu.VMEM((256, 256), F32),
            pltpu.VMEM((NY, 32, 256), BF16),
            pltpu.VMEM((NY, 32, 256), BF16),
            pltpu.VMEM((NZ, 16, 256), BF16),
            pltpu.VMEM((NZ, 16, 256), BF16),
            pltpu.VMEM((2, 128, 256), BF16),
            pltpu.VMEM((2, 128, 256), BF16),
            pltpu.VMEM((2, 128, 256), BF16),
            pltpu.VMEM((2, 128, 256), BF16),
            pltpu.VMEM((NZ, 16, 256), BF16),
            pltpu.VMEM((NZ, 16, 256), BF16),
            pltpu.VMEM((NZ, 16, 128), BF16),
            pltpu.VMEM((NZ, 16, 128), BF16),
            pltpu.VMEM((NY, 16, 384), BF16),
            pltpu.VMEM((NZ, 16, 384), BF16),
            pltpu.VMEM((NZ, 16, 256), BF16),
            pltpu.VMEM((NZ, 16, 256), BF16),
            pltpu.VMEM((NY, 16, 256), BF16),
            pltpu.VMEM((NZ, 16, 256), BF16),
            pltpu.VMEM((NX, 16, 640), BF16),
            pltpu.SemaphoreType.DMA((7,)),
            pltpu.SemaphoreType.DMA((18,)),
            pltpu.SemaphoreType.DMA((18,)),
        ],
        compiler_params=pltpu.CompilerParams(
            collective_id=0, has_side_effects=True, vmem_limit_bytes=16 * 1024 * 1024
        ),
    )(*args[:5], slot_blocks, live_count, *args[5:])


def solution(mesh):
    return jax.shard_map(
        body,
        mesh=mesh,
        in_specs=(
            P("rep", "dom", None),
            P("rep", "dom"),
            P(),
            P(),
            P(),
            P("rep", "dom", None),
            P("rep", "dom"),
            P("rep", "dom", None, None),
            P("rep", "dom", None),
        ),
        out_specs=(P("rep", "dom", None), P(), P(), P()),
        check_vma=False,
    )
```

```python
import functools
import math

import jax
import jax.numpy as jnp
from jax import lax
from jax.experimental import pallas as pl
from jax.experimental.pallas import tpu as pltpu
from jax.sharding import PartitionSpec as P

loop_weight = 4.0
NY = 8
NZ = 16
NX = 4
F32 = jnp.float32
BF16 = jnp.bfloat16


def dot(a, b):
    return jnp.dot(a, b, preferred_element_type=F32)


def dot_nt(a, b):
    return lax.dot_general(a, b, (((1,), (1,)), ((), ())), preferred_element_type=F32)


def sigmoid(value):
    return 1.0 / (1.0 + jnp.exp(-value))


def wait_for(ref, sem):
    pltpu.make_async_copy(ref, ref, sem).wait()


def tile(k):
    return 16 * (k // 2), 128 * (k % 2)


def iota(shape, dim):
    return lax.broadcasted_iota(jnp.int32, shape, dim)


def one_where(mask):
    return jnp.where(mask, 1.0, 0.0).astype(BF16)


def step_kernel(
    scale_loss,
    events_in, perm_in, w_enc_in, w_one_in, w_two_in, slots_in, live, counts_in, out_grad_in,
    embed, grad_enc, grad_one, grad_two,
    events, perm, w_enc, w_one, w_two, counts, out_grad, slots,
    adj_f, adj, adj_t, inv_deg, mid, regroup, spread, finish, w_one_t, w_two_t,
    ev_win, z_two, gz_ref, gh_ref,
    a_src, a_dst, ai_src, ai_dst, b_src, b_dst, bi_src, bi_dst, qa_src, qa_dst, qb_src, qb_dst,
    two_src, two_dst, two_mid, two_x, two_all,
    lo_src, lo_dst, lo_mid, lo_all, hi_src, hi_dst, hi_mid, hi_all, late_x,
    load_sem, send_sem, recv_sem,
):
    me = lax.axis_index("dom")
    rep = lax.axis_index("rep")
    ndom = NY * NZ
    my_y = me // NZ
    my_z = me % NZ
    core = me % 2
    my_yc = my_y * 2 + core
    my_zc = my_z // 2
    left = {"dom": (me + ndom - 1) % ndom}
    right = {"dom": (me + 1) % ndom}

    loads = [
        pltpu.make_async_copy(src, dst, load_sem.at[i])
        for i, (src, dst) in enumerate(
            (
                (perm_in, perm), (events_in, events), (slots_in, slots), (counts_in, counts),
                (out_grad_in, out_grad), (w_two_in, w_two), (w_enc_in, w_enc), (w_one_in, w_one),
            )
        )
    ]
    for load in loads:
        load.start()

    def others(group):
        if group == "yc":
            ranks = [(my_yc + j) % NZ for j in range(1, NZ)]
            return [(k, {"dom": (k // 2) * NZ + my_zc * 2 + k % 2}) for k in ranks]
        if group == "zc":
            return [(k, {"dom": my_y * NZ + k}) for k in ((my_z + j) % NZ for j in range(1, NZ))]
        if group == "y":
            return [(k, {"dom": k * NZ + my_z}) for k in ((my_y + j) % NY for j in range(1, NY))]
        if group == "z":
            ranks = [(my_zc + j) % NY for j in range(1, NY)]
            return [(k, {"dom": my_y * NZ + k * 2 + core}) for k in ranks]
        return [(k, {"rep": k}) for k in ((rep + j) % NX for j in range(1, NX))]

    barrier = pltpu.get_barrier_semaphore()
    friends = [dev for group in ("yc", "zc", "x") for _, dev in others(group)] + [left, right]
    for device in friends:
        pl.semaphore_signal(barrier, inc=1, device_id=device, device_id_type=pl.DeviceIdType.MESH)

    def send(src, dst, step, device):
        pltpu.make_async_remote_copy(
            src_ref=src, dst_ref=dst, send_sem=send_sem.at[step], recv_sem=recv_sem.at[step],
            device_id=device, device_id_type=pl.DeviceIdType.MESH,
        ).start()

    def scatter(src, dst, mine, step, group):
        for k, device in others(group):
            send(src.at[k], dst.at[mine], step, device)
        dst[mine] = src[mine]

    def spread_out(ref, mine, step, group):
        for _, device in others(group):
            send(ref.at[mine], ref.at[mine], step, device)

    def arrived(ref, step, count):
        wait_for(ref.at[pl.ds(0, count)], recv_sem.at[step])

    def left_all(ref, step, count):
        wait_for(ref.at[pl.ds(0, count)], send_sem.at[step])

    rows = iota((256, 256), 0)
    cols = iota((256, 256), 1)
    half_rows = rows[0:128]
    half_cols = cols[0:128]
    loads[0].wait()
    ids = perm[...]
    ids_row = ids.astype(F32)
    ids_col = jnp.sum(jnp.where(rows == cols, ids_row, 0.0), axis=1, keepdims=True)
    place = jnp.sum(jnp.where(ids_col < ids_row, 1.0, 0.0), axis=0, keepdims=True).astype(jnp.int32)
    local_row = (ids & 255).astype(F32)
    id_left = jnp.where((place >> 5) == rows[0:16], local_row, 0.0).astype(BF16)
    id_right = one_where((place & 31) == half_rows)
    ai_src[...] = dot_nt(id_left, id_right)[0:NY].reshape(NY, 1, 128)
    loads[1].wait()
    a_src[...] = dot(one_where(rows == place), events[0]).astype(BF16).reshape(NY, 32, 128)

    pl.semaphore_wait(barrier, len(friends))
    scatter(ai_src, ai_dst, my_y, 1, "y")
    scatter(a_src, a_dst, my_y, 0, "y")

    loads[2].wait()
    loads[3].wait()
    weights = []
    for s in range(10):
        row = slots[0, 0, s] - 2 * me
        col = (slots[0, 1, s] - 2 * me + 1 + 2 * ndom) % (2 * ndom)
        used = s < live[0, 0]
        weights.append(
            [
                [jnp.where(used & (row == r) & (col == c), 1.0, 0.0) for c in (1, 2, 0, 3)]
                for r in range(2)
            ]
        )
    for part in range(4):
        here = slice(part * 32, part * 32 + 32)
        sums = [[None] * 4 for _ in range(2)]
        for s in range(10):
            cell = counts[0, s, here, :].astype(F32)
            for r in range(2):
                for c in range(4):
                    term = cell * weights[s][r][c]
                    sums[r][c] = term if s == 0 else sums[r][c] + term
        diag = iota((32, 128), 0) + part * 32 == iota((32, 128), 1)
        for r in range(2):
            sums[r][r] = sums[r][r] + jnp.where(diag, loop_weight, 0.0)
            for c in range(4):
                adj_f[r * 128 + part * 32 : r * 128 + part * 32 + 32, c * 128 : c * 128 + 128] = sums[r][c]
    adj[...] = adj_f[...].astype(BF16)
    for r in range(2):
        for c in range(4):
            adj_t[c * 128 : c * 128 + 128, r * 128 : r * 128 + 128] = (
                adj_f[r * 128 : r * 128 + 128, c * 128 : c * 128 + 128].T.astype(BF16)
            )
    inverse = 1.0 / dot(adj[...], jnp.ones((512, 128), BF16))
    inv_deg[:, 0:128] = inverse
    inv_deg[:, 128:256] = inverse

    loads[4].wait()
    gs_two = (out_grad[0].astype(F32) * scale_loss * inv_deg[...]).astype(BF16)
    qa_src[...] = dot(adj_t[256:512], gs_two).astype(BF16).reshape(2, 128, 256)
    send(qa_src.at[0], qa_dst.at[1], 4, left)
    send(qa_src.at[1], qa_dst.at[0], 5, right)
    gz_ref[...] = dot(adj_t[0:256], gs_two)

    source = ((rows >> 1) & (NY - 1)) * 32 + (rows >> 4) * 2 + (rows & 1)
    mid[...] = one_where(cols == source)
    regroup[...] = one_where(half_rows == (half_cols >> 4) * 2 + (half_cols & 1))
    spread[...] = one_where(half_rows == (half_cols & 15))
    loads[5].wait()
    loads[6].wait()
    loads[7].wait()
    w_two_t[...] = w_two[...].T
    w_one_t[...] = w_one[...].T

    arrived(ai_dst, 1, NY - 1)
    ids_mid = dot(ai_dst[...].reshape(NY, 128).astype(BF16), regroup[...])
    ids_mid = jnp.sum(
        jnp.where(rows[0:NY] == ((cols[0:NY] >> 1) & (NY - 1)), ids_mid, 0.0), axis=0, keepdims=True
    )
    id_left = jnp.where((cols[0:NZ] >> 4) == rows[0:NZ], ids_mid, 0.0).astype(BF16)
    bi_src[...] = dot_nt(id_left, spread[...]).reshape(NZ, 1, 128)
    scatter(bi_src, bi_dst, my_z, 3, "zc")
    arrived(a_dst, 0, NY - 1)
    b_src[...] = dot(mid[...], a_dst[...].reshape(256, 128)).astype(BF16).reshape(NZ, 16, 128)
    scatter(b_src, b_dst, my_z, 2, "zc")

    wait_for(qa_dst.at[1], recv_sem.at[4])
    wait_for(qa_dst.at[0], recv_sem.at[5])
    gz_two = (gz_ref[...] + qa_dst[...].astype(F32).reshape(256, 256)).astype(BF16)
    gh_ref[...] = dot(gz_two, w_two_t[...]) * inv_deg[...]

    arrived(bi_dst, 3, NZ - 1)
    ids_got = dot(bi_dst[...].reshape(NZ, 128).astype(BF16), spread[...])
    ids_got = jnp.sum(
        jnp.where(rows[0:NZ] == (cols[0:NZ] >> 4), ids_got, 0.0), axis=0, keepdims=True
    )
    finish[...] = one_where(rows.astype(F32) == ids_got)
    arrived(b_dst, 2, NZ - 1)
    ev_own = dot(finish[...], b_dst[...].reshape(256, 128)).astype(BF16)
    ev_win[0:256] = ev_own
    send(ev_win.at[pl.ds(0, 128)], ev_win.at[pl.ds(384, 128)], 6, left)
    send(ev_win.at[pl.ds(128, 128)], ev_win.at[pl.ds(256, 128)], 7, right)

    def encoded(rows_in):
        pre_rows = dot(rows_in, w_enc[...])
        return pre_rows, (pre_rows * sigmoid(pre_rows)).astype(BF16)

    pre, h_zero = encoded(ev_own)
    z_own = dot(h_zero, w_one[...]).astype(BF16)
    total = dot(adj[:, 0:256], z_own)
    sig = sigmoid(pre)
    enc_slope = sig * (1.0 + pre * (1.0 - sig))
    h_zero_t = h_zero.T
    ev_t = ev_own.T
    wait_for(ev_win.at[pl.ds(384, 128)], recv_sem.at[6])
    wait_for(ev_win.at[pl.ds(256, 128)], recv_sem.at[7])
    z_side = dot(encoded(ev_win[256:512])[1], w_one[...]).astype(BF16)
    agg_one = (total + dot(adj[:, 256:512], z_side)) * inv_deg[...]
    sig = sigmoid(agg_one)
    gs_one = (gh_ref[...] * (sig * (1.0 + agg_one * (1.0 - sig)))).astype(BF16)
    qb_src[...] = dot(adj_t[256:512], gs_one).astype(BF16).reshape(2, 128, 256)
    send(qb_src.at[0], qb_dst.at[1], 10, left)
    send(qb_src.at[1], qb_dst.at[0], 11, right)
    h_one = (agg_one * sig).astype(BF16)
    two_src[...] = dot(h_one.T, gz_two).astype(BF16).reshape(NZ, 16, 256)
    scatter(two_src, two_dst, my_yc, 12, "yc")
    z_two[0:256] = dot(h_one, w_two[...]).astype(BF16)
    send(z_two.at[pl.ds(0, 128)], z_two.at[pl.ds(384, 128)], 8, left)
    send(z_two.at[pl.ds(128, 128)], z_two.at[pl.ds(256, 128)], 9, right)
    gz_own = dot(adj_t[0:256], gs_one)

    wait_for(qb_dst.at[1], recv_sem.at[10])
    wait_for(qb_dst.at[0], recv_sem.at[11])
    gz_one = (gz_own + qb_dst[...].astype(F32).reshape(256, 256)).astype(BF16)
    l_one = dot(h_zero_t, gz_one).astype(BF16)
    for k in range(NZ):
        r, c = tile(k)
        lo_src[k] = l_one[r : r + 16, c : c + 128]
        hi_src[k, :, 0:128] = l_one[128 + r : 144 + r, c : c + 128]
    scatter(lo_src, lo_dst, my_yc, 13, "yc")
    gh_zero = dot(gz_one, w_one_t[...]).astype(BF16)
    g_enc = (gh_zero.astype(F32) * enc_slope).astype(BF16)
    l_enc = dot(ev_t, g_enc).astype(BF16)
    for k in range(NZ):
        r, c = tile(k)
        hi_src[k, :, 128:256] = l_enc[r : r + 16, c : c + 128]
    scatter(hi_src, hi_dst, my_z, 14, "zc")

    wait_for(z_two.at[pl.ds(384, 128)], recv_sem.at[8])
    wait_for(z_two.at[pl.ds(256, 128)], recv_sem.at[9])
    embed[0] = (dot(adj[...], z_two[...]) * inv_deg[...]).astype(BF16)

    def summed(ref):
        return jnp.sum(ref[...].astype(F32), axis=0).astype(BF16)

    arrived(two_dst, 12, NZ - 1)
    two_mid[my_zc] = summed(two_dst)
    spread_out(two_mid, my_zc, 15, "z")
    arrived(lo_dst, 13, NZ - 1)
    lo_mid[my_zc] = summed(lo_dst)
    spread_out(lo_mid, my_zc, 16, "z")
    arrived(hi_dst, 14, NZ - 1)
    hi_mid[my_y] = summed(hi_dst)
    spread_out(hi_mid, my_y, 17, "y")
    arrived(two_mid, 15, NY - 1)
    two_x[rep] = summed(two_mid)
    spread_out(two_x, rep, 18, "x")
    arrived(lo_mid, 16, NY - 1)
    late_x[rep, :, 0:128] = summed(lo_mid)
    arrived(hi_mid, 17, NY - 1)
    late_x[rep, :, 128:384] = summed(hi_mid)
    spread_out(late_x, rep, 19, "x")
    arrived(two_x, 18, NX - 1)
    two_all[my_yc] = summed(two_x)
    spread_out(two_all, my_yc, 20, "yc")
    arrived(late_x, 19, NX - 1)
    late = summed(late_x)
    hi_all[my_z] = late[:, 128:384]
    spread_out(hi_all, my_z, 22, "zc")
    lo_all[my_yc] = late[:, 0:128]
    spread_out(lo_all, my_yc, 21, "yc")
    arrived(two_all, 20, NZ - 1)
    grad_two[...] = two_all[...].astype(F32).reshape(256, 256)
    arrived(lo_all, 21, NZ - 1)
    for k in range(NZ):
        r, c = tile(k)
        grad_one[r : r + 16, c : c + 128] = lo_all[k].astype(F32)
    arrived(hi_all, 22, NZ - 1)
    for k in range(NZ):
        r, c = tile(k)
        grad_one[128 + r : 144 + r, c : c + 128] = hi_all[k, :, 0:128].astype(F32)
        grad_enc[r : r + 16, c : c + 128] = hi_all[k, :, 128:256].astype(F32)

    left_all(a_src, 0, NY - 1)
    left_all(ai_src, 1, NY - 1)
    left_all(b_src, 2, NZ - 1)
    left_all(bi_src, 3, NZ - 1)
    for step, ref in ((4, qa_src), (5, qa_src), (10, qb_src), (11, qb_src)):
        left_all(ref, step, 1)
    for step, ref in ((6, ev_win), (7, ev_win), (8, z_two), (9, z_two)):
        left_all(ref, step, 128)
    for step, ref in ((12, two_src), (13, lo_src), (14, hi_src), (20, two_all), (21, lo_all), (22, hi_all)):
        left_all(ref, step, NZ - 1)
    for step, ref in ((15, two_mid), (16, lo_mid), (17, hi_mid)):
        left_all(ref, step, NY - 1)
    left_all(two_x, 18, NX - 1)
    left_all(late_x, 19, NX - 1)


def body(events, perm, w_enc, w_one, w_two, slot_blocks, live_count, block_counts, out_grad):
    scale_loss = 1.0 / math.sqrt(lax.axis_size("rep") * lax.axis_size("dom") * events.shape[1])
    vmem = pl.BlockSpec(memory_space=pltpu.VMEM)
    smem = pl.BlockSpec(memory_space=pltpu.SMEM)
    hbm = pl.BlockSpec(memory_space=pltpu.HBM)
    slot_rows = jnp.swapaxes(slot_blocks, 1, 2)
    args = [
        pltpu.with_memory_space_constraint(x, pltpu.HBM)
        for x in (events, perm, w_enc, w_one, w_two, slot_rows, block_counts, out_grad)
    ]

    def pieces(*shape, dtype=BF16):
        return pltpu.VMEM(shape, dtype)

    return pl.pallas_call(
        functools.partial(step_kernel, scale_loss),
        out_shape=(
            jax.ShapeDtypeStruct((1, 256, 256), BF16),
            jax.ShapeDtypeStruct((128, 256), F32),
            jax.ShapeDtypeStruct((256, 256), F32),
            jax.ShapeDtypeStruct((256, 256), F32),
        ),
        in_specs=[hbm, hbm, hbm, hbm, hbm, hbm, smem, hbm, hbm],
        out_specs=(vmem, vmem, vmem, vmem),
        scratch_shapes=[
            pieces(1, 256, 128),
            pieces(1, 256, dtype=jnp.int32),
            pieces(128, 256),
            pieces(256, 256),
            pieces(256, 256),
            pieces(1, 10, 128, 128, dtype=jnp.int32),
            pieces(1, 256, 256),
            pltpu.SMEM((1, 2, 10), jnp.int32),
            pieces(256, 512, dtype=F32),
            pieces(256, 512),
            pieces(512, 256),
            pieces(256, 256, dtype=F32),
            pieces(256, 256),
            pieces(128, 256),
            pieces(128, 256),
            pieces(256, 256),
            pieces(256, 256),
            pieces(256, 256),
            pieces(512, 128),
            pieces(512, 256),
            pieces(256, 256, dtype=F32),
            pieces(256, 256, dtype=F32),
            pieces(NY, 32, 128),
            pieces(NY, 32, 128),
            pieces(NY, 1, 128, dtype=F32),
            pieces(NY, 1, 128, dtype=F32),
            pieces(NZ, 16, 128),
            pieces(NZ, 16, 128),
            pieces(NZ, 1, 128, dtype=F32),
            pieces(NZ, 1, 128, dtype=F32),
            pieces(2, 128, 256),
            pieces(2, 128, 256),
            pieces(2, 128, 256),
            pieces(2, 128, 256),
            pieces(NZ, 16, 256),
            pieces(NZ, 16, 256),
            pieces(NY, 16, 256),
            pieces(NX, 16, 256),
            pieces(NZ, 16, 256),
            pieces(NZ, 16, 128),
            pieces(NZ, 16, 128),
            pieces(NY, 16, 128),
            pieces(NZ, 16, 128),
            pieces(NZ, 16, 256),
            pieces(NZ, 16, 256),
            pieces(NY, 16, 256),
            pieces(NZ, 16, 256),
            pieces(NX, 16, 384),
            pltpu.SemaphoreType.DMA((8,)),
            pltpu.SemaphoreType.DMA((23,)),
            pltpu.SemaphoreType.DMA((23,)),
        ],
        compiler_params=pltpu.CompilerParams(
            collective_id=0, has_side_effects=True, vmem_limit_bytes=16 * 1024 * 1024
        ),
    )(*args[:6], live_count, *args[6:])


def solution(mesh):
    return jax.shard_map(
        body,
        mesh=mesh,
        in_specs=(
            P("rep", "dom", None),
            P("rep", "dom"),
            P(),
            P(),
            P(),
            P("rep", "dom", None),
            P("rep", "dom"),
            P("rep", "dom", None, None),
            P("rep", "dom", None),
        ),
        out_specs=(P("rep", "dom", None), P(), P(), P()),
        check_vma=False,
    )
```

```python
import functools
import math

import jax
import jax.numpy as jnp
from jax import lax
from jax.experimental import pallas as pl
from jax.experimental.pallas import tpu as pltpu
from jax.sharding import PartitionSpec as P

loop_weight = 4.0
NY = 8
NZ = 16
NX = 4
F32 = jnp.float32
BF16 = jnp.bfloat16


def dot(a, b):
    return jnp.dot(a, b, preferred_element_type=F32)


def dot_nt(a, b):
    return lax.dot_general(a, b, (((1,), (1,)), ((), ())), preferred_element_type=F32)


def sigmoid(value):
    return 1.0 / (1.0 + jnp.exp(-value))


def wait_for(ref, sem):
    pltpu.make_async_copy(ref, ref, sem).wait()


def iota(shape, dim):
    return lax.broadcasted_iota(jnp.int32, shape, dim)


def one_where(mask):
    return jnp.where(mask, 1.0, 0.0).astype(BF16)


def step_kernel(
    scale_loss,
    events_in, perm_in, w_enc_in, w_one_in, w_two_in, slots_in, live, counts_in, out_grad_in,
    embed, grad_enc, grad_one, grad_two,
    events, perm, w_enc, w_one, w_two, counts, out_grad, slots,
    adj_f, adj, adj_t, inv_deg, mid, regroup, spread, finish, w_one_t, w_two_t,
    ev_win, z_two, gz_ref, gh_ref,
    a_src, a_dst, ai_src, ai_dst, b_src, b_dst, bi_src, bi_dst, qa_src, qa_dst,
    two_src, two_dst, two_mid, two_x, two_all, one_src, one_dst, one_mid, one_x, one_all,
    enc_src, enc_dst, enc_y, enc_z, enc_all, h_win_t, ev_win_t, slope,
    load_sem, send_sem, recv_sem,
):
    me = lax.axis_index("dom")
    rep = lax.axis_index("rep")
    ndom = NY * NZ
    my_y = me // NZ
    my_z = me % NZ
    core = me % 2
    my_yc = my_y * 2 + core
    my_xc = rep * 2 + core
    my_zc = my_z // 2
    left = {"dom": (me + ndom - 1) % ndom}
    right = {"dom": (me + 1) % ndom}

    loads = [
        pltpu.make_async_copy(src, dst, load_sem.at[i])
        for i, (src, dst) in enumerate(
            (
                (perm_in, perm), (events_in, events), (slots_in, slots), (counts_in, counts),
                (out_grad_in, out_grad), (w_two_in, w_two), (w_enc_in, w_enc), (w_one_in, w_one),
            )
        )
    ]
    for load in loads:
        load.start()

    def others(group):
        if group == "yc":
            ranks = [(my_yc + j) % NZ for j in range(1, NZ)]
            return [(k, {"dom": (k // 2) * NZ + my_zc * 2 + k % 2}) for k in ranks]
        if group == "zc":
            return [(k, {"dom": my_y * NZ + k}) for k in ((my_z + j) % NZ for j in range(1, NZ))]
        if group == "y":
            return [(k, {"dom": k * NZ + my_z}) for k in ((my_y + j) % NY for j in range(1, NY))]
        if group == "z":
            ranks = [(my_zc + j) % NY for j in range(1, NY)]
            return [(k, {"dom": my_y * NZ + k * 2 + core}) for k in ranks]
        if group == "xc":
            ranks = [(my_xc + j) % NY for j in range(1, NY)]
            return [(k, {"dom": me - core + k % 2, "rep": k // 2}) for k in ranks]
        return [(k, {"rep": k}) for k in ((rep + j) % NX for j in range(1, NX))]

    barrier = pltpu.get_barrier_semaphore()
    friends = [dev for group in ("yc", "zc", "xc") for _, dev in others(group)] + [left, right]
    for device in friends:
        pl.semaphore_signal(barrier, inc=1, device_id=device, device_id_type=pl.DeviceIdType.MESH)

    def send(src, dst, step, device):
        pltpu.make_async_remote_copy(
            src_ref=src, dst_ref=dst, send_sem=send_sem.at[step], recv_sem=recv_sem.at[step],
            device_id=device, device_id_type=pl.DeviceIdType.MESH,
        ).start()

    def scatter(src, dst, mine, step, group):
        for k, device in others(group):
            send(src.at[k], dst.at[mine], step, device)
        dst[mine] = src[mine]

    def spread_out(ref, mine, step, group):
        for _, device in others(group):
            send(ref.at[mine], ref.at[mine], step, device)

    def arrived(ref, step, count):
        wait_for(ref.at[pl.ds(0, count)], recv_sem.at[step])

    def left_all(ref, step, count):
        wait_for(ref.at[pl.ds(0, count)], send_sem.at[step])

    rows = iota((256, 256), 0)
    cols = iota((256, 256), 1)
    half_rows = rows[0:128]
    half_cols = cols[0:128]
    loads[0].wait()
    ids = perm[...]
    ids_row = ids.astype(F32)
    ids_col = jnp.sum(jnp.where(rows == cols, ids_row, 0.0), axis=1, keepdims=True)
    place = jnp.sum(jnp.where(ids_col < ids_row, 1.0, 0.0), axis=0, keepdims=True).astype(jnp.int32)
    local_row = (ids & 255).astype(F32)
    id_left = jnp.where((place >> 5) == rows[0:16], local_row, 0.0).astype(BF16)
    id_right = one_where((place & 31) == half_rows)
    ai_src[...] = dot_nt(id_left, id_right)[0:NY].reshape(NY, 1, 128)
    loads[1].wait()
    a_src[...] = dot(one_where(rows == place), events[0]).astype(BF16).reshape(NY, 32, 128)

    pl.semaphore_wait(barrier, len(friends))
    scatter(ai_src, ai_dst, my_y, 1, "y")
    scatter(a_src, a_dst, my_y, 0, "y")

    loads[2].wait()
    loads[3].wait()
    weights = []
    for s in range(10):
        row = slots[0, 0, s] - 2 * me
        col = (slots[0, 1, s] - 2 * me + 1 + 2 * ndom) % (2 * ndom)
        used = s < live[0, 0]
        weights.append(
            [
                [jnp.where(used & (row == r) & (col == c), 1.0, 0.0) for c in (1, 2, 0, 3)]
                for r in range(2)
            ]
        )
    for part in range(4):
        here = slice(part * 32, part * 32 + 32)
        sums = [[None] * 4 for _ in range(2)]
        for s in range(10):
            cell = counts[0, s, here, :].astype(F32)
            for r in range(2):
                for c in range(4):
                    term = cell * weights[s][r][c]
                    sums[r][c] = term if s == 0 else sums[r][c] + term
        diag = iota((32, 128), 0) + part * 32 == iota((32, 128), 1)
        for r in range(2):
            sums[r][r] = sums[r][r] + jnp.where(diag, loop_weight, 0.0)
            for c in range(4):
                adj_f[r * 128 + part * 32 : r * 128 + part * 32 + 32, c * 128 : c * 128 + 128] = sums[r][c]
    adj[...] = adj_f[...].astype(BF16)
    for r in range(2):
        for c in range(4):
            adj_t[c * 128 : c * 128 + 128, r * 128 : r * 128 + 128] = (
                adj_f[r * 128 : r * 128 + 128, c * 128 : c * 128 + 128].T.astype(BF16)
            )
    inverse = 1.0 / dot(adj[...], jnp.ones((512, 128), BF16))
    inv_deg[:, 0:128] = inverse
    inv_deg[:, 128:256] = inverse

    loads[4].wait()
    gs_two = (out_grad[0].astype(F32) * scale_loss * inv_deg[...]).astype(BF16)
    qa_src[...] = dot(adj_t[256:512], gs_two).astype(BF16).reshape(2, 128, 256)
    send(qa_src.at[0], qa_dst.at[1], 4, left)
    send(qa_src.at[1], qa_dst.at[0], 5, right)
    gz_ref[...] = dot(adj_t[0:256], gs_two)

    source = ((rows >> 1) & (NY - 1)) * 32 + (rows >> 4) * 2 + (rows & 1)
    mid[...] = one_where(cols == source)
    regroup[...] = one_where(half_rows == (half_cols >> 4) * 2 + (half_cols & 1))
    spread[...] = one_where(half_rows == (half_cols & 15))
    loads[5].wait()
    loads[6].wait()
    loads[7].wait()
    w_two_t[...] = w_two[...].T
    w_one_t[...] = w_one[...].T

    arrived(ai_dst, 1, NY - 1)
    ids_mid = dot(ai_dst[...].reshape(NY, 128).astype(BF16), regroup[...])
    ids_mid = jnp.sum(
        jnp.where(rows[0:NY] == ((cols[0:NY] >> 1) & (NY - 1)), ids_mid, 0.0), axis=0, keepdims=True
    )
    id_left = jnp.where((cols[0:NZ] >> 4) == rows[0:NZ], ids_mid, 0.0).astype(BF16)
    bi_src[...] = dot_nt(id_left, spread[...]).reshape(NZ, 1, 128)
    scatter(bi_src, bi_dst, my_z, 3, "zc")
    arrived(a_dst, 0, NY - 1)
    b_src[...] = dot(mid[...], a_dst[...].reshape(256, 128)).astype(BF16).reshape(NZ, 16, 128)
    scatter(b_src, b_dst, my_z, 2, "zc")

    wait_for(qa_dst.at[1], recv_sem.at[4])
    wait_for(qa_dst.at[0], recv_sem.at[5])
    gz_two = (gz_ref[...] + qa_dst[...].astype(F32).reshape(256, 256)).astype(BF16)
    gh_ref[...] = dot(gz_two, w_two_t[...]) * inv_deg[...]

    arrived(bi_dst, 3, NZ - 1)
    ids_got = dot(bi_dst[...].reshape(NZ, 128).astype(BF16), spread[...])
    ids_got = jnp.sum(
        jnp.where(rows[0:NZ] == (cols[0:NZ] >> 4), ids_got, 0.0), axis=0, keepdims=True
    )
    finish[...] = one_where(rows.astype(F32) == ids_got)
    arrived(b_dst, 2, NZ - 1)
    ev_own = dot(finish[...], b_dst[...].reshape(256, 128)).astype(BF16)
    ev_win[0:256] = ev_own
    send(ev_win.at[pl.ds(0, 128)], ev_win.at[pl.ds(384, 128)], 6, left)
    send(ev_win.at[pl.ds(128, 128)], ev_win.at[pl.ds(256, 128)], 7, right)

    def encoded(rows_in):
        pre_rows = dot(rows_in, w_enc[...])
        return pre_rows, (pre_rows * sigmoid(pre_rows)).astype(BF16)

    pre, h_zero = encoded(ev_own)
    z_own = dot(h_zero, w_one[...]).astype(BF16)
    total = dot(adj[:, 0:256], z_own)
    sig = sigmoid(pre)
    slope[0:256] = sig * (1.0 + pre * (1.0 - sig))
    h_win_t[:, 0:256] = h_zero.T
    ev_win_t[:, 0:256] = ev_own.T
    wait_for(ev_win.at[pl.ds(384, 128)], recv_sem.at[6])
    wait_for(ev_win.at[pl.ds(256, 128)], recv_sem.at[7])
    ev_side = ev_win[256:512]
    pre, h_zero = encoded(ev_side)
    z_side = dot(h_zero, w_one[...]).astype(BF16)
    agg_one = (total + dot(adj[:, 256:512], z_side)) * inv_deg[...]
    h_win_t[:, 256:512] = h_zero.T
    ev_win_t[:, 256:512] = ev_side.T
    sig = sigmoid(pre)
    slope[256:512] = sig * (1.0 + pre * (1.0 - sig))

    sig = sigmoid(agg_one)
    gs_one = (gh_ref[...] * (sig * (1.0 + agg_one * (1.0 - sig)))).astype(BF16)
    gz_one = dot(adj_t[...], gs_one).astype(BF16)
    one_src[...] = dot(h_win_t[...], gz_one).astype(BF16).reshape(NZ, 16, 256)
    scatter(one_src, one_dst, my_z, 10, "zc")
    h_one = (agg_one * sig).astype(BF16)
    two_src[...] = dot(h_one.T, gz_two).astype(BF16).reshape(NZ, 16, 256)
    scatter(two_src, two_dst, my_yc, 11, "yc")
    gh_zero = dot(gz_one, w_one_t[...]).astype(BF16)
    g_enc = (gh_zero.astype(F32) * slope[...]).astype(BF16)
    enc_src[...] = dot(ev_win_t[...], g_enc).astype(BF16).reshape(NY, 16, 256)
    scatter(enc_src, enc_dst, my_xc, 12, "xc")
    z_two[0:256] = dot(h_one, w_two[...]).astype(BF16)
    send(z_two.at[pl.ds(0, 128)], z_two.at[pl.ds(384, 128)], 8, left)
    send(z_two.at[pl.ds(128, 128)], z_two.at[pl.ds(256, 128)], 9, right)

    def summed(ref):
        return jnp.sum(ref[...].astype(F32), axis=0).astype(BF16)

    arrived(enc_dst, 12, NY - 1)
    enc_y[my_y] = summed(enc_dst)
    spread_out(enc_y, my_y, 13, "y")
    arrived(one_dst, 10, NZ - 1)
    one_mid[my_y] = summed(one_dst)
    spread_out(one_mid, my_y, 14, "y")
    arrived(two_dst, 11, NZ - 1)
    two_mid[my_zc] = summed(two_dst)
    spread_out(two_mid, my_zc, 15, "z")
    wait_for(z_two.at[pl.ds(384, 128)], recv_sem.at[8])
    wait_for(z_two.at[pl.ds(256, 128)], recv_sem.at[9])
    embed[0] = (dot(adj[...], z_two[...]) * inv_deg[...]).astype(BF16)
    arrived(enc_y, 13, NY - 1)
    enc_z[my_zc] = summed(enc_y)
    spread_out(enc_z, my_zc, 16, "z")
    arrived(one_mid, 14, NY - 1)
    one_x[rep] = summed(one_mid)
    spread_out(one_x, rep, 17, "x")
    arrived(two_mid, 15, NY - 1)
    two_x[rep] = summed(two_mid)
    spread_out(two_x, rep, 18, "x")
    arrived(one_x, 17, NX - 1)
    one_all[my_z] = summed(one_x)
    spread_out(one_all, my_z, 19, "zc")
    arrived(two_x, 18, NX - 1)
    two_all[my_yc] = summed(two_x)
    spread_out(two_all, my_yc, 20, "yc")
    arrived(enc_z, 16, NY - 1)
    enc_all[my_xc] = summed(enc_z)
    spread_out(enc_all, my_xc, 21, "xc")
    arrived(enc_all, 21, NY - 1)
    grad_enc[...] = enc_all[...].astype(F32).reshape(128, 256)
    arrived(one_all, 19, NZ - 1)
    grad_one[...] = one_all[...].astype(F32).reshape(256, 256)
    arrived(two_all, 20, NZ - 1)
    grad_two[...] = two_all[...].astype(F32).reshape(256, 256)

    for step, ref in ((0, a_src), (1, ai_src), (13, enc_y), (14, one_mid), (15, two_mid), (16, enc_z)):
        left_all(ref, step, NY - 1)
    for step, ref in ((2, b_src), (3, bi_src), (10, one_src), (11, two_src), (19, one_all), (20, two_all)):
        left_all(ref, step, NZ - 1)
    for step, ref in ((12, enc_src), (21, enc_all)):
        left_all(ref, step, NY - 1)
    for step, ref in ((17, one_x), (18, two_x)):
        left_all(ref, step, NX - 1)
    for step, ref in ((4, qa_src), (5, qa_src)):
        left_all(ref, step, 1)
    for step, ref in ((6, ev_win), (7, ev_win), (8, z_two), (9, z_two)):
        left_all(ref, step, 128)


def body(events, perm, w_enc, w_one, w_two, slot_blocks, live_count, block_counts, out_grad):
    scale_loss = 1.0 / math.sqrt(lax.axis_size("rep") * lax.axis_size("dom") * events.shape[1])
    vmem = pl.BlockSpec(memory_space=pltpu.VMEM)
    smem = pl.BlockSpec(memory_space=pltpu.SMEM)
    hbm = pl.BlockSpec(memory_space=pltpu.HBM)
    slot_rows = jnp.swapaxes(slot_blocks, 1, 2)
    args = [
        pltpu.with_memory_space_constraint(x, pltpu.HBM)
        for x in (events, perm, w_enc, w_one, w_two, slot_rows, block_counts, out_grad)
    ]

    def pieces(*shape, dtype=BF16):
        return pltpu.VMEM(shape, dtype)

    return pl.pallas_call(
        functools.partial(step_kernel, scale_loss),
        out_shape=(
            jax.ShapeDtypeStruct((1, 256, 256), BF16),
            jax.ShapeDtypeStruct((128, 256), F32),
            jax.ShapeDtypeStruct((256, 256), F32),
            jax.ShapeDtypeStruct((256, 256), F32),
        ),
        in_specs=[hbm, hbm, hbm, hbm, hbm, hbm, smem, hbm, hbm],
        out_specs=(vmem, vmem, vmem, vmem),
        scratch_shapes=[
            pieces(1, 256, 128),
            pieces(1, 256, dtype=jnp.int32),
            pieces(128, 256),
            pieces(256, 256),
            pieces(256, 256),
            pieces(1, 10, 128, 128, dtype=jnp.int32),
            pieces(1, 256, 256),
            pltpu.SMEM((1, 2, 10), jnp.int32),
            pieces(256, 512, dtype=F32),
            pieces(256, 512),
            pieces(512, 256),
            pieces(256, 256, dtype=F32),
            pieces(256, 256),
            pieces(128, 256),
            pieces(128, 256),
            pieces(256, 256),
            pieces(256, 256),
            pieces(256, 256),
            pieces(512, 128),
            pieces(512, 256),
            pieces(256, 256, dtype=F32),
            pieces(256, 256, dtype=F32),
            pieces(NY, 32, 128),
            pieces(NY, 32, 128),
            pieces(NY, 1, 128, dtype=F32),
            pieces(NY, 1, 128, dtype=F32),
            pieces(NZ, 16, 128),
            pieces(NZ, 16, 128),
            pieces(NZ, 1, 128, dtype=F32),
            pieces(NZ, 1, 128, dtype=F32),
            pieces(2, 128, 256),
            pieces(2, 128, 256),
            pieces(NZ, 16, 256),
            pieces(NZ, 16, 256),
            pieces(NY, 16, 256),
            pieces(NX, 16, 256),
            pieces(NZ, 16, 256),
            pieces(NZ, 16, 256),
            pieces(NZ, 16, 256),
            pieces(NY, 16, 256),
            pieces(NX, 16, 256),
            pieces(NZ, 16, 256),
            pieces(NY, 16, 256),
            pieces(NY, 16, 256),
            pieces(NY, 16, 256),
            pieces(NY, 16, 256),
            pieces(NY, 16, 256),
            pieces(256, 512),
            pieces(128, 512),
            pieces(512, 256, dtype=F32),
            pltpu.SemaphoreType.DMA((8,)),
            pltpu.SemaphoreType.DMA((22,)),
            pltpu.SemaphoreType.DMA((22,)),
        ],
        compiler_params=pltpu.CompilerParams(
            collective_id=0, has_side_effects=True, vmem_limit_bytes=16 * 1024 * 1024
        ),
    )(*args[:6], live_count, *args[6:])


def solution(mesh):
    return jax.shard_map(
        body,
        mesh=mesh,
        in_specs=(
            P("rep", "dom", None),
            P("rep", "dom"),
            P(),
            P(),
            P(),
            P("rep", "dom", None),
            P("rep", "dom"),
            P("rep", "dom", None, None),
            P("rep", "dom", None),
        ),
        out_specs=(P("rep", "dom", None), P(), P(), P()),
        check_vma=False,
    )
```

```python
import functools
import math

import jax
import jax.numpy as jnp
from jax import lax
from jax.experimental import pallas as pl
from jax.experimental.pallas import tpu as pltpu
from jax.sharding import PartitionSpec as P

loop_weight = 4.0
NY = 8
NZ = 16
NX = 4
F32 = jnp.float32
BF16 = jnp.bfloat16


def dot(a, b):
    return jnp.dot(a, b, preferred_element_type=F32)


def dot_nt(a, b):
    return lax.dot_general(a, b, (((1,), (1,)), ((), ())), preferred_element_type=F32)


def sigmoid(value):
    return 1.0 / (1.0 + jnp.exp(-value))


def wait_for(ref, sem):
    pltpu.make_async_copy(ref, ref, sem).wait()


def iota(shape, dim):
    return lax.broadcasted_iota(jnp.int32, shape, dim)


def one_where(mask):
    return jnp.where(mask, 1.0, 0.0).astype(BF16)


def step_kernel(
    scale_loss,
    events_in, perm_in, w_enc_in, w_one_in, w_two_in, slots_in, live, counts_in, out_grad_in,
    embed, enc_all, one_all, two_all,
    events, perm, w_enc, w_one, w_two, counts, out_grad, slots,
    adj_f, adj, adj_t, inv_deg, mid, regroup, spread, finish, w_one_t, w_two_t,
    ev_win, z_two, gz_ref, gh_ref,
    a_src, a_dst, ai_src, ai_dst, b_src, b_dst, bi_src, bi_dst, qa_src, qa_dst,
    two_src, two_dst, two_mid, two_x, one_src, one_dst, one_mid, one_x,
    enc_src, enc_dst, enc_y, enc_z, h_win_t, ev_win_t, slope,
    load_sem, send_sem, recv_sem,
):
    me = lax.axis_index("dom")
    rep = lax.axis_index("rep")
    ndom = NY * NZ
    my_y = me // NZ
    my_z = me % NZ
    core = me % 2
    my_yc = my_y * 2 + core
    my_xc = rep * 2 + core
    my_zc = my_z // 2
    left = {"dom": (me + ndom - 1) % ndom}
    right = {"dom": (me + 1) % ndom}

    loads = [
        pltpu.make_async_copy(src, dst, load_sem.at[i])
        for i, (src, dst) in enumerate(
            (
                (perm_in, perm), (events_in, events), (slots_in, slots), (counts_in, counts),
                (out_grad_in, out_grad), (w_two_in, w_two), (w_enc_in, w_enc), (w_one_in, w_one),
            )
        )
    ]
    for load in loads:
        load.start()

    def others(group):
        ring = NX if group[0] == "x" else NY
        here = {"x": rep, "y": my_y, "z": my_zc}[group[0]]
        found = []
        for ahead in sorted(range(ring), key=lambda n: -min(n, ring - n)):
            chip = (here + ahead) % ring
            for flip in range(len(group)):
                if ahead or flip:
                    side = (core + flip) % 2
                    y = chip if group[0] == "y" else my_y
                    z = chip if group[0] == "z" else my_zc
                    x = chip if group[0] == "x" else rep
                    rank = chip * 2 + side if len(group) == 2 else chip
                    found.append((rank, {"dom": y * NZ + z * 2 + side, "rep": x}))
        return found

    barrier = pltpu.get_barrier_semaphore()
    friends = [dev for group in ("yc", "zc", "xc") for _, dev in others(group)] + [left, right]
    for device in friends:
        pl.semaphore_signal(barrier, inc=1, device_id=device, device_id_type=pl.DeviceIdType.MESH)

    def send(src, dst, step, device):
        pltpu.make_async_remote_copy(
            src_ref=src, dst_ref=dst, send_sem=send_sem.at[step], recv_sem=recv_sem.at[step],
            device_id=device, device_id_type=pl.DeviceIdType.MESH,
        ).start()

    def scatter(src, dst, mine, step, group):
        for k, device in others(group):
            send(src.at[k], dst.at[mine], step, device)
        dst[mine] = src[mine]

    def spread_out(ref, mine, step, group):
        for _, device in others(group):
            send(ref.at[mine], ref.at[mine], step, device)

    def arrived(ref, step, count):
        wait_for(ref.at[pl.ds(0, count)], recv_sem.at[step])

    def left_all(ref, step, count):
        wait_for(ref.at[pl.ds(0, count)], send_sem.at[step])

    rows = iota((256, 256), 0)
    cols = iota((256, 256), 1)
    half_rows = rows[0:128]
    half_cols = cols[0:128]
    loads[0].wait()
    ids = perm[...]
    ids_row = ids.astype(F32)
    ids_col = jnp.sum(jnp.where(rows == cols, ids_row, 0.0), axis=1, keepdims=True)
    place = jnp.sum(jnp.where(ids_col < ids_row, 1.0, 0.0), axis=0, keepdims=True).astype(jnp.int32)
    local_row = (ids & 255).astype(F32)
    id_left = jnp.where((place >> 5) == rows[0:16], local_row, 0.0).astype(BF16)
    id_right = one_where((place & 31) == half_rows)
    ai_src[...] = dot_nt(id_left, id_right)[0:NY].reshape(NY, 1, 128)
    loads[1].wait()
    a_src[...] = dot(one_where(rows == place), events[0]).astype(BF16).reshape(NY, 32, 128)

    pl.semaphore_wait(barrier, len(friends))
    scatter(ai_src, ai_dst, my_y, 1, "y")
    scatter(a_src, a_dst, my_y, 0, "y")

    loads[2].wait()
    loads[3].wait()
    weights = []
    for s in range(10):
        row = slots[0, 0, s] - 2 * me
        col = (slots[0, 1, s] - 2 * me + 1 + 2 * ndom) % (2 * ndom)
        used = s < live[0, 0]
        weights.append(
            [
                [jnp.where(used & (row == r) & (col == c), 1.0, 0.0) for c in (1, 2, 0, 3)]
                for r in range(2)
            ]
        )
    for part in range(4):
        here = slice(part * 32, part * 32 + 32)
        sums = [[None] * 4 for _ in range(2)]
        for s in range(10):
            cell = counts[0, s, here, :].astype(F32)
            for r in range(2):
                for c in range(4):
                    term = cell * weights[s][r][c]
                    sums[r][c] = term if s == 0 else sums[r][c] + term
        diag = iota((32, 128), 0) + part * 32 == iota((32, 128), 1)
        for r in range(2):
            sums[r][r] = sums[r][r] + jnp.where(diag, loop_weight, 0.0)
            for c in range(4):
                adj_f[r * 128 + part * 32 : r * 128 + part * 32 + 32, c * 128 : c * 128 + 128] = sums[r][c]
    adj[...] = adj_f[...].astype(BF16)
    for r in range(2):
        for c in range(4):
            adj_t[c * 128 : c * 128 + 128, r * 128 : r * 128 + 128] = (
                adj_f[r * 128 : r * 128 + 128, c * 128 : c * 128 + 128].T.astype(BF16)
            )
    inverse = 1.0 / dot(adj[...], jnp.ones((512, 128), BF16))
    inv_deg[:, 0:128] = inverse
    inv_deg[:, 128:256] = inverse

    loads[4].wait()
    gs_two = (out_grad[0].astype(F32) * scale_loss * inv_deg[...]).astype(BF16)
    qa_src[...] = dot(adj_t[256:512], gs_two).astype(BF16).reshape(2, 128, 256)
    send(qa_src.at[0], qa_dst.at[1], 4, left)
    send(qa_src.at[1], qa_dst.at[0], 5, right)
    gz_ref[...] = dot(adj_t[0:256], gs_two)

    source = ((rows >> 1) & (NY - 1)) * 32 + (rows >> 4) * 2 + (rows & 1)
    mid[...] = one_where(cols == source)
    regroup[...] = one_where(half_rows == (half_cols >> 4) * 2 + (half_cols & 1))
    spread[...] = one_where(half_rows == (half_cols & 15))
    loads[5].wait()
    loads[6].wait()
    loads[7].wait()
    w_two_t[...] = w_two[...].T
    w_one_t[...] = w_one[...].T

    arrived(ai_dst, 1, NY - 1)
    ids_mid = dot(ai_dst[...].reshape(NY, 128).astype(BF16), regroup[...])
    ids_mid = jnp.sum(
        jnp.where(rows[0:NY] == ((cols[0:NY] >> 1) & (NY - 1)), ids_mid, 0.0), axis=0, keepdims=True
    )
    id_left = jnp.where((cols[0:NZ] >> 4) == rows[0:NZ], ids_mid, 0.0).astype(BF16)
    bi_src[...] = dot_nt(id_left, spread[...]).reshape(NZ, 1, 128)
    scatter(bi_src, bi_dst, my_z, 3, "zc")
    arrived(a_dst, 0, NY - 1)
    b_src[...] = dot(mid[...], a_dst[...].reshape(256, 128)).astype(BF16).reshape(NZ, 16, 128)
    scatter(b_src, b_dst, my_z, 2, "zc")

    wait_for(qa_dst.at[1], recv_sem.at[4])
    wait_for(qa_dst.at[0], recv_sem.at[5])
    gz_two = (gz_ref[...] + qa_dst[...].astype(F32).reshape(256, 256)).astype(BF16)
    gh_ref[...] = dot(gz_two, w_two_t[...]) * inv_deg[...]

    arrived(bi_dst, 3, NZ - 1)
    ids_got = dot(bi_dst[...].reshape(NZ, 128).astype(BF16), spread[...])
    ids_got = jnp.sum(
        jnp.where(rows[0:NZ] == (cols[0:NZ] >> 4), ids_got, 0.0), axis=0, keepdims=True
    )
    finish[...] = one_where(rows.astype(F32) == ids_got)
    arrived(b_dst, 2, NZ - 1)
    ev_own = dot(finish[...], b_dst[...].reshape(256, 128)).astype(BF16)
    ev_win[0:256] = ev_own
    send(ev_win.at[pl.ds(0, 128)], ev_win.at[pl.ds(384, 128)], 6, left)
    send(ev_win.at[pl.ds(128, 128)], ev_win.at[pl.ds(256, 128)], 7, right)

    def encoded(rows_in):
        pre_rows = dot(rows_in, w_enc[...])
        return pre_rows, (pre_rows * sigmoid(pre_rows)).astype(BF16)

    pre, h_zero = encoded(ev_own)
    z_own = dot(h_zero, w_one[...]).astype(BF16)
    total = dot(adj[:, 0:256], z_own)
    sig = sigmoid(pre)
    slope[0:256] = sig * (1.0 + pre * (1.0 - sig))
    h_win_t[:, 0:256] = h_zero.T
    ev_win_t[:, 0:256] = ev_own.T
    wait_for(ev_win.at[pl.ds(384, 128)], recv_sem.at[6])
    wait_for(ev_win.at[pl.ds(256, 128)], recv_sem.at[7])
    ev_side = ev_win[256:512]
    pre, h_zero = encoded(ev_side)
    z_side = dot(h_zero, w_one[...]).astype(BF16)
    agg_one = (total + dot(adj[:, 256:512], z_side)) * inv_deg[...]
    h_win_t[:, 256:512] = h_zero.T
    ev_win_t[:, 256:512] = ev_side.T
    sig = sigmoid(pre)
    slope[256:512] = sig * (1.0 + pre * (1.0 - sig))

    sig = sigmoid(agg_one)
    gs_one = (gh_ref[...] * (sig * (1.0 + agg_one * (1.0 - sig)))).astype(BF16)
    gz_one = dot(adj_t[...], gs_one).astype(BF16)
    one_src[...] = dot(h_win_t[...], gz_one).astype(BF16).reshape(NZ, 16, 256)
    scatter(one_src, one_dst, my_z, 10, "zc")
    h_one = (agg_one * sig).astype(BF16)
    two_src[...] = dot(h_one.T, gz_two).astype(BF16).reshape(NZ, 16, 256)
    scatter(two_src, two_dst, my_yc, 11, "yc")
    gh_zero = dot(gz_one, w_one_t[...]).astype(BF16)
    g_enc = (gh_zero.astype(F32) * slope[...]).astype(BF16)
    enc_src[...] = dot(ev_win_t[...], g_enc).astype(BF16).reshape(NY, 16, 256)
    scatter(enc_src, enc_dst, my_xc, 12, "xc")
    z_two[0:256] = dot(h_one, w_two[...]).astype(BF16)
    send(z_two.at[pl.ds(0, 128)], z_two.at[pl.ds(384, 128)], 8, left)
    send(z_two.at[pl.ds(128, 128)], z_two.at[pl.ds(256, 128)], 9, right)

    def summed(ref):
        return jnp.sum(ref[...].astype(F32), axis=0).astype(BF16)

    arrived(enc_dst, 12, NY - 1)
    enc_y[my_y] = summed(enc_dst)
    spread_out(enc_y, my_y, 13, "y")
    arrived(one_dst, 10, NZ - 1)
    one_mid[my_y] = summed(one_dst)
    spread_out(one_mid, my_y, 14, "y")
    arrived(two_dst, 11, NZ - 1)
    two_mid[my_zc] = summed(two_dst)
    spread_out(two_mid, my_zc, 15, "z")
    wait_for(z_two.at[pl.ds(384, 128)], recv_sem.at[8])
    wait_for(z_two.at[pl.ds(256, 128)], recv_sem.at[9])
    embed[0] = (dot(adj[...], z_two[...]) * inv_deg[...]).astype(BF16)
    arrived(enc_y, 13, NY - 1)
    enc_z[my_zc] = summed(enc_y)
    spread_out(enc_z, my_zc, 16, "z")
    arrived(one_mid, 14, NY - 1)
    one_x[rep] = summed(one_mid)
    spread_out(one_x, rep, 17, "x")
    arrived(two_mid, 15, NY - 1)
    two_x[rep] = summed(two_mid)
    spread_out(two_x, rep, 18, "x")
    arrived(one_x, 17, NX - 1)
    one_all[my_z] = summed(one_x)
    spread_out(one_all, my_z, 19, "zc")
    arrived(two_x, 18, NX - 1)
    two_all[my_yc] = summed(two_x)
    spread_out(two_all, my_yc, 20, "yc")
    arrived(enc_z, 16, NY - 1)
    enc_all[my_xc] = summed(enc_z)
    spread_out(enc_all, my_xc, 21, "xc")
    arrived(enc_all, 21, NY - 1)
    arrived(one_all, 19, NZ - 1)
    arrived(two_all, 20, NZ - 1)

    for step, ref in ((0, a_src), (1, ai_src), (13, enc_y), (14, one_mid), (15, two_mid), (16, enc_z)):
        left_all(ref, step, NY - 1)
    for step, ref in ((2, b_src), (3, bi_src), (10, one_src), (11, two_src), (19, one_all), (20, two_all)):
        left_all(ref, step, NZ - 1)
    for step, ref in ((12, enc_src), (21, enc_all)):
        left_all(ref, step, NY - 1)
    for step, ref in ((17, one_x), (18, two_x)):
        left_all(ref, step, NX - 1)
    for step, ref in ((4, qa_src), (5, qa_src)):
        left_all(ref, step, 1)
    for step, ref in ((6, ev_win), (7, ev_win), (8, z_two), (9, z_two)):
        left_all(ref, step, 128)


def result_kernel(
    embed, enc_all, one_all, two_all, embed_out, grad_enc, grad_one, grad_two, enc, one, two, sem
):
    stores = [pltpu.make_async_copy(embed, embed_out, sem.at[0])]
    stores[0].start()
    for i, (src, wide, out) in enumerate(
        ((enc_all, enc, grad_enc), (one_all, one, grad_one), (two_all, two, grad_two))
    ):
        wide[...] = src[...].astype(F32).reshape(wide.shape)
        stores.append(pltpu.make_async_copy(wide, out, sem.at[i + 1]))
        stores[-1].start()
    for store in stores:
        store.wait()


def body(events, perm, w_enc, w_one, w_two, slot_blocks, live_count, block_counts, out_grad):
    scale_loss = 1.0 / math.sqrt(lax.axis_size("rep") * lax.axis_size("dom") * events.shape[1])
    vmem = pl.BlockSpec(memory_space=pltpu.VMEM)
    smem = pl.BlockSpec(memory_space=pltpu.SMEM)
    hbm = pl.BlockSpec(memory_space=pltpu.HBM)
    slot_rows = jnp.swapaxes(slot_blocks, 1, 2)
    args = [
        pltpu.with_memory_space_constraint(x, pltpu.HBM)
        for x in (events, perm, w_enc, w_one, w_two, slot_rows, block_counts, out_grad)
    ]

    def pieces(*shape, dtype=BF16):
        return pltpu.VMEM(shape, dtype)

    found = pl.pallas_call(
        functools.partial(step_kernel, scale_loss),
        out_shape=(
            jax.ShapeDtypeStruct((1, 256, 256), BF16),
            jax.ShapeDtypeStruct((NY, 16, 256), BF16),
            jax.ShapeDtypeStruct((NZ, 16, 256), BF16),
            jax.ShapeDtypeStruct((NZ, 16, 256), BF16),
        ),
        in_specs=[hbm] * 6 + [smem] + [hbm] * 2,
        out_specs=(vmem, vmem, vmem, vmem),
        scratch_shapes=[
            pieces(1, 256, 128),
            pieces(1, 256, dtype=jnp.int32),
            pieces(128, 256),
            pieces(256, 256),
            pieces(256, 256),
            pieces(1, 10, 128, 128, dtype=jnp.int32),
            pieces(1, 256, 256),
            pltpu.SMEM((1, 2, 10), jnp.int32),
            pieces(256, 512, dtype=F32),
            pieces(256, 512),
            pieces(512, 256),
            pieces(256, 256, dtype=F32),
            pieces(256, 256),
            pieces(128, 256),
            pieces(128, 256),
            pieces(256, 256),
            pieces(256, 256),
            pieces(256, 256),
            pieces(512, 128),
            pieces(512, 256),
            pieces(256, 256, dtype=F32),
            pieces(256, 256, dtype=F32),
            pieces(NY, 32, 128),
            pieces(NY, 32, 128),
            pieces(NY, 1, 128, dtype=F32),
            pieces(NY, 1, 128, dtype=F32),
            pieces(NZ, 16, 128),
            pieces(NZ, 16, 128),
            pieces(NZ, 1, 128, dtype=F32),
            pieces(NZ, 1, 128, dtype=F32),
            pieces(2, 128, 256),
            pieces(2, 128, 256),
            pieces(NZ, 16, 256),
            pieces(NZ, 16, 256),
            pieces(NY, 16, 256),
            pieces(NX, 16, 256),
            pieces(NZ, 16, 256),
            pieces(NZ, 16, 256),
            pieces(NY, 16, 256),
            pieces(NX, 16, 256),
            pieces(NY, 16, 256),
            pieces(NY, 16, 256),
            pieces(NY, 16, 256),
            pieces(NY, 16, 256),
            pieces(256, 512),
            pieces(128, 512),
            pieces(512, 256, dtype=F32),
            pltpu.SemaphoreType.DMA((8,)),
            pltpu.SemaphoreType.DMA((22,)),
            pltpu.SemaphoreType.DMA((22,)),
        ],
        compiler_params=pltpu.CompilerParams(
            collective_id=0, has_side_effects=True, vmem_limit_bytes=16 * 1024 * 1024
        ),
    )(*args[:6], live_count, *args[6:])
    return pl.pallas_call(
        result_kernel,
        out_shape=(
            jax.ShapeDtypeStruct((1, 256, 256), BF16),
            jax.ShapeDtypeStruct((128, 256), F32),
            jax.ShapeDtypeStruct((256, 256), F32),
            jax.ShapeDtypeStruct((256, 256), F32),
        ),
        in_specs=[vmem] * 4,
        out_specs=(pl.BlockSpec(memory_space=pl.ANY),) * 4,
        scratch_shapes=[
            pieces(128, 256, dtype=F32),
            pieces(256, 256, dtype=F32),
            pieces(256, 256, dtype=F32),
            pltpu.SemaphoreType.DMA((4,)),
        ],
        compiler_params=pltpu.CompilerParams(vmem_limit_bytes=8 * 1024 * 1024),
    )(*found)


def solution(mesh):
    return jax.shard_map(
        body,
        mesh=mesh,
        in_specs=(
            P("rep", "dom", None),
            P("rep", "dom"),
            P(),
            P(),
            P(),
            P("rep", "dom", None),
            P("rep", "dom"),
            P("rep", "dom", None, None),
            P("rep", "dom", None),
        ),
        out_specs=(P("rep", "dom", None), P(), P(), P()),
        check_vma=False,
    )
```

```python
import functools
import math

import jax
import jax.numpy as jnp
from jax import lax
from jax.experimental import pallas as pl
from jax.experimental.pallas import tpu as pltpu
from jax.sharding import PartitionSpec as P

loop_weight = 4.0
NY = 8
NZ = 16
NX = 4
F32 = jnp.float32
BF16 = jnp.bfloat16


def dot(a, b):
    return jnp.dot(a, b, preferred_element_type=F32)


def dot_nt(a, b):
    return lax.dot_general(a, b, (((1,), (1,)), ((), ())), preferred_element_type=F32)


def sigmoid(value):
    return 1.0 / (1.0 + jnp.exp(-value))


def wait_for(ref, sem):
    pltpu.make_async_copy(ref, ref, sem).wait()


def iota(shape, dim):
    return lax.broadcasted_iota(jnp.int32, shape, dim)


def one_where(mask):
    return jnp.where(mask, 1.0, 0.0).astype(BF16)


def step_kernel(
    scale_loss,
    events_in, perm_in, w_enc_in, w_one_in, w_two_in, slots_in, live, counts_in, out_grad_in,
    embed, enc_all, one_all, two_all,
    events, perm, w_enc, w_one, w_two, counts, out_grad, slots,
    adj_f, adj, adj_t, inv_deg, mid, regroup, spread, finish, w_one_t, w_two_t,
    ev_win, z_two, gz_ref, gh_ref,
    a_src, a_dst, ai_src, ai_dst, b_src, b_dst, bi_src, bi_dst, qa_src, qa_dst,
    two_src, two_dst, two_mid, two_x, one_src, one_dst, one_mid, one_x,
    enc_src, enc_dst, enc_y, enc_z, h_win_t, ev_win_t, slope,
    load_sem, send_sem, recv_sem,
):
    me = lax.axis_index("dom")
    rep = lax.axis_index("rep")
    ndom = NY * NZ
    my_y = me // NZ
    my_z = me % NZ
    core = me % 2
    my_yc = my_y * 2 + core
    my_xc = rep * 2 + core
    my_zc = my_z // 2
    left = {"dom": (me + ndom - 1) % ndom}
    right = {"dom": (me + 1) % ndom}

    loads = [
        pltpu.make_async_copy(src, dst, load_sem.at[i])
        for i, (src, dst) in enumerate(
            (
                (perm_in, perm), (events_in, events), (slots_in, slots), (counts_in, counts),
                (out_grad_in, out_grad), (w_two_in, w_two), (w_enc_in, w_enc), (w_one_in, w_one),
            )
        )
    ]
    for load in loads[:2]:
        load.start()

    def others(group):
        ring = NX if group[0] == "x" else NY
        here = {"x": rep, "y": my_y, "z": my_zc}[group[0]]
        found = []
        for ahead in sorted(range(ring), key=lambda n: -min(n, ring - n)):
            chip = (here + ahead) % ring
            for flip in range(len(group)):
                if ahead or flip:
                    side = (core + flip) % 2
                    y = chip if group[0] == "y" else my_y
                    z = chip if group[0] == "z" else my_zc
                    x = chip if group[0] == "x" else rep
                    rank = chip * 2 + side if len(group) == 2 else chip
                    found.append((min(ahead, ring - ahead), rank, {"dom": y * NZ + z * 2 + side, "rep": x}))
        return found

    barrier = pltpu.get_barrier_semaphore()

    def hello(device):
        pl.semaphore_signal(barrier, inc=1, device_id=device, device_id_type=pl.DeviceIdType.MESH)

    friends = others("y") + others("zc") + [f for f in others("xc") if f[0]]
    friends.sort(key=lambda f: -f[0])
    for _, _, device in friends:
        hello(device)
    at_start = my_z == 0
    at_end = my_z == NZ - 1
    pl.when(at_start)(lambda: hello(left))
    pl.when(at_end)(lambda: hello(right))
    for load in loads[2:]:
        load.start()

    def send(src, dst, step, device):
        pltpu.make_async_remote_copy(
            src_ref=src, dst_ref=dst, send_sem=send_sem.at[step], recv_sem=recv_sem.at[step],
            device_id=device, device_id_type=pl.DeviceIdType.MESH,
        ).start()

    def scatter(src, dst, mine, step, group):
        for _, k, device in others(group):
            send(src.at[k], dst.at[mine], step, device)
        dst[mine] = src[mine]

    def spread_out(ref, mine, step, group):
        for _, _, device in others(group):
            send(ref.at[mine], ref.at[mine], step, device)

    def arrived(ref, step, count):
        wait_for(ref.at[pl.ds(0, count)], recv_sem.at[step])

    def left_all(ref, step, count):
        wait_for(ref.at[pl.ds(0, count)], send_sem.at[step])

    rows = iota((256, 256), 0)
    cols = iota((256, 256), 1)
    half_rows = rows[0:128]
    half_cols = cols[0:128]
    loads[0].wait()
    ids = perm[...]
    ids_row = ids.astype(F32)
    ids_col = jnp.sum(jnp.where(rows == cols, ids_row, 0.0), axis=1, keepdims=True)
    place = jnp.sum(jnp.where(ids_col < ids_row, 1.0, 0.0), axis=0, keepdims=True).astype(jnp.int32)
    local_row = (ids & 255).astype(F32)
    id_left = jnp.where((place >> 5) == rows[0:16], local_row, 0.0).astype(BF16)
    id_right = one_where((place & 31) == half_rows)
    ai_src[...] = dot_nt(id_left, id_right)[0:NY].reshape(NY, 1, 128)
    loads[1].wait()
    a_src[...] = dot(one_where(rows == place), events[0]).astype(BF16).reshape(NY, 32, 128)

    edge = jnp.where(at_start | at_end, 1, 0)
    pl.semaphore_wait(barrier, len(friends) + edge)
    scatter(ai_src, ai_dst, my_y, 1, "y")
    scatter(a_src, a_dst, my_y, 0, "y")

    loads[2].wait()
    loads[3].wait()
    weights = []
    for s in range(10):
        row = slots[0, 0, s] - 2 * me
        col = (slots[0, 1, s] - 2 * me + 1 + 2 * ndom) % (2 * ndom)
        used = s < live[0, 0]
        weights.append(
            [
                [jnp.where(used & (row == r) & (col == c), 1.0, 0.0) for c in (1, 2, 0, 3)]
                for r in range(2)
            ]
        )
    for part in range(4):
        here = slice(part * 32, part * 32 + 32)
        sums = [[None] * 4 for _ in range(2)]
        for s in range(10):
            cell = counts[0, s, here, :].astype(F32)
            for r in range(2):
                for c in range(4):
                    term = cell * weights[s][r][c]
                    sums[r][c] = term if s == 0 else sums[r][c] + term
        diag = iota((32, 128), 0) + part * 32 == iota((32, 128), 1)
        for r in range(2):
            sums[r][r] = sums[r][r] + jnp.where(diag, loop_weight, 0.0)
            for c in range(4):
                adj_f[r * 128 + part * 32 : r * 128 + part * 32 + 32, c * 128 : c * 128 + 128] = sums[r][c]
    adj[...] = adj_f[...].astype(BF16)
    for r in range(2):
        for c in range(4):
            adj_t[c * 128 : c * 128 + 128, r * 128 : r * 128 + 128] = (
                adj_f[r * 128 : r * 128 + 128, c * 128 : c * 128 + 128].T.astype(BF16)
            )
    inverse = 1.0 / dot(adj[...], jnp.ones((512, 128), BF16))
    inv_deg[:, 0:128] = inverse
    inv_deg[:, 128:256] = inverse

    loads[4].wait()
    gs_two = (out_grad[0].astype(F32) * scale_loss * inv_deg[...]).astype(BF16)
    qa_src[...] = dot(adj_t[256:512], gs_two).astype(BF16).reshape(2, 128, 256)
    send(qa_src.at[0], qa_dst.at[1], 4, left)
    send(qa_src.at[1], qa_dst.at[0], 5, right)
    gz_ref[...] = dot(adj_t[0:256], gs_two)

    source = ((rows >> 1) & (NY - 1)) * 32 + (rows >> 4) * 2 + (rows & 1)
    mid[...] = one_where(cols == source)
    regroup[...] = one_where(half_rows == (half_cols >> 4) * 2 + (half_cols & 1))
    spread[...] = one_where(half_rows == (half_cols & 15))
    loads[5].wait()
    loads[6].wait()
    loads[7].wait()
    w_two_t[...] = w_two[...].T
    w_one_t[...] = w_one[...].T

    arrived(ai_dst, 1, NY - 1)
    ids_mid = dot(ai_dst[...].reshape(NY, 128).astype(BF16), regroup[...])
    ids_mid = jnp.sum(
        jnp.where(rows[0:NY] == ((cols[0:NY] >> 1) & (NY - 1)), ids_mid, 0.0), axis=0, keepdims=True
    )
    id_left = jnp.where((cols[0:NZ] >> 4) == rows[0:NZ], ids_mid, 0.0).astype(BF16)
    bi_src[...] = dot_nt(id_left, spread[...]).reshape(NZ, 1, 128)
    scatter(bi_src, bi_dst, my_z, 3, "zc")
    arrived(a_dst, 0, NY - 1)
    b_src[...] = dot(mid[...], a_dst[...].reshape(256, 128)).astype(BF16).reshape(NZ, 16, 128)
    scatter(b_src, b_dst, my_z, 2, "zc")

    wait_for(qa_dst.at[1], recv_sem.at[4])
    wait_for(qa_dst.at[0], recv_sem.at[5])
    gz_two = (gz_ref[...] + qa_dst[...].astype(F32).reshape(256, 256)).astype(BF16)
    gh_ref[...] = dot(gz_two, w_two_t[...]) * inv_deg[...]

    arrived(bi_dst, 3, NZ - 1)
    ids_got = dot(bi_dst[...].reshape(NZ, 128).astype(BF16), spread[...])
    ids_got = jnp.sum(
        jnp.where(rows[0:NZ] == (cols[0:NZ] >> 4), ids_got, 0.0), axis=0, keepdims=True
    )
    finish[...] = one_where(rows.astype(F32) == ids_got)
    arrived(b_dst, 2, NZ - 1)
    ev_own = dot(finish[...], b_dst[...].reshape(256, 128)).astype(BF16)
    ev_win[0:256] = ev_own
    send(ev_win.at[pl.ds(0, 128)], ev_win.at[pl.ds(384, 128)], 6, left)
    send(ev_win.at[pl.ds(128, 128)], ev_win.at[pl.ds(256, 128)], 7, right)

    def encoded(rows_in):
        pre_rows = dot(rows_in, w_enc[...])
        return pre_rows, (pre_rows * sigmoid(pre_rows)).astype(BF16)

    pre, h_zero = encoded(ev_own)
    z_own = dot(h_zero, w_one[...]).astype(BF16)
    total = dot(adj[:, 0:256], z_own)
    sig = sigmoid(pre)
    slope[0:256] = sig * (1.0 + pre * (1.0 - sig))
    h_win_t[:, 0:256] = h_zero.T
    ev_win_t[:, 0:256] = ev_own.T
    wait_for(ev_win.at[pl.ds(384, 128)], recv_sem.at[6])
    wait_for(ev_win.at[pl.ds(256, 128)], recv_sem.at[7])
    ev_side = ev_win[256:512]
    pre, h_zero = encoded(ev_side)
    z_side = dot(h_zero, w_one[...]).astype(BF16)
    agg_one = (total + dot(adj[:, 256:512], z_side)) * inv_deg[...]
    h_win_t[:, 256:512] = h_zero.T
    ev_win_t[:, 256:512] = ev_side.T
    sig = sigmoid(pre)
    slope[256:512] = sig * (1.0 + pre * (1.0 - sig))

    sig = sigmoid(agg_one)
    gs_one = (gh_ref[...] * (sig * (1.0 + agg_one * (1.0 - sig)))).astype(BF16)
    gz_one = dot(adj_t[...], gs_one).astype(BF16)
    one_src[...] = dot(h_win_t[...], gz_one).astype(BF16).reshape(NZ, 16, 256)
    scatter(one_src, one_dst, my_z, 10, "zc")
    h_one = (agg_one * sig).astype(BF16)
    two_src[...] = dot(h_one.T, gz_two).astype(BF16).reshape(NZ, 16, 256)
    scatter(two_src, two_dst, my_yc, 11, "yc")
    gh_zero = dot(gz_one, w_one_t[...]).astype(BF16)
    g_enc = (gh_zero.astype(F32) * slope[...]).astype(BF16)
    enc_src[...] = dot(ev_win_t[...], g_enc).astype(BF16).reshape(NY, 16, 256)
    scatter(enc_src, enc_dst, my_xc, 12, "xc")
    z_two[0:256] = dot(h_one, w_two[...]).astype(BF16)
    send(z_two.at[pl.ds(0, 128)], z_two.at[pl.ds(384, 128)], 8, left)
    send(z_two.at[pl.ds(128, 128)], z_two.at[pl.ds(256, 128)], 9, right)

    def summed(ref):
        return jnp.sum(ref[...].astype(F32), axis=0).astype(BF16)

    arrived(enc_dst, 12, NY - 1)
    enc_y[my_y] = summed(enc_dst)
    spread_out(enc_y, my_y, 13, "y")
    arrived(one_dst, 10, NZ - 1)
    one_mid[my_y] = summed(one_dst)
    spread_out(one_mid, my_y, 14, "y")
    arrived(two_dst, 11, NZ - 1)
    two_mid[my_zc] = summed(two_dst)
    spread_out(two_mid, my_zc, 15, "z")
    wait_for(z_two.at[pl.ds(384, 128)], recv_sem.at[8])
    wait_for(z_two.at[pl.ds(256, 128)], recv_sem.at[9])
    embed[0] = (dot(adj[...], z_two[...]) * inv_deg[...]).astype(BF16)
    arrived(enc_y, 13, NY - 1)
    enc_z[my_zc] = summed(enc_y)
    spread_out(enc_z, my_zc, 16, "z")
    arrived(one_mid, 14, NY - 1)
    one_x[rep] = summed(one_mid)
    spread_out(one_x, rep, 17, "x")
    arrived(two_mid, 15, NY - 1)
    two_x[rep] = summed(two_mid)
    spread_out(two_x, rep, 18, "x")
    arrived(one_x, 17, NX - 1)
    one_all[my_z] = summed(one_x)
    spread_out(one_all, my_z, 19, "zc")
    arrived(two_x, 18, NX - 1)
    two_all[my_yc] = summed(two_x)
    spread_out(two_all, my_yc, 20, "yc")
    arrived(enc_z, 16, NY - 1)
    enc_all[my_xc] = summed(enc_z)
    spread_out(enc_all, my_xc, 21, "xc")
    arrived(enc_all, 21, NY - 1)
    arrived(one_all, 19, NZ - 1)
    arrived(two_all, 20, NZ - 1)

    for step, ref in ((0, a_src), (1, ai_src), (13, enc_y), (14, one_mid), (15, two_mid), (16, enc_z)):
        left_all(ref, step, NY - 1)
    for step, ref in ((2, b_src), (3, bi_src), (10, one_src), (11, two_src), (19, one_all), (20, two_all)):
        left_all(ref, step, NZ - 1)
    for step, ref in ((12, enc_src), (21, enc_all)):
        left_all(ref, step, NY - 1)
    for step, ref in ((17, one_x), (18, two_x)):
        left_all(ref, step, NX - 1)
    for step, ref in ((4, qa_src), (5, qa_src)):
        left_all(ref, step, 1)
    for step, ref in ((6, ev_win), (7, ev_win), (8, z_two), (9, z_two)):
        left_all(ref, step, 128)


def result_kernel(
    embed, enc_all, one_all, two_all, embed_out, grad_enc, grad_one, grad_two, enc, one, two, sem
):
    stores = [pltpu.make_async_copy(embed, embed_out, sem.at[0])]
    stores[0].start()
    for i, (src, wide, out) in enumerate(
        ((enc_all, enc, grad_enc), (one_all, one, grad_one), (two_all, two, grad_two))
    ):
        wide[...] = src[...].astype(F32).reshape(wide.shape)
        stores.append(pltpu.make_async_copy(wide, out, sem.at[i + 1]))
        stores[-1].start()
    for store in stores:
        store.wait()


def body(events, perm, w_enc, w_one, w_two, slot_blocks, live_count, block_counts, out_grad):
    scale_loss = 1.0 / math.sqrt(lax.axis_size("rep") * lax.axis_size("dom") * events.shape[1])
    vmem = pl.BlockSpec(memory_space=pltpu.VMEM)
    smem = pl.BlockSpec(memory_space=pltpu.SMEM)
    hbm = pl.BlockSpec(memory_space=pltpu.HBM)
    slot_rows = jnp.swapaxes(slot_blocks, 1, 2)
    args = [
        pltpu.with_memory_space_constraint(x, pltpu.HBM)
        for x in (events, perm, w_enc, w_one, w_two, slot_rows, block_counts, out_grad)
    ]

    def pieces(*shape, dtype=BF16):
        return pltpu.VMEM(shape, dtype)

    found = pl.pallas_call(
        functools.partial(step_kernel, scale_loss),
        out_shape=(
            jax.ShapeDtypeStruct((1, 256, 256), BF16),
            jax.ShapeDtypeStruct((NY, 16, 256), BF16),
            jax.ShapeDtypeStruct((NZ, 16, 256), BF16),
            jax.ShapeDtypeStruct((NZ, 16, 256), BF16),
        ),
        in_specs=[hbm] * 6 + [smem] + [hbm] * 2,
        out_specs=(vmem, vmem, vmem, vmem),
        scratch_shapes=[
            pieces(1, 256, 128),
            pieces(1, 256, dtype=jnp.int32),
            pieces(128, 256),
            pieces(256, 256),
            pieces(256, 256),
            pieces(1, 10, 128, 128, dtype=jnp.int32),
            pieces(1, 256, 256),
            pltpu.SMEM((1, 2, 10), jnp.int32),
            pieces(256, 512, dtype=F32),
            pieces(256, 512),
            pieces(512, 256),
            pieces(256, 256, dtype=F32),
            pieces(256, 256),
            pieces(128, 256),
            pieces(128, 256),
            pieces(256, 256),
            pieces(256, 256),
            pieces(256, 256),
            pieces(512, 128),
            pieces(512, 256),
            pieces(256, 256, dtype=F32),
            pieces(256, 256, dtype=F32),
            pieces(NY, 32, 128),
            pieces(NY, 32, 128),
            pieces(NY, 1, 128, dtype=F32),
            pieces(NY, 1, 128, dtype=F32),
            pieces(NZ, 16, 128),
            pieces(NZ, 16, 128),
            pieces(NZ, 1, 128, dtype=F32),
            pieces(NZ, 1, 128, dtype=F32),
            pieces(2, 128, 256),
            pieces(2, 128, 256),
            pieces(NZ, 16, 256),
            pieces(NZ, 16, 256),
            pieces(NY, 16, 256),
            pieces(NX, 16, 256),
            pieces(NZ, 16, 256),
            pieces(NZ, 16, 256),
            pieces(NY, 16, 256),
            pieces(NX, 16, 256),
            pieces(NY, 16, 256),
            pieces(NY, 16, 256),
            pieces(NY, 16, 256),
            pieces(NY, 16, 256),
            pieces(256, 512),
            pieces(128, 512),
            pieces(512, 256, dtype=F32),
            pltpu.SemaphoreType.DMA((8,)),
            pltpu.SemaphoreType.DMA((22,)),
            pltpu.SemaphoreType.DMA((22,)),
        ],
        compiler_params=pltpu.CompilerParams(
            collective_id=0, has_side_effects=True, vmem_limit_bytes=16 * 1024 * 1024
        ),
    )(*args[:6], live_count, *args[6:])
    return pl.pallas_call(
        result_kernel,
        out_shape=(
            jax.ShapeDtypeStruct((1, 256, 256), BF16),
            jax.ShapeDtypeStruct((128, 256), F32),
            jax.ShapeDtypeStruct((256, 256), F32),
            jax.ShapeDtypeStruct((256, 256), F32),
        ),
        in_specs=[vmem] * 4,
        out_specs=(pl.BlockSpec(memory_space=pl.ANY),) * 4,
        scratch_shapes=[
            pieces(128, 256, dtype=F32),
            pieces(256, 256, dtype=F32),
            pieces(256, 256, dtype=F32),
            pltpu.SemaphoreType.DMA((4,)),
        ],
        compiler_params=pltpu.CompilerParams(vmem_limit_bytes=8 * 1024 * 1024),
    )(*found)


def solution(mesh):
    return jax.shard_map(
        body,
        mesh=mesh,
        in_specs=(
            P("rep", "dom", None),
            P("rep", "dom"),
            P(),
            P(),
            P(),
            P("rep", "dom", None),
            P("rep", "dom"),
            P("rep", "dom", None, None),
            P("rep", "dom", None),
        ),
        out_specs=(P("rep", "dom", None), P(), P(), P()),
        check_vma=False,
    )
```

```python
import functools
import math

import jax
import jax.numpy as jnp
from jax import lax
from jax.experimental import pallas as pl
from jax.experimental.pallas import tpu as pltpu
from jax.sharding import PartitionSpec as P

loop_weight = 4.0
NY = 8
NZ = 16
NX = 4
F32 = jnp.float32
BF16 = jnp.bfloat16


def dot(a, b):
    return jnp.dot(a, b, preferred_element_type=F32)


def dot_nt(a, b):
    return lax.dot_general(a, b, (((1,), (1,)), ((), ())), preferred_element_type=F32)


def sigmoid(value):
    return 1.0 / (1.0 + jnp.exp(-value))


def wait_for(ref, sem):
    pltpu.make_async_copy(ref, ref, sem).wait()


def iota(shape, dim):
    return lax.broadcasted_iota(jnp.int32, shape, dim)


def one_where(mask):
    return jnp.where(mask, 1.0, 0.0).astype(BF16)


def step_kernel(
    scale_loss,
    events_in, perm_in, w_enc_in, w_one_in, w_two_in, slots_in, live, counts_in, out_grad_in,
    embed, enc_all, one_all, two_all,
    events, perm, w_enc, w_one, w_two, counts, out_grad, slots,
    adj_f, adj, adj_t, inv_deg, mid, regroup, spread, finish, w_one_t, w_two_t,
    ev_win, z_two, gz_ref, gh_ref,
    a_src, a_dst, ai_src, ai_dst, b_src, b_dst, bi_src, bi_dst, qa_src, qa_dst,
    two_src, two_dst, two_mid, two_x, one_src, one_dst, one_mid, one_x,
    enc_src, enc_dst, enc_y, enc_z, h_win_t, ev_win_t, slope,
    load_sem, send_sem, recv_sem,
):
    me = lax.axis_index("dom")
    rep = lax.axis_index("rep")
    ndom = NY * NZ
    my_y = me // NZ
    my_z = me % NZ
    core = me % 2
    my_yc = my_y * 2 + core
    my_xc = rep * 2 + core
    my_zc = my_z // 2
    left = {"dom": (me + ndom - 1) % ndom}
    right = {"dom": (me + 1) % ndom}

    loads = [
        pltpu.make_async_copy(src, dst, load_sem.at[i])
        for i, (src, dst) in enumerate(
            (
                (perm_in, perm), (events_in, events), (slots_in, slots), (counts_in, counts),
                (out_grad_in, out_grad), (w_two_in, w_two), (w_enc_in, w_enc), (w_one_in, w_one),
            )
        )
    ]
    for load in loads[:2]:
        load.start()

    def others(group):
        ring = NX if group[0] == "x" else NY
        here = {"x": rep, "y": my_y, "z": my_zc}[group[0]]
        found = []
        for ahead in sorted(range(ring), key=lambda n: -min(n, ring - n)):
            chip = (here + ahead) % ring
            for flip in range(len(group)):
                if ahead or flip:
                    side = (core + flip) % 2
                    y = chip if group[0] == "y" else my_y
                    z = chip if group[0] == "z" else my_zc
                    x = chip if group[0] == "x" else rep
                    rank = chip * 2 + side if len(group) == 2 else chip
                    found.append((min(ahead, ring - ahead), rank, {"dom": y * NZ + z * 2 + side, "rep": x}))
        return found

    barrier = pltpu.get_barrier_semaphore()

    def hello(device):
        pl.semaphore_signal(barrier, inc=1, device_id=device, device_id_type=pl.DeviceIdType.MESH)

    friends = others("y") + others("zc") + [f for f in others("xc") if f[0]]
    friends.sort(key=lambda f: -f[0])
    for _, _, device in friends:
        hello(device)
    at_start = my_z == 0
    at_end = my_z == NZ - 1
    pl.when(at_start)(lambda: hello(left))
    pl.when(at_end)(lambda: hello(right))
    for load in loads[2:]:
        load.start()

    def send(src, dst, step, device):
        pltpu.make_async_remote_copy(
            src_ref=src, dst_ref=dst, send_sem=send_sem.at[step], recv_sem=recv_sem.at[step],
            device_id=device, device_id_type=pl.DeviceIdType.MESH,
        ).start()

    def scatter(*flows):
        starts = []
        for src, dst, mine, step, group in flows:
            starts += [(away, src.at[k], dst.at[mine], step, dev) for away, k, dev in others(group)]
        for _, src, dst, step, device in sorted(starts, key=lambda start: -start[0]):
            send(src, dst, step, device)
        for src, dst, mine, _, _ in flows:
            dst[mine] = src[mine]

    def spread_out(ref, mine, step, group):
        for _, _, device in others(group):
            send(ref.at[mine], ref.at[mine], step, device)

    def arrived(ref, step, count):
        wait_for(ref.at[pl.ds(0, count)], recv_sem.at[step])

    def left_all(ref, step, count):
        wait_for(ref.at[pl.ds(0, count)], send_sem.at[step])

    rows = iota((256, 256), 0)
    cols = iota((256, 256), 1)
    half_rows = rows[0:128]
    half_cols = cols[0:128]
    loads[0].wait()
    ids = perm[...]
    ids_row = ids.astype(F32)
    ids_col = jnp.sum(jnp.where(rows == cols, ids_row, 0.0), axis=1, keepdims=True)
    place = jnp.sum(jnp.where(ids_col < ids_row, 1.0, 0.0), axis=0, keepdims=True).astype(jnp.int32)
    local_row = (ids & 255).astype(F32)
    id_left = jnp.where((place >> 5) == rows[0:16], local_row, 0.0).astype(BF16)
    id_right = one_where((place & 31) == half_rows)
    ai_src[...] = dot_nt(id_left, id_right)[0:NY].reshape(NY, 1, 128)
    loads[1].wait()
    a_src[...] = dot(one_where(rows == place), events[0]).astype(BF16).reshape(NY, 32, 128)

    edge = jnp.where(at_start | at_end, 1, 0)
    pl.semaphore_wait(barrier, len(friends) + edge)
    scatter((ai_src, ai_dst, my_y, 1, "y"), (a_src, a_dst, my_y, 0, "y"))

    loads[2].wait()
    loads[3].wait()
    weights = []
    for s in range(10):
        row = slots[0, 0, s] - 2 * me
        col = (slots[0, 1, s] - 2 * me + 1 + 2 * ndom) % (2 * ndom)
        used = s < live[0, 0]
        weights.append(
            [
                [jnp.where(used & (row == r) & (col == c), 1.0, 0.0) for c in (1, 2, 0, 3)]
                for r in range(2)
            ]
        )
    for part in range(4):
        here = slice(part * 32, part * 32 + 32)
        sums = [[None] * 4 for _ in range(2)]
        for s in range(10):
            cell = counts[0, s, here, :].astype(F32)
            for r in range(2):
                for c in range(4):
                    term = cell * weights[s][r][c]
                    sums[r][c] = term if s == 0 else sums[r][c] + term
        diag = iota((32, 128), 0) + part * 32 == iota((32, 128), 1)
        for r in range(2):
            sums[r][r] = sums[r][r] + jnp.where(diag, loop_weight, 0.0)
            for c in range(4):
                adj_f[r * 128 + part * 32 : r * 128 + part * 32 + 32, c * 128 : c * 128 + 128] = sums[r][c]
    adj[...] = adj_f[...].astype(BF16)
    for r in range(2):
        for c in range(4):
            adj_t[c * 128 : c * 128 + 128, r * 128 : r * 128 + 128] = (
                adj_f[r * 128 : r * 128 + 128, c * 128 : c * 128 + 128].T.astype(BF16)
            )
    inverse = 1.0 / dot(adj[...], jnp.ones((512, 128), BF16))
    inv_deg[:, 0:128] = inverse
    inv_deg[:, 128:256] = inverse

    loads[4].wait()
    gs_two = (out_grad[0].astype(F32) * scale_loss * inv_deg[...]).astype(BF16)
    qa_src[...] = dot(adj_t[256:512], gs_two).astype(BF16).reshape(2, 128, 256)
    send(qa_src.at[0], qa_dst.at[1], 4, left)
    send(qa_src.at[1], qa_dst.at[0], 5, right)
    gz_ref[...] = dot(adj_t[0:256], gs_two)

    source = ((rows >> 1) & (NY - 1)) * 32 + (rows >> 4) * 2 + (rows & 1)
    mid[...] = one_where(cols == source)
    regroup[...] = one_where(half_rows == (half_cols >> 4) * 2 + (half_cols & 1))
    spread[...] = one_where(half_rows == (half_cols & 15))
    loads[5].wait()
    loads[6].wait()
    loads[7].wait()
    w_two_t[...] = w_two[...].T
    w_one_t[...] = w_one[...].T

    arrived(ai_dst, 1, NY - 1)
    ids_mid = dot(ai_dst[...].reshape(NY, 128).astype(BF16), regroup[...])
    ids_mid = jnp.sum(
        jnp.where(rows[0:NY] == ((cols[0:NY] >> 1) & (NY - 1)), ids_mid, 0.0), axis=0, keepdims=True
    )
    id_left = jnp.where((cols[0:NZ] >> 4) == rows[0:NZ], ids_mid, 0.0).astype(BF16)
    bi_src[...] = dot_nt(id_left, spread[...]).reshape(NZ, 1, 128)
    arrived(a_dst, 0, NY - 1)
    b_src[...] = dot(mid[...], a_dst[...].reshape(256, 128)).astype(BF16).reshape(NZ, 16, 128)
    scatter((bi_src, bi_dst, my_z, 3, "zc"), (b_src, b_dst, my_z, 2, "zc"))

    wait_for(qa_dst.at[1], recv_sem.at[4])
    wait_for(qa_dst.at[0], recv_sem.at[5])
    gz_two = (gz_ref[...] + qa_dst[...].astype(F32).reshape(256, 256)).astype(BF16)
    gh_ref[...] = dot(gz_two, w_two_t[...]) * inv_deg[...]

    arrived(bi_dst, 3, NZ - 1)
    ids_got = dot(bi_dst[...].reshape(NZ, 128).astype(BF16), spread[...])
    ids_got = jnp.sum(
        jnp.where(rows[0:NZ] == (cols[0:NZ] >> 4), ids_got, 0.0), axis=0, keepdims=True
    )
    finish[...] = one_where(rows.astype(F32) == ids_got)
    arrived(b_dst, 2, NZ - 1)
    ev_own = dot(finish[...], b_dst[...].reshape(256, 128)).astype(BF16)
    ev_win[0:256] = ev_own
    send(ev_win.at[pl.ds(0, 128)], ev_win.at[pl.ds(384, 128)], 6, left)
    send(ev_win.at[pl.ds(128, 128)], ev_win.at[pl.ds(256, 128)], 7, right)

    def encoded(rows_in):
        pre_rows = dot(rows_in, w_enc[...])
        return pre_rows, (pre_rows * sigmoid(pre_rows)).astype(BF16)

    pre, h_zero = encoded(ev_own)
    z_own = dot(h_zero, w_one[...]).astype(BF16)
    total = dot(adj[:, 0:256], z_own)
    sig = sigmoid(pre)
    slope[0:256] = sig * (1.0 + pre * (1.0 - sig))
    h_win_t[:, 0:256] = h_zero.T
    ev_win_t[:, 0:256] = ev_own.T
    wait_for(ev_win.at[pl.ds(384, 128)], recv_sem.at[6])
    wait_for(ev_win.at[pl.ds(256, 128)], recv_sem.at[7])
    ev_side = ev_win[256:512]
    pre, h_zero = encoded(ev_side)
    z_side = dot(h_zero, w_one[...]).astype(BF16)
    agg_one = (total + dot(adj[:, 256:512], z_side)) * inv_deg[...]
    h_win_t[:, 256:512] = h_zero.T
    ev_win_t[:, 256:512] = ev_side.T
    sig = sigmoid(pre)
    slope[256:512] = sig * (1.0 + pre * (1.0 - sig))

    sig = sigmoid(agg_one)
    gs_one = (gh_ref[...] * (sig * (1.0 + agg_one * (1.0 - sig)))).astype(BF16)
    gz_one = dot(adj_t[...], gs_one).astype(BF16)
    one_src[...] = dot(h_win_t[...], gz_one).astype(BF16).reshape(NZ, 16, 256)
    h_one = (agg_one * sig).astype(BF16)
    two_src[...] = dot(h_one.T, gz_two).astype(BF16).reshape(NZ, 16, 256)
    scatter((one_src, one_dst, my_z, 10, "zc"), (two_src, two_dst, my_yc, 11, "yc"))
    gh_zero = dot(gz_one, w_one_t[...]).astype(BF16)
    g_enc = (gh_zero.astype(F32) * slope[...]).astype(BF16)
    enc_src[...] = dot(ev_win_t[...], g_enc).astype(BF16).reshape(NY, 16, 256)
    scatter((enc_src, enc_dst, my_xc, 12, "xc"))
    z_two[0:256] = dot(h_one, w_two[...]).astype(BF16)

    def summed(ref):
        return jnp.sum(ref[...].astype(F32), axis=0).astype(BF16)

    arrived(enc_dst, 12, NY - 1)
    enc_y[my_y] = summed(enc_dst)
    spread_out(enc_y, my_y, 13, "y")
    arrived(one_dst, 10, NZ - 1)
    one_mid[my_y] = summed(one_dst)
    spread_out(one_mid, my_y, 14, "y")
    arrived(two_dst, 11, NZ - 1)
    two_mid[my_zc] = summed(two_dst)
    spread_out(two_mid, my_zc, 15, "z")
    send(z_two.at[pl.ds(0, 128)], z_two.at[pl.ds(384, 128)], 8, left)
    send(z_two.at[pl.ds(128, 128)], z_two.at[pl.ds(256, 128)], 9, right)
    arrived(enc_y, 13, NY - 1)
    enc_z[my_zc] = summed(enc_y)
    spread_out(enc_z, my_zc, 16, "z")
    arrived(one_mid, 14, NY - 1)
    one_x[rep] = summed(one_mid)
    spread_out(one_x, rep, 17, "x")
    arrived(two_mid, 15, NY - 1)
    two_x[rep] = summed(two_mid)
    spread_out(two_x, rep, 18, "x")
    wait_for(z_two.at[pl.ds(384, 128)], recv_sem.at[8])
    wait_for(z_two.at[pl.ds(256, 128)], recv_sem.at[9])
    embed[0] = (dot(adj[...], z_two[...]) * inv_deg[...]).astype(BF16)
    arrived(one_x, 17, NX - 1)
    one_all[my_z] = summed(one_x)
    spread_out(one_all, my_z, 19, "zc")
    arrived(two_x, 18, NX - 1)
    two_all[my_yc] = summed(two_x)
    spread_out(two_all, my_yc, 20, "yc")
    arrived(enc_z, 16, NY - 1)
    enc_all[my_xc] = summed(enc_z)
    spread_out(enc_all, my_xc, 21, "xc")
    arrived(enc_all, 21, NY - 1)
    arrived(one_all, 19, NZ - 1)
    arrived(two_all, 20, NZ - 1)

    for step, ref in ((0, a_src), (1, ai_src), (13, enc_y), (14, one_mid), (15, two_mid), (16, enc_z)):
        left_all(ref, step, NY - 1)
    for step, ref in ((2, b_src), (3, bi_src), (10, one_src), (11, two_src), (19, one_all), (20, two_all)):
        left_all(ref, step, NZ - 1)
    for step, ref in ((12, enc_src), (21, enc_all)):
        left_all(ref, step, NY - 1)
    for step, ref in ((17, one_x), (18, two_x)):
        left_all(ref, step, NX - 1)
    for step, ref in ((4, qa_src), (5, qa_src)):
        left_all(ref, step, 1)
    for step, ref in ((6, ev_win), (7, ev_win), (8, z_two), (9, z_two)):
        left_all(ref, step, 128)


def result_kernel(
    embed, enc_all, one_all, two_all, embed_out, grad_enc, grad_one, grad_two, enc, one, two, sem
):
    stores = [pltpu.make_async_copy(embed, embed_out, sem.at[0])]
    stores[0].start()
    for i, (src, wide, out) in enumerate(
        ((enc_all, enc, grad_enc), (one_all, one, grad_one), (two_all, two, grad_two))
    ):
        wide[...] = src[...].astype(F32).reshape(wide.shape)
        stores.append(pltpu.make_async_copy(wide, out, sem.at[i + 1]))
        stores[-1].start()
    for store in stores:
        store.wait()


def body(events, perm, w_enc, w_one, w_two, slot_blocks, live_count, block_counts, out_grad):
    scale_loss = 1.0 / math.sqrt(lax.axis_size("rep") * lax.axis_size("dom") * events.shape[1])
    vmem = pl.BlockSpec(memory_space=pltpu.VMEM)
    smem = pl.BlockSpec(memory_space=pltpu.SMEM)
    hbm = pl.BlockSpec(memory_space=pltpu.HBM)
    slot_rows = jnp.swapaxes(slot_blocks, 1, 2)
    args = [
        pltpu.with_memory_space_constraint(x, pltpu.HBM)
        for x in (events, perm, w_enc, w_one, w_two, slot_rows, block_counts, out_grad)
    ]

    def pieces(*shape, dtype=BF16):
        return pltpu.VMEM(shape, dtype)

    found = pl.pallas_call(
        functools.partial(step_kernel, scale_loss),
        out_shape=(
            jax.ShapeDtypeStruct((1, 256, 256), BF16),
            jax.ShapeDtypeStruct((NY, 16, 256), BF16),
            jax.ShapeDtypeStruct((NZ, 16, 256), BF16),
            jax.ShapeDtypeStruct((NZ, 16, 256), BF16),
        ),
        in_specs=[hbm] * 6 + [smem] + [hbm] * 2,
        out_specs=(vmem, vmem, vmem, vmem),
        scratch_shapes=[
            pieces(1, 256, 128),
            pieces(1, 256, dtype=jnp.int32),
            pieces(128, 256),
            pieces(256, 256),
            pieces(256, 256),
            pieces(1, 10, 128, 128, dtype=jnp.int32),
            pieces(1, 256, 256),
            pltpu.SMEM((1, 2, 10), jnp.int32),
            pieces(256, 512, dtype=F32),
            pieces(256, 512),
            pieces(512, 256),
            pieces(256, 256, dtype=F32),
            pieces(256, 256),
            pieces(128, 256),
            pieces(128, 256),
            pieces(256, 256),
            pieces(256, 256),
            pieces(256, 256),
            pieces(512, 128),
            pieces(512, 256),
            pieces(256, 256, dtype=F32),
            pieces(256, 256, dtype=F32),
            pieces(NY, 32, 128),
            pieces(NY, 32, 128),
            pieces(NY, 1, 128, dtype=F32),
            pieces(NY, 1, 128, dtype=F32),
            pieces(NZ, 16, 128),
            pieces(NZ, 16, 128),
            pieces(NZ, 1, 128, dtype=F32),
            pieces(NZ, 1, 128, dtype=F32),
            pieces(2, 128, 256),
            pieces(2, 128, 256),
            pieces(NZ, 16, 256),
            pieces(NZ, 16, 256),
            pieces(NY, 16, 256),
            pieces(NX, 16, 256),
            pieces(NZ, 16, 256),
            pieces(NZ, 16, 256),
            pieces(NY, 16, 256),
            pieces(NX, 16, 256),
            pieces(NY, 16, 256),
            pieces(NY, 16, 256),
            pieces(NY, 16, 256),
            pieces(NY, 16, 256),
            pieces(256, 512),
            pieces(128, 512),
            pieces(512, 256, dtype=F32),
            pltpu.SemaphoreType.DMA((8,)),
            pltpu.SemaphoreType.DMA((22,)),
            pltpu.SemaphoreType.DMA((22,)),
        ],
        compiler_params=pltpu.CompilerParams(
            collective_id=0, has_side_effects=True, vmem_limit_bytes=16 * 1024 * 1024
        ),
    )(*args[:6], live_count, *args[6:])
    return pl.pallas_call(
        result_kernel,
        out_shape=(
            jax.ShapeDtypeStruct((1, 256, 256), BF16),
            jax.ShapeDtypeStruct((128, 256), F32),
            jax.ShapeDtypeStruct((256, 256), F32),
            jax.ShapeDtypeStruct((256, 256), F32),
        ),
        in_specs=[vmem] * 4,
        out_specs=(pl.BlockSpec(memory_space=pl.ANY),) * 4,
        scratch_shapes=[
            pieces(128, 256, dtype=F32),
            pieces(256, 256, dtype=F32),
            pieces(256, 256, dtype=F32),
            pltpu.SemaphoreType.DMA((4,)),
        ],
        compiler_params=pltpu.CompilerParams(vmem_limit_bytes=8 * 1024 * 1024),
    )(*found)


def solution(mesh):
    return jax.shard_map(
        body,
        mesh=mesh,
        in_specs=(
            P("rep", "dom", None),
            P("rep", "dom"),
            P(),
            P(),
            P(),
            P("rep", "dom", None),
            P("rep", "dom"),
            P("rep", "dom", None, None),
            P("rep", "dom", None),
        ),
        out_specs=(P("rep", "dom", None), P(), P(), P()),
        check_vma=False,
    )
```

```python
import functools
import math

import jax
import jax.numpy as jnp
from jax import lax
from jax.experimental import pallas as pl
from jax.experimental.pallas import tpu as pltpu
from jax.sharding import PartitionSpec as P

loop_weight = 4.0
NY = 8
NZ = 16
NX = 4
F32 = jnp.float32
BF16 = jnp.bfloat16


def dot(a, b):
    return jnp.dot(a, b, preferred_element_type=F32)


def dot_nt(a, b):
    return lax.dot_general(a, b, (((1,), (1,)), ((), ())), preferred_element_type=F32)


def sigmoid(value):
    return 1.0 / (1.0 + jnp.exp(-value))


def wait_for(ref, sem):
    pltpu.make_async_copy(ref, ref, sem).wait()


def iota(shape, dim):
    return lax.broadcasted_iota(jnp.int32, shape, dim)


def one_where(mask):
    return jnp.where(mask, 1.0, 0.0).astype(BF16)


def step_kernel(
    scale_loss,
    events_in, perm_in, w_enc_in, w_one_in, w_two_in, slots_in, live, counts_in, out_grad_in,
    embed, enc_all, one_all, two_all,
    events, perm, w_enc, w_one, w_two, counts, out_grad, slots,
    adj_f, adj, adj_t, inv_deg, mid, regroup, spread, finish, w_one_t, w_two_t,
    ev_win, z_two, gz_ref, gh_ref,
    a_src, a_dst, ai_src, ai_dst, b_src, b_dst, bi_src, bi_dst, edge, edge_i, far_rows, far_ids, qa_src, qa_dst,
    two_src, two_dst, two_mid, two_x, one_src, one_dst, one_mid, one_x,
    enc_src, enc_dst, enc_y, enc_z, h_win_t, ev_win_t, slope,
    load_sem, send_sem, recv_sem,
):
    me = lax.axis_index("dom")
    rep = lax.axis_index("rep")
    ndom = NY * NZ
    my_y = me // NZ
    my_z = me % NZ
    core = me % 2
    my_yc = my_y * 2 + core
    my_xc = rep * 2 + core
    my_zc = my_z // 2
    left = {"dom": (me + ndom - 1) % ndom}
    right = {"dom": (me + 1) % ndom}

    loads = [
        pltpu.make_async_copy(src, dst, load_sem.at[i])
        for i, (src, dst) in enumerate(
            (
                (perm_in, perm), (events_in, events), (slots_in, slots), (counts_in, counts),
                (out_grad_in, out_grad), (w_two_in, w_two), (w_enc_in, w_enc), (w_one_in, w_one),
            )
        )
    ]
    for load in loads[:2]:
        load.start()

    def others(group):
        ring = NX if group[0] == "x" else NY
        here = {"x": rep, "y": my_y, "z": my_zc}[group[0]]
        found = []
        for ahead in sorted(range(ring), key=lambda n: -min(n, ring - n)):
            chip = (here + ahead) % ring
            for flip in range(len(group)):
                if ahead or flip:
                    side = (core + flip) % 2
                    y = chip if group[0] == "y" else my_y
                    z = chip if group[0] == "z" else my_zc
                    x = chip if group[0] == "x" else rep
                    rank = chip * 2 + side if len(group) == 2 else chip
                    found.append((min(ahead, ring - ahead), rank, {"dom": y * NZ + z * 2 + side, "rep": x}))
        return found

    barrier = pltpu.get_barrier_semaphore()

    def hello(device):
        pl.semaphore_signal(barrier, inc=1, device_id=device, device_id_type=pl.DeviceIdType.MESH)

    friends = others("y") + others("zc") + [f for f in others("xc") if f[0]]
    friends.sort(key=lambda f: -f[0])
    for _, _, device in friends:
        hello(device)
    at_start = my_z == 0
    at_end = my_z == NZ - 1
    pl.when(at_start)(lambda: hello(left))
    pl.when(at_end)(lambda: hello(right))
    for load in loads[2:]:
        load.start()

    def send(src, dst, step, device):
        pltpu.make_async_remote_copy(
            src_ref=src, dst_ref=dst, send_sem=send_sem.at[step], recv_sem=recv_sem.at[step],
            device_id=device, device_id_type=pl.DeviceIdType.MESH,
        ).start()

    def scatter(*flows):
        starts = []
        for src, dst, mine, step, group in flows:
            starts += [(away, src.at[k], dst.at[mine], step, dev) for away, k, dev in others(group)]
        for _, src, dst, step, device in sorted(starts, key=lambda start: -start[0]):
            send(src, dst, step, device)
        for src, dst, mine, _, _ in flows:
            dst[mine] = src[mine]

    def spread_out(ref, mine, step, group):
        for _, _, device in others(group):
            send(ref.at[mine], ref.at[mine], step, device)

    def arrived(ref, step, count):
        wait_for(ref.at[pl.ds(0, count)], recv_sem.at[step])

    def left_all(ref, step, count):
        wait_for(ref.at[pl.ds(0, count)], send_sem.at[step])

    rows = iota((256, 256), 0)
    cols = iota((256, 256), 1)
    half_rows = rows[0:128]
    half_cols = cols[0:128]
    loads[0].wait()
    ids = perm[...]
    ids_row = ids.astype(F32)
    ids_col = jnp.sum(jnp.where(rows == cols, ids_row, 0.0), axis=1, keepdims=True)
    place = jnp.sum(jnp.where(ids_col < ids_row, 1.0, 0.0), axis=0, keepdims=True).astype(jnp.int32)
    local_row = (ids & 255).astype(F32)
    id_left = jnp.where((place >> 5) == rows[0:16], local_row, 0.0).astype(BF16)
    id_right = one_where((place & 31) == half_rows)
    ai_src[...] = dot_nt(id_left, id_right)[0:NY].reshape(NY, 1, 128)
    loads[1].wait()
    a_src[...] = dot(one_where(rows == place), events[0]).astype(BF16).reshape(NY, 32, 128)

    extra = jnp.where(at_start | at_end, 1, 0)
    pl.semaphore_wait(barrier, len(friends) + extra)
    scatter((ai_src, ai_dst, my_y, 1, "y"), (a_src, a_dst, my_y, 0, "y"))

    loads[2].wait()
    loads[3].wait()
    weights = []
    for s in range(10):
        row = slots[0, 0, s] - 2 * me
        col = (slots[0, 1, s] - 2 * me + 1 + 2 * ndom) % (2 * ndom)
        used = s < live[0, 0]
        weights.append(
            [
                [jnp.where(used & (row == r) & (col == c), 1.0, 0.0) for c in (1, 2, 0, 3)]
                for r in range(2)
            ]
        )
    for part in range(4):
        here = slice(part * 32, part * 32 + 32)
        sums = [[None] * 4 for _ in range(2)]
        for s in range(10):
            cell = counts[0, s, here, :].astype(F32)
            for r in range(2):
                for c in range(4):
                    term = cell * weights[s][r][c]
                    sums[r][c] = term if s == 0 else sums[r][c] + term
        diag = iota((32, 128), 0) + part * 32 == iota((32, 128), 1)
        for r in range(2):
            sums[r][r] = sums[r][r] + jnp.where(diag, loop_weight, 0.0)
            for c in range(4):
                adj_f[r * 128 + part * 32 : r * 128 + part * 32 + 32, c * 128 : c * 128 + 128] = sums[r][c]
    adj[...] = adj_f[...].astype(BF16)
    for r in range(2):
        for c in range(4):
            adj_t[c * 128 : c * 128 + 128, r * 128 : r * 128 + 128] = (
                adj_f[r * 128 : r * 128 + 128, c * 128 : c * 128 + 128].T.astype(BF16)
            )
    inverse = 1.0 / dot(adj[...], jnp.ones((512, 128), BF16))
    inv_deg[:, 0:128] = inverse
    inv_deg[:, 128:256] = inverse

    loads[4].wait()
    gs_two = (out_grad[0].astype(F32) * scale_loss * inv_deg[...]).astype(BF16)
    qa_src[...] = dot(adj_t[256:512], gs_two).astype(BF16).reshape(2, 128, 256)
    send(qa_src.at[0], qa_dst.at[1], 4, left)
    send(qa_src.at[1], qa_dst.at[0], 5, right)
    gz_ref[...] = dot(adj_t[0:256], gs_two)

    source = ((rows >> 1) & (NY - 1)) * 32 + (rows >> 4) * 2 + (rows & 1)
    mid[...] = one_where(cols == source)
    regroup[...] = one_where(half_rows == (half_cols >> 4) * 2 + (half_cols & 1))
    spread[...] = one_where(half_rows == (half_cols & 15))
    loads[5].wait()
    loads[6].wait()
    loads[7].wait()
    w_two_t[...] = w_two[...].T
    w_one_t[...] = w_one[...].T

    arrived(ai_dst, 1, NY - 1)
    ids_mid = dot(ai_dst[...].reshape(NY, 128).astype(BF16), regroup[...])
    ids_mid = jnp.sum(
        jnp.where(rows[0:NY] == ((cols[0:NY] >> 1) & (NY - 1)), ids_mid, 0.0), axis=0, keepdims=True
    )
    id_left = jnp.where((cols[0:NZ] >> 4) == rows[0:NZ], ids_mid, 0.0).astype(BF16)
    bi_src[1:17] = dot_nt(id_left, spread[...]).reshape(NZ, 1, 128)
    arrived(a_dst, 0, NY - 1)
    b_src[1:17] = dot(mid[...], a_dst[...].reshape(256, 128)).astype(BF16).reshape(NZ, 16, 128)
    for ref in (b_src, bi_src):
        ref[0] = ref[NZ]
        ref[NZ + 1] = ref[1]
    up = {"dom": ((my_y + 1) % NY) * NZ}
    down = {"dom": ((my_y + NY - 1) % NY) * NZ + NZ - 1}
    for src, dst, step in ((bi_src, edge_i, 23), (b_src, edge, 22)):
        send(src.at[NZ], dst.at[my_z], step, up)
        send(src.at[1], dst.at[my_z], step, down)
    for _, k, device in others("zc"):
        send(bi_src.at[pl.ds(k + k % 2, 2)], bi_dst.at[my_z], 3, device)
        send(b_src.at[pl.ds(k + k % 2, 2)], b_dst.at[my_z], 2, device)
    bi_dst[my_z] = bi_src[pl.ds(my_z + core, 2)]
    b_dst[my_z] = b_src[pl.ds(my_z + core, 2)]

    wait_for(qa_dst.at[1], recv_sem.at[4])
    wait_for(qa_dst.at[0], recv_sem.at[5])
    gz_two = (gz_ref[...] + qa_dst[...].astype(F32).reshape(256, 256)).astype(BF16)
    gh_ref[...] = dot(gz_two, w_two_t[...]) * inv_deg[...]

    def lane_ids(found):
        found = dot(found.astype(BF16), spread[...])
        return jnp.sum(jnp.where(rows[0:NZ] == (cols[0:NZ] >> 4), found, 0.0), axis=0, keepdims=True)

    low = core == 0
    arrived(bi_dst, 3, NZ - 1)
    first = bi_dst[:, 0].reshape(NZ, 128)
    second = bi_dst[:, 1].reshape(NZ, 128)
    far_ids[...] = jnp.where(low, first, second)
    finish[...] = one_where(rows.astype(F32) == lane_ids(jnp.where(low, second, first)))
    arrived(b_dst, 2, NZ - 1)
    first = b_dst[:, 0].reshape(256, 128)
    second = b_dst[:, 1].reshape(256, 128)
    far_rows[...] = jnp.where(low, first, second)
    ev_own = dot(finish[...], jnp.where(low, second, first)).astype(BF16)
    ev_win[0:256] = ev_own
    send(
        ev_win.at[pl.ds(128 * (1 - core), 128)], ev_win.at[pl.ds(256 + 128 * core, 128)], 6,
        {"dom": me + 1 - 2 * core},
    )

    @pl.when(at_start | at_end)
    def _():
        arrived(edge_i, 23, NZ)
        far_ids[...] = edge_i[...].reshape(NZ, 128)
        arrived(edge, 22, NZ)
        far_rows[...] = edge[...].reshape(256, 128)

    far_place = one_where((half_rows + 128 * (1 - core)).astype(F32) == lane_ids(far_ids[...]))
    ev_win[pl.ds(256 + 128 * core, 128)] = dot(far_place, far_rows[...]).astype(BF16)

    def encoded(rows_in):
        pre_rows = dot(rows_in, w_enc[...])
        return pre_rows, (pre_rows * sigmoid(pre_rows)).astype(BF16)

    pre, h_zero = encoded(ev_own)
    z_own = dot(h_zero, w_one[...]).astype(BF16)
    total = dot(adj[:, 0:256], z_own)
    sig = sigmoid(pre)
    slope[0:256] = sig * (1.0 + pre * (1.0 - sig))
    h_win_t[:, 0:256] = h_zero.T
    ev_win_t[:, 0:256] = ev_own.T
    wait_for(ev_win.at[pl.ds(384 - 128 * core, 128)], recv_sem.at[6])
    ev_side = ev_win[256:512]
    pre, h_zero = encoded(ev_side)
    z_side = dot(h_zero, w_one[...]).astype(BF16)
    agg_one = (total + dot(adj[:, 256:512], z_side)) * inv_deg[...]
    h_win_t[:, 256:512] = h_zero.T
    ev_win_t[:, 256:512] = ev_side.T
    sig = sigmoid(pre)
    slope[256:512] = sig * (1.0 + pre * (1.0 - sig))

    sig = sigmoid(agg_one)
    gs_one = (gh_ref[...] * (sig * (1.0 + agg_one * (1.0 - sig)))).astype(BF16)
    gz_one = dot(adj_t[...], gs_one).astype(BF16)
    one_src[...] = dot(h_win_t[...], gz_one).astype(BF16).reshape(NZ, 16, 256)
    h_one = (agg_one * sig).astype(BF16)
    two_src[...] = dot(h_one.T, gz_two).astype(BF16).reshape(NZ, 16, 256)
    scatter((one_src, one_dst, my_z, 10, "zc"), (two_src, two_dst, my_yc, 11, "yc"))
    gh_zero = dot(gz_one, w_one_t[...]).astype(BF16)
    g_enc = (gh_zero.astype(F32) * slope[...]).astype(BF16)
    enc_src[...] = dot(ev_win_t[...], g_enc).astype(BF16).reshape(NY, 16, 256)
    scatter((enc_src, enc_dst, my_xc, 12, "xc"))
    z_two[0:256] = dot(h_one, w_two[...]).astype(BF16)

    def summed(ref):
        return jnp.sum(ref[...].astype(F32), axis=0).astype(BF16)

    arrived(enc_dst, 12, NY - 1)
    enc_y[my_y] = summed(enc_dst)
    spread_out(enc_y, my_y, 13, "y")
    arrived(one_dst, 10, NZ - 1)
    one_mid[my_y] = summed(one_dst)
    spread_out(one_mid, my_y, 14, "y")
    arrived(two_dst, 11, NZ - 1)
    two_mid[my_zc] = summed(two_dst)
    spread_out(two_mid, my_zc, 15, "z")
    send(z_two.at[pl.ds(0, 128)], z_two.at[pl.ds(384, 128)], 8, left)
    send(z_two.at[pl.ds(128, 128)], z_two.at[pl.ds(256, 128)], 9, right)
    arrived(enc_y, 13, NY - 1)
    enc_z[my_zc] = summed(enc_y)
    spread_out(enc_z, my_zc, 16, "z")
    arrived(one_mid, 14, NY - 1)
    one_x[rep] = summed(one_mid)
    spread_out(one_x, rep, 17, "x")
    arrived(two_mid, 15, NY - 1)
    two_x[rep] = summed(two_mid)
    spread_out(two_x, rep, 18, "x")
    wait_for(z_two.at[pl.ds(384, 128)], recv_sem.at[8])
    wait_for(z_two.at[pl.ds(256, 128)], recv_sem.at[9])
    embed[0] = (dot(adj[...], z_two[...]) * inv_deg[...]).astype(BF16)
    arrived(one_x, 17, NX - 1)
    one_all[my_z] = summed(one_x)
    spread_out(one_all, my_z, 19, "zc")
    arrived(two_x, 18, NX - 1)
    two_all[my_yc] = summed(two_x)
    spread_out(two_all, my_yc, 20, "yc")
    arrived(enc_z, 16, NY - 1)
    enc_all[my_xc] = summed(enc_z)
    spread_out(enc_all, my_xc, 21, "xc")
    arrived(enc_all, 21, NY - 1)
    arrived(one_all, 19, NZ - 1)
    arrived(two_all, 20, NZ - 1)

    for step, ref in ((0, a_src), (1, ai_src), (13, enc_y), (14, one_mid), (15, two_mid), (16, enc_z)):
        left_all(ref, step, NY - 1)
    for step, ref in ((2, b_dst), (3, bi_dst), (10, one_src), (11, two_src), (19, one_all), (20, two_all)):
        left_all(ref, step, NZ - 1)
    for step, ref in ((12, enc_src), (21, enc_all)):
        left_all(ref, step, NY - 1)
    for step, ref in ((17, one_x), (18, two_x)):
        left_all(ref, step, NX - 1)
    for step, ref in ((4, qa_src), (5, qa_src)):
        left_all(ref, step, 1)
    left_all(b_src, 22, 2)
    left_all(bi_src, 23, 2)
    for step, ref in ((6, ev_win), (8, z_two), (9, z_two)):
        left_all(ref, step, 128)


def result_kernel(
    embed, enc_all, one_all, two_all, embed_out, grad_enc, grad_one, grad_two, enc, one, two, sem
):
    stores = [pltpu.make_async_copy(embed, embed_out, sem.at[0])]
    stores[0].start()
    for i, (src, wide, out) in enumerate(
        ((enc_all, enc, grad_enc), (one_all, one, grad_one), (two_all, two, grad_two))
    ):
        wide[...] = src[...].astype(F32).reshape(wide.shape)
        stores.append(pltpu.make_async_copy(wide, out, sem.at[i + 1]))
        stores[-1].start()
    for store in stores:
        store.wait()


def body(events, perm, w_enc, w_one, w_two, slot_blocks, live_count, block_counts, out_grad):
    scale_loss = 1.0 / math.sqrt(lax.axis_size("rep") * lax.axis_size("dom") * events.shape[1])
    vmem = pl.BlockSpec(memory_space=pltpu.VMEM)
    smem = pl.BlockSpec(memory_space=pltpu.SMEM)
    hbm = pl.BlockSpec(memory_space=pltpu.HBM)
    slot_rows = jnp.swapaxes(slot_blocks, 1, 2)
    args = [
        pltpu.with_memory_space_constraint(x, pltpu.HBM)
        for x in (events, perm, w_enc, w_one, w_two, slot_rows, block_counts, out_grad)
    ]

    def pieces(*shape, dtype=BF16):
        return pltpu.VMEM(shape, dtype)

    found = pl.pallas_call(
        functools.partial(step_kernel, scale_loss),
        out_shape=(
            jax.ShapeDtypeStruct((1, 256, 256), BF16),
            jax.ShapeDtypeStruct((NY, 16, 256), BF16),
            jax.ShapeDtypeStruct((NZ, 16, 256), BF16),
            jax.ShapeDtypeStruct((NZ, 16, 256), BF16),
        ),
        in_specs=[hbm] * 6 + [smem] + [hbm] * 2,
        out_specs=(vmem, vmem, vmem, vmem),
        scratch_shapes=[
            pieces(1, 256, 128),
            pieces(1, 256, dtype=jnp.int32),
            pieces(128, 256),
            pieces(256, 256),
            pieces(256, 256),
            pieces(1, 10, 128, 128, dtype=jnp.int32),
            pieces(1, 256, 256),
            pltpu.SMEM((1, 2, 10), jnp.int32),
            pieces(256, 512, dtype=F32),
            pieces(256, 512),
            pieces(512, 256),
            pieces(256, 256, dtype=F32),
            pieces(256, 256),
            pieces(128, 256),
            pieces(128, 256),
            pieces(256, 256),
            pieces(256, 256),
            pieces(256, 256),
            pieces(512, 128),
            pieces(512, 256),
            pieces(256, 256, dtype=F32),
            pieces(256, 256, dtype=F32),
            pieces(NY, 32, 128),
            pieces(NY, 32, 128),
            pieces(NY, 1, 128, dtype=F32),
            pieces(NY, 1, 128, dtype=F32),
            pieces(NZ + 2, 16, 128),
            pieces(NZ, 2, 16, 128),
            pieces(NZ + 2, 1, 128, dtype=F32),
            pieces(NZ, 2, 1, 128, dtype=F32),
            pieces(NZ, 16, 128),
            pieces(NZ, 1, 128, dtype=F32),
            pieces(256, 128),
            pieces(NZ, 128, dtype=F32),
            pieces(2, 128, 256),
            pieces(2, 128, 256),
            pieces(NZ, 16, 256),
            pieces(NZ, 16, 256),
            pieces(NY, 16, 256),
            pieces(NX, 16, 256),
            pieces(NZ, 16, 256),
            pieces(NZ, 16, 256),
            pieces(NY, 16, 256),
            pieces(NX, 16, 256),
            pieces(NY, 16, 256),
            pieces(NY, 16, 256),
            pieces(NY, 16, 256),
            pieces(NY, 16, 256),
            pieces(256, 512),
            pieces(128, 512),
            pieces(512, 256, dtype=F32),
            pltpu.SemaphoreType.DMA((8,)),
            pltpu.SemaphoreType.DMA((24,)),
            pltpu.SemaphoreType.DMA((24,)),
        ],
        compiler_params=pltpu.CompilerParams(
            collective_id=0, has_side_effects=True, vmem_limit_bytes=16 * 1024 * 1024
        ),
    )(*args[:6], live_count, *args[6:])
    return pl.pallas_call(
        result_kernel,
        out_shape=(
            jax.ShapeDtypeStruct((1, 256, 256), BF16),
            jax.ShapeDtypeStruct((128, 256), F32),
            jax.ShapeDtypeStruct((256, 256), F32),
            jax.ShapeDtypeStruct((256, 256), F32),
        ),
        in_specs=[vmem] * 4,
        out_specs=(pl.BlockSpec(memory_space=pl.ANY),) * 4,
        scratch_shapes=[
            pieces(128, 256, dtype=F32),
            pieces(256, 256, dtype=F32),
            pieces(256, 256, dtype=F32),
            pltpu.SemaphoreType.DMA((4,)),
        ],
        compiler_params=pltpu.CompilerParams(vmem_limit_bytes=8 * 1024 * 1024),
    )(*found)


def solution(mesh):
    return jax.shard_map(
        body,
        mesh=mesh,
        in_specs=(
            P("rep", "dom", None),
            P("rep", "dom"),
            P(),
            P(),
            P(),
            P("rep", "dom", None),
            P("rep", "dom"),
            P("rep", "dom", None, None),
            P("rep", "dom", None),
        ),
        out_specs=(P("rep", "dom", None), P(), P(), P()),
        check_vma=False,
    )
```

```python
import functools
import math

import jax
import jax.numpy as jnp
from jax import lax
from jax.experimental import pallas as pl
from jax.experimental.pallas import tpu as pltpu
from jax.sharding import PartitionSpec as P

loop_weight = 4.0
NY = 8
NZ = 16
NX = 4
F32 = jnp.float32
BF16 = jnp.bfloat16


def dot(a, b):
    return jnp.dot(a, b, preferred_element_type=F32)


def dot_nt(a, b):
    return lax.dot_general(a, b, (((1,), (1,)), ((), ())), preferred_element_type=F32)


def sigmoid(value):
    return 1.0 / (1.0 + jnp.exp(-value))


def wait_for(ref, sem):
    pltpu.make_async_copy(ref, ref, sem).wait()


def iota(shape, dim):
    return lax.broadcasted_iota(jnp.int32, shape, dim)


def one_where(mask):
    return jnp.where(mask, 1.0, 0.0).astype(BF16)


def step_kernel(
    scale_loss,
    events_in, perm_in, w_enc_in, w_one_in, w_two_in, slots_in, live, counts_in, out_grad_in,
    embed, enc_all, one_a_all, one_b_all, two_a_all, two_b_all,
    events, perm, w_enc, w_one, w_two, counts, out_grad, slots,
    adj_f, adj, adj_t, inv_deg, mid, regroup, spread, finish, w_one_t, w_two_t,
    ev_win, z_two, gz_ref, gh_ref,
    a_src, a_dst, ai_src, ai_dst, b_src, b_dst, bi_src, bi_dst, edge, edge_i, far_rows, far_ids, qa_src, qa_dst,
    two_a_src, two_a_dst, two_a_mid, two_b_src, two_b_dst, two_b_mid, two_x,
    one_a_src, one_a_dst, one_a_mid, one_b_src, one_b_dst, one_b_mid, one_x,
    enc_src, enc_dst, enc_y, enc_z, h_win_t, ev_win_t, slope,
    load_sem, send_sem, recv_sem,
):
    me = lax.axis_index("dom")
    rep = lax.axis_index("rep")
    ndom = NY * NZ
    my_y = me // NZ
    my_z = me % NZ
    core = me % 2
    my_yc = my_y * 2 + core
    my_xc = rep * 2 + core
    my_zc = my_z // 2
    left = {"dom": (me + ndom - 1) % ndom}
    right = {"dom": (me + 1) % ndom}

    loads = [
        pltpu.make_async_copy(src, dst, load_sem.at[i])
        for i, (src, dst) in enumerate(
            (
                (perm_in, perm), (events_in, events), (slots_in, slots), (counts_in, counts),
                (out_grad_in, out_grad), (w_two_in, w_two), (w_enc_in, w_enc), (w_one_in, w_one),
            )
        )
    ]
    for load in loads[:2]:
        load.start()

    def others(group):
        ring = NX if group[0] == "x" else NY
        here = {"x": rep, "y": my_y, "z": my_zc}[group[0]]
        found = []
        for ahead in sorted(range(ring), key=lambda n: -min(n, ring - n)):
            chip = (here + ahead) % ring
            for flip in range(len(group)):
                if ahead or flip:
                    side = (core + flip) % 2
                    y = chip if group[0] == "y" else my_y
                    z = chip if group[0] == "z" else my_zc
                    x = chip if group[0] == "x" else rep
                    rank = chip * 2 + side if len(group) == 2 else chip
                    found.append((min(ahead, ring - ahead), rank, {"dom": y * NZ + z * 2 + side, "rep": x}))
        return found

    barrier = pltpu.get_barrier_semaphore()

    def hello(device):
        pl.semaphore_signal(barrier, inc=1, device_id=device, device_id_type=pl.DeviceIdType.MESH)

    friends = others("y") + others("zc") + [f for f in others("xc") if f[0]]
    friends.sort(key=lambda f: -f[0])
    for _, _, device in friends:
        hello(device)
    at_start = my_z == 0
    at_end = my_z == NZ - 1
    pl.when(at_start)(lambda: hello(left))
    pl.when(at_end)(lambda: hello(right))
    for load in loads[2:]:
        load.start()

    def send(src, dst, step, device):
        pltpu.make_async_remote_copy(
            src_ref=src, dst_ref=dst, send_sem=send_sem.at[step], recv_sem=recv_sem.at[step],
            device_id=device, device_id_type=pl.DeviceIdType.MESH,
        ).start()

    def scatter(*flows):
        starts = []
        for src, dst, mine, step, group in flows:
            starts += [(away, src.at[k], dst.at[mine], step, dev) for away, k, dev in others(group)]
        for _, src, dst, step, device in sorted(starts, key=lambda start: -start[0]):
            send(src, dst, step, device)
        for src, dst, mine, _, _ in flows:
            dst[mine] = src[mine]

    def spread_out(*flows):
        starts = []
        for ref, mine, step, group in flows:
            starts += [(away, ref.at[mine], step, dev) for away, _, dev in others(group)]
        for _, piece, step, device in sorted(starts, key=lambda start: -start[0]):
            send(piece, piece, step, device)

    def arrived(ref, step, count):
        wait_for(ref.at[pl.ds(0, count)], recv_sem.at[step])

    def left_all(ref, step, count):
        wait_for(ref.at[pl.ds(0, count)], send_sem.at[step])

    rows = iota((256, 256), 0)
    cols = iota((256, 256), 1)
    half_rows = rows[0:128]
    half_cols = cols[0:128]
    loads[0].wait()
    ids = perm[...]
    ids_row = ids.astype(F32)
    ids_col = jnp.sum(jnp.where(rows == cols, ids_row, 0.0), axis=1, keepdims=True)
    place = jnp.sum(jnp.where(ids_col < ids_row, 1.0, 0.0), axis=0, keepdims=True).astype(jnp.int32)
    local_row = (ids & 255).astype(F32)
    id_left = jnp.where((place >> 5) == rows[0:16], local_row, 0.0).astype(BF16)
    id_right = one_where((place & 31) == half_rows)
    ai_src[...] = dot_nt(id_left, id_right)[0:NY].reshape(NY, 1, 128)
    loads[1].wait()
    a_src[...] = dot(one_where(rows == place), events[0]).astype(BF16).reshape(NY, 32, 128)

    extra = jnp.where(at_start | at_end, 1, 0)
    pl.semaphore_wait(barrier, len(friends) + extra)
    scatter((ai_src, ai_dst, my_y, 1, "y"), (a_src, a_dst, my_y, 0, "y"))

    loads[2].wait()
    loads[3].wait()
    weights = []
    for s in range(10):
        row = slots[0, 0, s] - 2 * me
        col = (slots[0, 1, s] - 2 * me + 1 + 2 * ndom) % (2 * ndom)
        used = s < live[0, 0]
        weights.append(
            [
                [jnp.where(used & (row == r) & (col == c), 1.0, 0.0) for c in (1, 2, 0, 3)]
                for r in range(2)
            ]
        )
    for part in range(4):
        here = slice(part * 32, part * 32 + 32)
        sums = [[None] * 4 for _ in range(2)]
        for s in range(10):
            cell = counts[0, s, here, :].astype(F32)
            for r in range(2):
                for c in range(4):
                    term = cell * weights[s][r][c]
                    sums[r][c] = term if s == 0 else sums[r][c] + term
        diag = iota((32, 128), 0) + part * 32 == iota((32, 128), 1)
        for r in range(2):
            sums[r][r] = sums[r][r] + jnp.where(diag, loop_weight, 0.0)
            for c in range(4):
                adj_f[r * 128 + part * 32 : r * 128 + part * 32 + 32, c * 128 : c * 128 + 128] = sums[r][c]
    adj[...] = adj_f[...].astype(BF16)
    for r in range(2):
        for c in range(4):
            adj_t[c * 128 : c * 128 + 128, r * 128 : r * 128 + 128] = (
                adj_f[r * 128 : r * 128 + 128, c * 128 : c * 128 + 128].T.astype(BF16)
            )
    inverse = 1.0 / dot(adj[...], jnp.ones((512, 128), BF16))
    inv_deg[:, 0:128] = inverse
    inv_deg[:, 128:256] = inverse

    loads[4].wait()
    gs_two = (out_grad[0].astype(F32) * scale_loss * inv_deg[...]).astype(BF16)
    qa_src[...] = dot(adj_t[256:512], gs_two).astype(BF16).reshape(2, 128, 256)
    send(qa_src.at[0], qa_dst.at[1], 4, left)
    send(qa_src.at[1], qa_dst.at[0], 5, right)
    gz_ref[...] = dot(adj_t[0:256], gs_two)

    source = ((rows >> 1) & (NY - 1)) * 32 + (rows >> 4) * 2 + (rows & 1)
    mid[...] = one_where(cols == source)
    regroup[...] = one_where(half_rows == (half_cols >> 4) * 2 + (half_cols & 1))
    spread[...] = one_where(half_rows == (half_cols & 15))
    loads[5].wait()
    loads[6].wait()
    loads[7].wait()
    w_two_t[...] = w_two[...].T
    w_one_t[...] = w_one[...].T

    arrived(ai_dst, 1, NY - 1)
    ids_mid = dot(ai_dst[...].reshape(NY, 128).astype(BF16), regroup[...])
    ids_mid = jnp.sum(
        jnp.where(rows[0:NY] == ((cols[0:NY] >> 1) & (NY - 1)), ids_mid, 0.0), axis=0, keepdims=True
    )
    id_left = jnp.where((cols[0:NZ] >> 4) == rows[0:NZ], ids_mid, 0.0).astype(BF16)
    bi_src[1:17] = dot_nt(id_left, spread[...]).reshape(NZ, 1, 128)
    arrived(a_dst, 0, NY - 1)
    b_src[1:17] = dot(mid[...], a_dst[...].reshape(256, 128)).astype(BF16).reshape(NZ, 16, 128)
    for ref in (b_src, bi_src):
        ref[0] = ref[NZ]
        ref[NZ + 1] = ref[1]
    up = {"dom": ((my_y + 1) % NY) * NZ}
    down = {"dom": ((my_y + NY - 1) % NY) * NZ + NZ - 1}
    for src, dst, step in ((bi_src, edge_i, 23), (b_src, edge, 22)):
        send(src.at[NZ], dst.at[my_z], step, up)
        send(src.at[1], dst.at[my_z], step, down)
    for _, k, device in others("zc"):
        send(bi_src.at[pl.ds(k + k % 2, 2)], bi_dst.at[my_z], 3, device)
        send(b_src.at[pl.ds(k + k % 2, 2)], b_dst.at[my_z], 2, device)
    bi_dst[my_z] = bi_src[pl.ds(my_z + core, 2)]
    b_dst[my_z] = b_src[pl.ds(my_z + core, 2)]

    wait_for(qa_dst.at[1], recv_sem.at[4])
    wait_for(qa_dst.at[0], recv_sem.at[5])
    gz_two = (gz_ref[...] + qa_dst[...].astype(F32).reshape(256, 256)).astype(BF16)
    gh_ref[...] = dot(gz_two, w_two_t[...]) * inv_deg[...]

    def lane_ids(found):
        found = dot(found.astype(BF16), spread[...])
        return jnp.sum(jnp.where(rows[0:NZ] == (cols[0:NZ] >> 4), found, 0.0), axis=0, keepdims=True)

    low = core == 0
    arrived(bi_dst, 3, NZ - 1)
    first = bi_dst[:, 0].reshape(NZ, 128)
    second = bi_dst[:, 1].reshape(NZ, 128)
    far_ids[...] = jnp.where(low, first, second)
    finish[...] = one_where(rows.astype(F32) == lane_ids(jnp.where(low, second, first)))
    arrived(b_dst, 2, NZ - 1)
    first = b_dst[:, 0].reshape(256, 128)
    second = b_dst[:, 1].reshape(256, 128)
    far_rows[...] = jnp.where(low, first, second)
    ev_own = dot(finish[...], jnp.where(low, second, first)).astype(BF16)
    ev_win[0:256] = ev_own
    send(
        ev_win.at[pl.ds(128 * (1 - core), 128)], ev_win.at[pl.ds(256 + 128 * core, 128)], 6,
        {"dom": me + 1 - 2 * core},
    )

    @pl.when(at_start | at_end)
    def _():
        arrived(edge_i, 23, NZ)
        far_ids[...] = edge_i[...].reshape(NZ, 128)
        arrived(edge, 22, NZ)
        far_rows[...] = edge[...].reshape(256, 128)

    far_place = one_where((half_rows + 128 * (1 - core)).astype(F32) == lane_ids(far_ids[...]))
    ev_win[pl.ds(256 + 128 * core, 128)] = dot(far_place, far_rows[...]).astype(BF16)

    def encoded(rows_in):
        pre_rows = dot(rows_in, w_enc[...])
        return pre_rows, (pre_rows * sigmoid(pre_rows)).astype(BF16)

    pre, h_zero = encoded(ev_own)
    z_own = dot(h_zero, w_one[...]).astype(BF16)
    total = dot(adj[:, 0:256], z_own)
    sig = sigmoid(pre)
    slope[0:256] = sig * (1.0 + pre * (1.0 - sig))
    h_win_t[:, 0:256] = h_zero.T
    ev_win_t[:, 0:256] = ev_own.T
    wait_for(ev_win.at[pl.ds(384 - 128 * core, 128)], recv_sem.at[6])
    ev_side = ev_win[256:512]
    pre, h_zero = encoded(ev_side)
    z_side = dot(h_zero, w_one[...]).astype(BF16)
    agg_one = (total + dot(adj[:, 256:512], z_side)) * inv_deg[...]
    h_win_t[:, 256:512] = h_zero.T
    ev_win_t[:, 256:512] = ev_side.T
    sig = sigmoid(pre)
    slope[256:512] = sig * (1.0 + pre * (1.0 - sig))

    sig = sigmoid(agg_one)
    h_one = (agg_one * sig).astype(BF16)
    grad = dot(h_one.T, gz_two).astype(BF16).reshape(NZ, 16, 256)
    two_a_src[...] = grad[:, :, 0:128]
    two_b_src[...] = grad[:, :, 128:256]
    scatter((two_a_src, two_a_dst, my_yc, 24, "yc"), (two_b_src, two_b_dst, my_z, 25, "zc"))
    gs_one = (gh_ref[...] * (sig * (1.0 + agg_one * (1.0 - sig)))).astype(BF16)
    gz_one = dot(adj_t[...], gs_one).astype(BF16)
    grad = dot(h_win_t[...], gz_one).astype(BF16).reshape(NZ, 16, 256)
    one_a_src[...] = grad[:, :, 0:128]
    one_b_src[...] = grad[:, :, 128:256]
    scatter((one_a_src, one_a_dst, my_yc, 10, "yc"), (one_b_src, one_b_dst, my_z, 11, "zc"))
    gh_zero = dot(gz_one, w_one_t[...]).astype(BF16)
    g_enc = (gh_zero.astype(F32) * slope[...]).astype(BF16)
    enc_src[...] = dot(ev_win_t[...], g_enc).astype(BF16).reshape(NY, 16, 256)
    scatter((enc_src, enc_dst, my_xc, 12, "xc"))
    z_two[0:256] = dot(h_one, w_two[...]).astype(BF16)

    def summed(ref):
        return jnp.sum(ref[...].astype(F32), axis=0).astype(BF16)

    arrived(two_a_dst, 24, NZ - 1)
    two_a_mid[my_zc] = summed(two_a_dst)
    spread_out((two_a_mid, my_zc, 14, "z"))
    arrived(two_b_dst, 25, NZ - 1)
    two_b_mid[my_y] = summed(two_b_dst)
    spread_out((two_b_mid, my_y, 15, "y"))
    arrived(enc_dst, 12, NY - 1)
    enc_y[my_y] = summed(enc_dst)
    spread_out((enc_y, my_y, 13, "y"))
    arrived(one_a_dst, 10, NZ - 1)
    one_a_mid[my_zc] = summed(one_a_dst)
    spread_out((one_a_mid, my_zc, 26, "z"))
    arrived(one_b_dst, 11, NZ - 1)
    one_b_mid[my_y] = summed(one_b_dst)
    spread_out((one_b_mid, my_y, 27, "y"))
    send(z_two.at[pl.ds(0, 128)], z_two.at[pl.ds(384, 128)], 8, left)
    send(z_two.at[pl.ds(128, 128)], z_two.at[pl.ds(256, 128)], 9, right)
    arrived(two_a_mid, 14, NY - 1)
    two_x[rep, :, 0:128] = summed(two_a_mid)
    arrived(two_b_mid, 15, NY - 1)
    two_x[rep, :, 128:256] = summed(two_b_mid)
    spread_out((two_x, rep, 18, "x"))
    arrived(enc_y, 13, NY - 1)
    enc_z[my_zc] = summed(enc_y)
    spread_out((enc_z, my_zc, 16, "z"))
    arrived(one_a_mid, 26, NY - 1)
    one_x[rep, :, 0:128] = summed(one_a_mid)
    arrived(one_b_mid, 27, NY - 1)
    one_x[rep, :, 128:256] = summed(one_b_mid)
    spread_out((one_x, rep, 17, "x"))
    arrived(two_x, 18, NX - 1)
    total = summed(two_x)
    two_a_all[my_yc] = total[:, 0:128]
    two_b_all[my_z] = total[:, 128:256]
    spread_out((two_a_all, my_yc, 20, "yc"), (two_b_all, my_z, 28, "zc"))
    arrived(one_x, 17, NX - 1)
    total = summed(one_x)
    one_a_all[my_yc] = total[:, 0:128]
    one_b_all[my_z] = total[:, 128:256]
    spread_out((one_a_all, my_yc, 19, "yc"), (one_b_all, my_z, 29, "zc"))
    arrived(enc_z, 16, NY - 1)
    enc_all[my_xc] = summed(enc_z)
    spread_out((enc_all, my_xc, 21, "xc"))
    wait_for(z_two.at[pl.ds(384, 128)], recv_sem.at[8])
    wait_for(z_two.at[pl.ds(256, 128)], recv_sem.at[9])
    embed[0] = (dot(adj[...], z_two[...]) * inv_deg[...]).astype(BF16)
    arrived(two_a_all, 20, NZ - 1)
    arrived(two_b_all, 28, NZ - 1)
    arrived(enc_all, 21, NY - 1)
    arrived(one_a_all, 19, NZ - 1)
    arrived(one_b_all, 29, NZ - 1)

    for step, ref in ((0, a_src), (1, ai_src), (13, enc_y), (16, enc_z)):
        left_all(ref, step, NY - 1)
    for step, ref in ((14, two_a_mid), (15, two_b_mid), (26, one_a_mid), (27, one_b_mid)):
        left_all(ref, step, NY - 1)
    for step, ref in ((2, b_dst), (3, bi_dst), (10, one_a_src), (11, one_b_src), (19, one_a_all), (29, one_b_all)):
        left_all(ref, step, NZ - 1)
    for step, ref in ((24, two_a_src), (25, two_b_src), (20, two_a_all), (28, two_b_all)):
        left_all(ref, step, NZ - 1)
    for step, ref in ((12, enc_src), (21, enc_all)):
        left_all(ref, step, NY - 1)
    for step, ref in ((17, one_x), (18, two_x)):
        left_all(ref, step, NX - 1)
    for step, ref in ((4, qa_src), (5, qa_src)):
        left_all(ref, step, 1)
    left_all(b_src, 22, 2)
    left_all(bi_src, 23, 2)
    for step, ref in ((6, ev_win), (8, z_two), (9, z_two)):
        left_all(ref, step, 128)


def result_kernel(
    embed, enc_all, one_a, one_b, two_a, two_b, embed_out, grad_enc, grad_one, grad_two, enc, one, two, sem
):
    stores = [pltpu.make_async_copy(embed, embed_out, sem.at[0])]
    stores[0].start()
    one[:, 0:128] = one_a[...].astype(F32).reshape(256, 128)
    one[:, 128:256] = one_b[...].astype(F32).reshape(256, 128)
    stores.append(pltpu.make_async_copy(one, grad_one, sem.at[1]))
    stores[1].start()
    two[:, 0:128] = two_a[...].astype(F32).reshape(256, 128)
    two[:, 128:256] = two_b[...].astype(F32).reshape(256, 128)
    stores.append(pltpu.make_async_copy(two, grad_two, sem.at[2]))
    stores[2].start()
    enc[...] = enc_all[...].astype(F32).reshape(128, 256)
    stores.append(pltpu.make_async_copy(enc, grad_enc, sem.at[3]))
    stores[3].start()
    for store in stores:
        store.wait()


def body(events, perm, w_enc, w_one, w_two, slot_blocks, live_count, block_counts, out_grad):
    scale_loss = 1.0 / math.sqrt(lax.axis_size("rep") * lax.axis_size("dom") * events.shape[1])
    vmem = pl.BlockSpec(memory_space=pltpu.VMEM)
    smem = pl.BlockSpec(memory_space=pltpu.SMEM)
    hbm = pl.BlockSpec(memory_space=pltpu.HBM)
    slot_rows = jnp.swapaxes(slot_blocks, 1, 2)
    args = [
        pltpu.with_memory_space_constraint(x, pltpu.HBM)
        for x in (events, perm, w_enc, w_one, w_two, slot_rows, block_counts, out_grad)
    ]

    def pieces(*shape, dtype=BF16):
        return pltpu.VMEM(shape, dtype)

    found = pl.pallas_call(
        functools.partial(step_kernel, scale_loss),
        out_shape=(
            jax.ShapeDtypeStruct((1, 256, 256), BF16),
            jax.ShapeDtypeStruct((NY, 16, 256), BF16),
            jax.ShapeDtypeStruct((NZ, 16, 128), BF16),
            jax.ShapeDtypeStruct((NZ, 16, 128), BF16),
            jax.ShapeDtypeStruct((NZ, 16, 128), BF16),
            jax.ShapeDtypeStruct((NZ, 16, 128), BF16),
        ),
        in_specs=[hbm] * 6 + [smem] + [hbm] * 2,
        out_specs=(vmem,) * 6,
        scratch_shapes=[
            pieces(1, 256, 128),
            pieces(1, 256, dtype=jnp.int32),
            pieces(128, 256),
            pieces(256, 256),
            pieces(256, 256),
            pieces(1, 10, 128, 128, dtype=jnp.int32),
            pieces(1, 256, 256),
            pltpu.SMEM((1, 2, 10), jnp.int32),
            pieces(256, 512, dtype=F32),
            pieces(256, 512),
            pieces(512, 256),
            pieces(256, 256, dtype=F32),
            pieces(256, 256),
            pieces(128, 256),
            pieces(128, 256),
            pieces(256, 256),
            pieces(256, 256),
            pieces(256, 256),
            pieces(512, 128),
            pieces(512, 256),
            pieces(256, 256, dtype=F32),
            pieces(256, 256, dtype=F32),
            pieces(NY, 32, 128),
            pieces(NY, 32, 128),
            pieces(NY, 1, 128, dtype=F32),
            pieces(NY, 1, 128, dtype=F32),
            pieces(NZ + 2, 16, 128),
            pieces(NZ, 2, 16, 128),
            pieces(NZ + 2, 1, 128, dtype=F32),
            pieces(NZ, 2, 1, 128, dtype=F32),
            pieces(NZ, 16, 128),
            pieces(NZ, 1, 128, dtype=F32),
            pieces(256, 128),
            pieces(NZ, 128, dtype=F32),
            pieces(2, 128, 256),
            pieces(2, 128, 256),
            pieces(NZ, 16, 128),
            pieces(NZ, 16, 128),
            pieces(NY, 16, 128),
            pieces(NZ, 16, 128),
            pieces(NZ, 16, 128),
            pieces(NY, 16, 128),
            pieces(NX, 16, 256),
            pieces(NZ, 16, 128),
            pieces(NZ, 16, 128),
            pieces(NY, 16, 128),
            pieces(NZ, 16, 128),
            pieces(NZ, 16, 128),
            pieces(NY, 16, 128),
            pieces(NX, 16, 256),
            pieces(NY, 16, 256),
            pieces(NY, 16, 256),
            pieces(NY, 16, 256),
            pieces(NY, 16, 256),
            pieces(256, 512),
            pieces(128, 512),
            pieces(512, 256, dtype=F32),
            pltpu.SemaphoreType.DMA((8,)),
            pltpu.SemaphoreType.DMA((30,)),
            pltpu.SemaphoreType.DMA((30,)),
        ],
        compiler_params=pltpu.CompilerParams(
            collective_id=0, has_side_effects=True, vmem_limit_bytes=16 * 1024 * 1024
        ),
    )(*args[:6], live_count, *args[6:])
    return pl.pallas_call(
        result_kernel,
        out_shape=(
            jax.ShapeDtypeStruct((1, 256, 256), BF16),
            jax.ShapeDtypeStruct((128, 256), F32),
            jax.ShapeDtypeStruct((256, 256), F32),
            jax.ShapeDtypeStruct((256, 256), F32),
        ),
        in_specs=[vmem] * 6,
        out_specs=(pl.BlockSpec(memory_space=pl.ANY),) * 4,
        scratch_shapes=[
            pieces(128, 256, dtype=F32),
            pieces(256, 256, dtype=F32),
            pieces(256, 256, dtype=F32),
            pltpu.SemaphoreType.DMA((4,)),
        ],
        compiler_params=pltpu.CompilerParams(vmem_limit_bytes=8 * 1024 * 1024),
    )(*found)


def solution(mesh):
    return jax.shard_map(
        body,
        mesh=mesh,
        in_specs=(
            P("rep", "dom", None),
            P("rep", "dom"),
            P(),
            P(),
            P(),
            P("rep", "dom", None),
            P("rep", "dom"),
            P("rep", "dom", None, None),
            P("rep", "dom", None),
        ),
        out_specs=(P("rep", "dom", None), P(), P(), P()),
        check_vma=False,
    )
```

```python
import functools
import math

import jax
import jax.numpy as jnp
from jax import lax
from jax.experimental import pallas as pl
from jax.experimental.pallas import tpu as pltpu
from jax.sharding import PartitionSpec as P

loop_weight = 4.0
NY = 8
NZ = 16
NX = 4
F32 = jnp.float32
BF16 = jnp.bfloat16


def dot(a, b):
    return jnp.dot(a, b, preferred_element_type=F32)


def dot_nt(a, b):
    return lax.dot_general(a, b, (((1,), (1,)), ((), ())), preferred_element_type=F32)


def sigmoid(value):
    return 1.0 / (1.0 + jnp.exp(-value))


def wait_for(ref, sem):
    pltpu.make_async_copy(ref, ref, sem).wait()


def iota(shape, dim):
    return lax.broadcasted_iota(jnp.int32, shape, dim)


def one_where(mask):
    return jnp.where(mask, 1.0, 0.0).astype(BF16)


def step_kernel(
    scale_loss,
    events_in, perm_in, w_enc_in, w_one_in, w_two_in, slots_in, live, counts_in, out_grad_in,
    embed, enc_all, one_all, two_all,
    events, perm, w_enc, w_one, w_two, counts, out_grad, slots,
    adj_f, adj, adj_t, inv_deg, mid, regroup, spread, finish, w_one_t, w_two_t,
    ev_win, z_two, gz_ref, gh_ref,
    a_src, a_dst, ai_src, ai_dst, b_src, b_dst, bi_src, bi_dst, edge, edge_i, far_rows, far_ids, qa_src, qa_dst,
    two_f, two_give, two_take, two_src, two_dst, two_mid, two_x,
    one_f, one_give, one_take, one_src, one_dst, one_mid, one_x,
    enc_src, enc_dst, enc_y, enc_z, h_win_t, ev_win_t, slope,
    load_sem, send_sem, recv_sem,
):
    me = lax.axis_index("dom")
    rep = lax.axis_index("rep")
    ndom = NY * NZ
    my_y = me // NZ
    my_z = me % NZ
    core = me % 2
    my_yc = my_y * 2 + core
    my_xc = rep * 2 + core
    my_zc = my_z // 2
    left = {"dom": (me + ndom - 1) % ndom}
    right = {"dom": (me + 1) % ndom}
    other_core = {"dom": me + 1 - 2 * core}

    loads = [
        pltpu.make_async_copy(src, dst, load_sem.at[i])
        for i, (src, dst) in enumerate(
            (
                (perm_in, perm), (events_in, events), (slots_in, slots), (counts_in, counts),
                (out_grad_in, out_grad), (w_two_in, w_two), (w_enc_in, w_enc), (w_one_in, w_one),
            )
        )
    ]
    for load in loads[:2]:
        load.start()

    def others(group):
        ring = NX if group[0] == "x" else NY
        here = {"x": rep, "y": my_y, "z": my_zc}[group[0]]
        found = []
        for ahead in sorted(range(ring), key=lambda n: -min(n, ring - n)):
            chip = (here + ahead) % ring
            for flip in range(len(group)):
                if ahead or flip:
                    side = (core + flip) % 2
                    y = chip if group[0] == "y" else my_y
                    z = chip if group[0] == "z" else my_zc
                    x = chip if group[0] == "x" else rep
                    rank = chip * 2 + side if len(group) == 2 else chip
                    found.append((min(ahead, ring - ahead), rank, {"dom": y * NZ + z * 2 + side, "rep": x}))
        return found

    barrier = pltpu.get_barrier_semaphore()

    def hello(device):
        pl.semaphore_signal(barrier, inc=1, device_id=device, device_id_type=pl.DeviceIdType.MESH)

    friends = others("y") + others("zc") + [f for f in others("xc") if f[0]]
    friends.sort(key=lambda f: -f[0])
    for _, _, device in friends:
        hello(device)
    at_start = my_z == 0
    at_end = my_z == NZ - 1
    pl.when(at_start)(lambda: hello(left))
    pl.when(at_end)(lambda: hello(right))
    for load in loads[2:]:
        load.start()

    def send(src, dst, step, device):
        pltpu.make_async_remote_copy(
            src_ref=src, dst_ref=dst, send_sem=send_sem.at[step], recv_sem=recv_sem.at[step],
            device_id=device, device_id_type=pl.DeviceIdType.MESH,
        ).start()

    def scatter(*flows):
        starts = []
        for src, dst, mine, step, group in flows:
            starts += [(away, src.at[k], dst.at[mine], step, dev) for away, k, dev in others(group)]
        for _, src, dst, step, device in sorted(starts, key=lambda start: -start[0]):
            send(src, dst, step, device)
        for src, dst, mine, _, _ in flows:
            dst[mine] = src[mine]

    def spread_out(ref, mine, step, group):
        for _, _, device in others(group):
            send(ref.at[mine], ref.at[mine], step, device)

    def arrived(ref, step, count):
        wait_for(ref.at[pl.ds(0, count)], recv_sem.at[step])

    def left_all(ref, step, count):
        wait_for(ref.at[pl.ds(0, count)], send_sem.at[step])

    rows = iota((256, 256), 0)
    cols = iota((256, 256), 1)
    half_rows = rows[0:128]
    half_cols = cols[0:128]
    loads[0].wait()
    ids = perm[...]
    ids_row = ids.astype(F32)
    ids_col = jnp.sum(jnp.where(rows == cols, ids_row, 0.0), axis=1, keepdims=True)
    place = jnp.sum(jnp.where(ids_col < ids_row, 1.0, 0.0), axis=0, keepdims=True).astype(jnp.int32)
    local_row = (ids & 255).astype(F32)
    id_left = jnp.where((place >> 5) == rows[0:16], local_row, 0.0).astype(BF16)
    id_right = one_where((place & 31) == half_rows)
    ai_src[...] = dot_nt(id_left, id_right)[0:NY].reshape(NY, 1, 128)
    loads[1].wait()
    a_src[...] = dot(one_where(rows == place), events[0]).astype(BF16).reshape(NY, 32, 128)

    extra = jnp.where(at_start | at_end, 1, 0)
    pl.semaphore_wait(barrier, len(friends) + extra)
    scatter((ai_src, ai_dst, my_y, 1, "y"), (a_src, a_dst, my_y, 0, "y"))

    loads[2].wait()
    loads[3].wait()
    weights = []
    for s in range(10):
        row = slots[0, 0, s] - 2 * me
        col = (slots[0, 1, s] - 2 * me + 1 + 2 * ndom) % (2 * ndom)
        used = s < live[0, 0]
        weights.append(
            [
                [jnp.where(used & (row == r) & (col == c), 1.0, 0.0) for c in (1, 2, 0, 3)]
                for r in range(2)
            ]
        )
    for part in range(4):
        here = slice(part * 32, part * 32 + 32)
        sums = [[None] * 4 for _ in range(2)]
        for s in range(10):
            cell = counts[0, s, here, :].astype(F32)
            for r in range(2):
                for c in range(4):
                    term = cell * weights[s][r][c]
                    sums[r][c] = term if s == 0 else sums[r][c] + term
        diag = iota((32, 128), 0) + part * 32 == iota((32, 128), 1)
        for r in range(2):
            sums[r][r] = sums[r][r] + jnp.where(diag, loop_weight, 0.0)
            for c in range(4):
                adj_f[r * 128 + part * 32 : r * 128 + part * 32 + 32, c * 128 : c * 128 + 128] = sums[r][c]
    adj[...] = adj_f[...].astype(BF16)
    for r in range(2):
        for c in range(4):
            adj_t[c * 128 : c * 128 + 128, r * 128 : r * 128 + 128] = (
                adj_f[r * 128 : r * 128 + 128, c * 128 : c * 128 + 128].T.astype(BF16)
            )
    inverse = 1.0 / dot(adj[...], jnp.ones((512, 128), BF16))
    inv_deg[:, 0:128] = inverse
    inv_deg[:, 128:256] = inverse

    loads[4].wait()
    gs_two = (out_grad[0].astype(F32) * scale_loss * inv_deg[...]).astype(BF16)
    qa_src[...] = dot(adj_t[256:512], gs_two).astype(BF16).reshape(2, 128, 256)
    send(qa_src.at[0], qa_dst.at[1], 4, left)
    send(qa_src.at[1], qa_dst.at[0], 5, right)
    gz_ref[...] = dot(adj_t[0:256], gs_two)

    source = ((rows >> 1) & (NY - 1)) * 32 + (rows >> 4) * 2 + (rows & 1)
    mid[...] = one_where(cols == source)
    regroup[...] = one_where(half_rows == (half_cols >> 4) * 2 + (half_cols & 1))
    spread[...] = one_where(half_rows == (half_cols & 15))
    loads[5].wait()
    loads[6].wait()
    loads[7].wait()
    w_two_t[...] = w_two[...].T
    w_one_t[...] = w_one[...].T

    arrived(ai_dst, 1, NY - 1)
    ids_mid = dot(ai_dst[...].reshape(NY, 128).astype(BF16), regroup[...])
    ids_mid = jnp.sum(
        jnp.where(rows[0:NY] == ((cols[0:NY] >> 1) & (NY - 1)), ids_mid, 0.0), axis=0, keepdims=True
    )
    id_left = jnp.where((cols[0:NZ] >> 4) == rows[0:NZ], ids_mid, 0.0).astype(BF16)
    bi_src[1:17] = dot_nt(id_left, spread[...]).reshape(NZ, 1, 128)
    arrived(a_dst, 0, NY - 1)
    b_src[1:17] = dot(mid[...], a_dst[...].reshape(256, 128)).astype(BF16).reshape(NZ, 16, 128)
    for ref in (b_src, bi_src):
        ref[0] = ref[NZ]
        ref[NZ + 1] = ref[1]
    up = {"dom": ((my_y + 1) % NY) * NZ}
    down = {"dom": ((my_y + NY - 1) % NY) * NZ + NZ - 1}
    for src, dst, step in ((bi_src, edge_i, 23), (b_src, edge, 22)):
        send(src.at[NZ], dst.at[my_z], step, up)
        send(src.at[1], dst.at[my_z], step, down)
    for _, k, device in others("zc"):
        send(bi_src.at[pl.ds(k + k % 2, 2)], bi_dst.at[my_z], 3, device)
        send(b_src.at[pl.ds(k + k % 2, 2)], b_dst.at[my_z], 2, device)
    bi_dst[my_z] = bi_src[pl.ds(my_z + core, 2)]
    b_dst[my_z] = b_src[pl.ds(my_z + core, 2)]

    wait_for(qa_dst.at[1], recv_sem.at[4])
    wait_for(qa_dst.at[0], recv_sem.at[5])
    gz_two = (gz_ref[...] + qa_dst[...].astype(F32).reshape(256, 256)).astype(BF16)
    gh_ref[...] = dot(gz_two, w_two_t[...]) * inv_deg[...]

    def lane_ids(found):
        found = dot(found.astype(BF16), spread[...])
        return jnp.sum(jnp.where(rows[0:NZ] == (cols[0:NZ] >> 4), found, 0.0), axis=0, keepdims=True)

    low = core == 0
    arrived(bi_dst, 3, NZ - 1)
    first = bi_dst[:, 0].reshape(NZ, 128)
    second = bi_dst[:, 1].reshape(NZ, 128)
    far_ids[...] = jnp.where(low, first, second)
    finish[...] = one_where(rows.astype(F32) == lane_ids(jnp.where(low, second, first)))
    arrived(b_dst, 2, NZ - 1)
    first = b_dst[:, 0].reshape(256, 128)
    second = b_dst[:, 1].reshape(256, 128)
    far_rows[...] = jnp.where(low, first, second)
    ev_own = dot(finish[...], jnp.where(low, second, first)).astype(BF16)
    ev_win[0:256] = ev_own
    send(
        ev_win.at[pl.ds(128 * (1 - core), 128)], ev_win.at[pl.ds(256 + 128 * core, 128)], 6,
        other_core,
    )

    @pl.when(at_start | at_end)
    def _():
        arrived(edge_i, 23, NZ)
        far_ids[...] = edge_i[...].reshape(NZ, 128)
        arrived(edge, 22, NZ)
        far_rows[...] = edge[...].reshape(256, 128)

    far_place = one_where((half_rows + 128 * (1 - core)).astype(F32) == lane_ids(far_ids[...]))
    ev_win[pl.ds(256 + 128 * core, 128)] = dot(far_place, far_rows[...]).astype(BF16)

    def encoded(rows_in):
        pre_rows = dot(rows_in, w_enc[...])
        return pre_rows, (pre_rows * sigmoid(pre_rows)).astype(BF16)

    pre, h_zero = encoded(ev_own)
    z_own = dot(h_zero, w_one[...]).astype(BF16)
    total = dot(adj[:, 0:256], z_own)
    sig = sigmoid(pre)
    slope[0:256] = sig * (1.0 + pre * (1.0 - sig))
    h_win_t[:, 0:256] = h_zero.T
    ev_win_t[:, 0:256] = ev_own.T
    wait_for(ev_win.at[pl.ds(384 - 128 * core, 128)], recv_sem.at[6])
    ev_side = ev_win[256:512]
    pre, h_zero = encoded(ev_side)
    z_side = dot(h_zero, w_one[...]).astype(BF16)
    agg_one = (total + dot(adj[:, 256:512], z_side)) * inv_deg[...]
    h_win_t[:, 256:512] = h_zero.T
    ev_win_t[:, 256:512] = ev_side.T
    sig = sigmoid(pre)
    slope[256:512] = sig * (1.0 + pre * (1.0 - sig))

    def give(grad, half, half_there, step):
        half[...] = grad[1 - core].astype(BF16)
        send(half, half_there, step, other_core)

    def take(grad, half, total, step):
        wait_for(half, recv_sem.at[step])
        total[...] = (grad[core] + half[...].astype(F32)).astype(BF16)

    sig = sigmoid(agg_one)
    h_one = (agg_one * sig).astype(BF16)
    two_f[...] = dot(h_one.T, gz_two).reshape(2, NY, 16, 256)
    give(two_f, two_give, two_take, 11)
    gs_one = (gh_ref[...] * (sig * (1.0 + agg_one * (1.0 - sig)))).astype(BF16)
    gz_one = dot(adj_t[...], gs_one).astype(BF16)
    one_f[...] = dot(h_win_t[...], gz_one).reshape(2, NY, 16, 256)
    give(one_f, one_give, one_take, 10)
    take(two_f, two_take, two_src, 11)
    scatter((two_src, two_dst, my_y, 25, "y"))
    gh_zero = dot(gz_one, w_one_t[...]).astype(BF16)
    g_enc = (gh_zero.astype(F32) * slope[...]).astype(BF16)
    take(one_f, one_take, one_src, 10)
    scatter((one_src, one_dst, my_zc, 24, "z"))
    enc_src[...] = dot(ev_win_t[...], g_enc).astype(BF16).reshape(NY, 16, 256)
    scatter((enc_src, enc_dst, my_xc, 12, "xc"))
    z_two[0:256] = dot(h_one, w_two[...]).astype(BF16)

    def summed(ref):
        return jnp.sum(ref[...].astype(F32), axis=0).astype(BF16)

    arrived(enc_dst, 12, NY - 1)
    enc_y[my_y] = summed(enc_dst)
    spread_out(enc_y, my_y, 13, "y")
    arrived(one_dst, 24, NY - 1)
    one_mid[my_y] = summed(one_dst)
    spread_out(one_mid, my_y, 14, "y")
    arrived(two_dst, 25, NY - 1)
    two_mid[my_zc] = summed(two_dst)
    spread_out(two_mid, my_zc, 15, "z")
    send(z_two.at[pl.ds(0, 128)], z_two.at[pl.ds(384, 128)], 8, left)
    send(z_two.at[pl.ds(128, 128)], z_two.at[pl.ds(256, 128)], 9, right)
    arrived(enc_y, 13, NY - 1)
    enc_z[my_zc] = summed(enc_y)
    spread_out(enc_z, my_zc, 16, "z")
    arrived(one_mid, 14, NY - 1)
    one_x[rep] = jnp.sum(one_mid[...].astype(F32), axis=0)
    spread_out(one_x, rep, 17, "x")
    arrived(two_mid, 15, NY - 1)
    two_x[rep] = jnp.sum(two_mid[...].astype(F32), axis=0)
    spread_out(two_x, rep, 18, "x")
    wait_for(z_two.at[pl.ds(384, 128)], recv_sem.at[8])
    wait_for(z_two.at[pl.ds(256, 128)], recv_sem.at[9])
    embed[0] = (dot(adj[...], z_two[...]) * inv_deg[...]).astype(BF16)
    arrived(one_x, 17, NX - 1)
    one_mine = one_all.at[core]
    one_mine[my_zc] = jnp.sum(one_x[...], axis=0).astype(BF16)
    spread_out(one_mine, my_zc, 19, "z")
    arrived(two_x, 18, NX - 1)
    two_mine = two_all.at[core]
    two_mine[my_y] = jnp.sum(two_x[...], axis=0).astype(BF16)
    spread_out(two_mine, my_y, 20, "y")
    arrived(enc_z, 16, NY - 1)
    enc_all[my_xc] = summed(enc_z)
    spread_out(enc_all, my_xc, 21, "xc")
    arrived(one_mine, 19, NY - 1)
    send(one_mine, one_mine, 26, other_core)
    arrived(two_mine, 20, NY - 1)
    send(two_mine, two_mine, 27, other_core)
    arrived(enc_all, 21, NY - 1)
    wait_for(one_all.at[1 - core], recv_sem.at[26])
    wait_for(two_all.at[1 - core], recv_sem.at[27])

    for step, ref in ((0, a_src), (1, ai_src), (13, enc_y), (14, one_mid), (15, two_mid), (16, enc_z)):
        left_all(ref, step, NY - 1)
    for step, ref in ((2, b_dst), (3, bi_dst)):
        left_all(ref, step, NZ - 1)
    for step, ref in ((24, one_src), (25, two_src), (19, one_mine), (20, two_mine)):
        left_all(ref, step, NY - 1)
    for step, ref in ((10, one_give), (11, two_give), (26, one_mine), (27, two_mine)):
        left_all(ref, step, NY)
    for step, ref in ((12, enc_src), (21, enc_all)):
        left_all(ref, step, NY - 1)
    for step, ref in ((17, one_x), (18, two_x)):
        left_all(ref, step, NX - 1)
    for step, ref in ((4, qa_src), (5, qa_src)):
        left_all(ref, step, 1)
    left_all(b_src, 22, 2)
    left_all(bi_src, 23, 2)
    for step, ref in ((6, ev_win), (8, z_two), (9, z_two)):
        left_all(ref, step, 128)


def result_kernel(
    embed, enc_all, one_all, two_all, embed_out, grad_enc, grad_one, grad_two, enc, one, two, sem
):
    stores = [pltpu.make_async_copy(embed, embed_out, sem.at[0])]
    stores[0].start()
    for i, (src, wide, out) in enumerate(
        ((enc_all, enc, grad_enc), (one_all, one, grad_one), (two_all, two, grad_two))
    ):
        wide[...] = src[...].astype(F32).reshape(wide.shape)
        stores.append(pltpu.make_async_copy(wide, out, sem.at[i + 1]))
        stores[-1].start()
    for store in stores:
        store.wait()


def body(events, perm, w_enc, w_one, w_two, slot_blocks, live_count, block_counts, out_grad):
    scale_loss = 1.0 / math.sqrt(lax.axis_size("rep") * lax.axis_size("dom") * events.shape[1])
    vmem = pl.BlockSpec(memory_space=pltpu.VMEM)
    smem = pl.BlockSpec(memory_space=pltpu.SMEM)
    hbm = pl.BlockSpec(memory_space=pltpu.HBM)
    slot_rows = jnp.swapaxes(slot_blocks, 1, 2)
    args = [
        pltpu.with_memory_space_constraint(x, pltpu.HBM)
        for x in (events, perm, w_enc, w_one, w_two, slot_rows, block_counts, out_grad)
    ]

    def pieces(*shape, dtype=BF16):
        return pltpu.VMEM(shape, dtype)

    found = pl.pallas_call(
        functools.partial(step_kernel, scale_loss),
        out_shape=(
            jax.ShapeDtypeStruct((1, 256, 256), BF16),
            jax.ShapeDtypeStruct((NY, 16, 256), BF16),
            jax.ShapeDtypeStruct((2, NY, 16, 256), BF16),
            jax.ShapeDtypeStruct((2, NY, 16, 256), BF16),
        ),
        in_specs=[hbm] * 6 + [smem] + [hbm] * 2,
        out_specs=(vmem, vmem, vmem, vmem),
        scratch_shapes=[
            pieces(1, 256, 128),
            pieces(1, 256, dtype=jnp.int32),
            pieces(128, 256),
            pieces(256, 256),
            pieces(256, 256),
            pieces(1, 10, 128, 128, dtype=jnp.int32),
            pieces(1, 256, 256),
            pltpu.SMEM((1, 2, 10), jnp.int32),
            pieces(256, 512, dtype=F32),
            pieces(256, 512),
            pieces(512, 256),
            pieces(256, 256, dtype=F32),
            pieces(256, 256),
            pieces(128, 256),
            pieces(128, 256),
            pieces(256, 256),
            pieces(256, 256),
            pieces(256, 256),
            pieces(512, 128),
            pieces(512, 256),
            pieces(256, 256, dtype=F32),
            pieces(256, 256, dtype=F32),
            pieces(NY, 32, 128),
            pieces(NY, 32, 128),
            pieces(NY, 1, 128, dtype=F32),
            pieces(NY, 1, 128, dtype=F32),
            pieces(NZ + 2, 16, 128),
            pieces(NZ, 2, 16, 128),
            pieces(NZ + 2, 1, 128, dtype=F32),
            pieces(NZ, 2, 1, 128, dtype=F32),
            pieces(NZ, 16, 128),
            pieces(NZ, 1, 128, dtype=F32),
            pieces(256, 128),
            pieces(NZ, 128, dtype=F32),
            pieces(2, 128, 256),
            pieces(2, 128, 256),
            pieces(2, NY, 16, 256, dtype=F32),
            pieces(NY, 16, 256),
            pieces(NY, 16, 256),
            pieces(NY, 16, 256),
            pieces(NY, 16, 256),
            pieces(NY, 16, 256),
            pieces(NX, 16, 256, dtype=F32),
            pieces(2, NY, 16, 256, dtype=F32),
            pieces(NY, 16, 256),
            pieces(NY, 16, 256),
            pieces(NY, 16, 256),
            pieces(NY, 16, 256),
            pieces(NY, 16, 256),
            pieces(NX, 16, 256, dtype=F32),
            pieces(NY, 16, 256),
            pieces(NY, 16, 256),
            pieces(NY, 16, 256),
            pieces(NY, 16, 256),
            pieces(256, 512),
            pieces(128, 512),
            pieces(512, 256, dtype=F32),
            pltpu.SemaphoreType.DMA((8,)),
            pltpu.SemaphoreType.DMA((28,)),
            pltpu.SemaphoreType.DMA((28,)),
        ],
        compiler_params=pltpu.CompilerParams(
            collective_id=0, has_side_effects=True, vmem_limit_bytes=16 * 1024 * 1024
        ),
    )(*args[:6], live_count, *args[6:])
    return pl.pallas_call(
        result_kernel,
        out_shape=(
            jax.ShapeDtypeStruct((1, 256, 256), BF16),
            jax.ShapeDtypeStruct((128, 256), F32),
            jax.ShapeDtypeStruct((256, 256), F32),
            jax.ShapeDtypeStruct((256, 256), F32),
        ),
        in_specs=[vmem] * 4,
        out_specs=(pl.BlockSpec(memory_space=pl.ANY),) * 4,
        scratch_shapes=[
            pieces(128, 256, dtype=F32),
            pieces(256, 256, dtype=F32),
            pieces(256, 256, dtype=F32),
            pltpu.SemaphoreType.DMA((4,)),
        ],
        compiler_params=pltpu.CompilerParams(vmem_limit_bytes=8 * 1024 * 1024),
    )(*found)


def solution(mesh):
    return jax.shard_map(
        body,
        mesh=mesh,
        in_specs=(
            P("rep", "dom", None),
            P("rep", "dom"),
            P(),
            P(),
            P(),
            P("rep", "dom", None),
            P("rep", "dom"),
            P("rep", "dom", None, None),
            P("rep", "dom", None),
        ),
        out_specs=(P("rep", "dom", None), P(), P(), P()),
        check_vma=False,
    )
```

```python
import functools
import math

import jax
import jax.numpy as jnp
from jax import lax
from jax.experimental import pallas as pl
from jax.experimental.pallas import tpu as pltpu
from jax.sharding import PartitionSpec as P

loop_weight = 4.0
NY = 8
NZ = 16
NX = 4
F32 = jnp.float32
BF16 = jnp.bfloat16


def dot(a, b):
    return jnp.dot(a, b, preferred_element_type=F32)


def dot_nt(a, b):
    return lax.dot_general(a, b, (((1,), (1,)), ((), ())), preferred_element_type=F32)


def sigmoid(value):
    return 1.0 / (1.0 + jnp.exp(-value))


def wait_for(ref, sem):
    pltpu.make_async_copy(ref, ref, sem).wait()


def iota(shape, dim):
    return lax.broadcasted_iota(jnp.int32, shape, dim)


def one_where(mask):
    return jnp.where(mask, 1.0, 0.0).astype(BF16)


def step_kernel(
    scale_loss,
    events_in, perm_in, w_enc_in, w_one_in, w_two_in, slots_in, live, counts_in, out_grad_in,
    embed, enc_all, one_all, two_all,
    events, perm, w_enc, w_one, w_two, counts, out_grad, slots,
    adj_f, adj, adj_t, inv_deg, mid, regroup, spread, finish, w_one_t, w_two_t,
    ev_win, z_two, gz_ref, gh_ref,
    a_src, a_dst, ai_src, ai_dst, b_src, b_dst, bi_src, bi_dst, edge, edge_i, far_rows, far_ids, qa_src, qa_dst,
    two_src, two_dst, two_mid, two_x, one_src, one_dst, one_mid, one_x,
    enc_src, enc_dst, enc_y, enc_z, h_win_t, pre_win,
    load_sem, send_sem, recv_sem,
):
    me = lax.axis_index("dom")
    rep = lax.axis_index("rep")
    ndom = NY * NZ
    my_y = me // NZ
    my_z = me % NZ
    core = me % 2
    my_yc = my_y * 2 + core
    my_xc = rep * 2 + core
    my_zc = my_z // 2
    left = {"dom": (me + ndom - 1) % ndom}
    right = {"dom": (me + 1) % ndom}

    loads = [
        pltpu.make_async_copy(src, dst, load_sem.at[i])
        for i, (src, dst) in enumerate(
            (
                (perm_in, perm), (events_in, events), (slots_in, slots), (counts_in, counts),
                (out_grad_in, out_grad), (w_two_in, w_two), (w_enc_in, w_enc), (w_one_in, w_one),
            )
        )
    ]
    for load in loads[:2]:
        load.start()

    def others(group):
        ring = NX if group[0] == "x" else NY
        here = {"x": rep, "y": my_y, "z": my_zc}[group[0]]
        found = []
        for ahead in sorted(range(ring), key=lambda n: -min(n, ring - n)):
            chip = (here + ahead) % ring
            for flip in range(len(group)):
                if ahead or flip:
                    side = (core + flip) % 2
                    y = chip if group[0] == "y" else my_y
                    z = chip if group[0] == "z" else my_zc
                    x = chip if group[0] == "x" else rep
                    rank = chip * 2 + side if len(group) == 2 else chip
                    found.append((min(ahead, ring - ahead), rank, {"dom": y * NZ + z * 2 + side, "rep": x}))
        return found

    barrier = pltpu.get_barrier_semaphore()

    def hello(device):
        pl.semaphore_signal(barrier, inc=1, device_id=device, device_id_type=pl.DeviceIdType.MESH)

    friends = others("y") + others("zc") + [f for f in others("xc") if f[0]]
    friends.sort(key=lambda f: -f[0])
    for _, _, device in friends:
        hello(device)
    at_start = my_z == 0
    at_end = my_z == NZ - 1
    pl.when(at_start)(lambda: hello(left))
    pl.when(at_end)(lambda: hello(right))
    for load in loads[2:]:
        load.start()

    def send(src, dst, step, device):
        pltpu.make_async_remote_copy(
            src_ref=src, dst_ref=dst, send_sem=send_sem.at[step], recv_sem=recv_sem.at[step],
            device_id=device, device_id_type=pl.DeviceIdType.MESH,
        ).start()

    def scatter(*flows):
        starts = []
        for src, dst, mine, step, group in flows:
            starts += [(away, src.at[k], dst.at[mine], step, dev) for away, k, dev in others(group)]
        for _, src, dst, step, device in sorted(starts, key=lambda start: -start[0]):
            send(src, dst, step, device)
        for src, dst, mine, _, _ in flows:
            dst[mine] = src[mine]

    def spread_out(ref, mine, step, group):
        for _, _, device in others(group):
            send(ref.at[mine], ref.at[mine], step, device)

    def arrived(ref, step, count):
        wait_for(ref.at[pl.ds(0, count)], recv_sem.at[step])

    def left_all(ref, step, count):
        wait_for(ref.at[pl.ds(0, count)], send_sem.at[step])

    rows = iota((256, 256), 0)
    cols = iota((256, 256), 1)
    half_rows = rows[0:128]
    half_cols = cols[0:128]
    loads[0].wait()
    ids = perm[...]
    ids_row = ids.astype(F32)
    ids_col = jnp.sum(jnp.where(rows == cols, ids_row, 0.0), axis=1, keepdims=True)
    place = jnp.sum(jnp.where(ids_col < ids_row, 1.0, 0.0), axis=0, keepdims=True).astype(jnp.int32)
    local_row = (ids & 255).astype(F32)
    id_left = jnp.where((place >> 5) == rows[0:16], local_row, 0.0).astype(BF16)
    id_right = one_where((place & 31) == half_rows)
    ai_src[...] = dot_nt(id_left, id_right)[0:NY].reshape(NY, 1, 128)
    loads[1].wait()
    a_src[...] = dot(one_where(rows == place), events[0]).astype(BF16).reshape(NY, 32, 128)

    extra = jnp.where(at_start | at_end, 1, 0)
    pl.semaphore_wait(barrier, len(friends) + extra)
    scatter((ai_src, ai_dst, my_y, 1, "y"), (a_src, a_dst, my_y, 0, "y"))

    loads[2].wait()
    loads[3].wait()
    weights = []
    for s in range(10):
        row = slots[0, 0, s] - 2 * me
        col = (slots[0, 1, s] - 2 * me + 1 + 2 * ndom) % (2 * ndom)
        used = s < live[0, 0]
        weights.append(
            [
                [jnp.where(used & (row == r) & (col == c), 1.0, 0.0) for c in (1, 2, 0, 3)]
                for r in range(2)
            ]
        )
    for part in range(4):
        here = slice(part * 32, part * 32 + 32)
        sums = [[None] * 4 for _ in range(2)]
        for s in range(10):
            cell = counts[0, s, here, :].astype(F32)
            for r in range(2):
                for c in range(4):
                    term = cell * weights[s][r][c]
                    sums[r][c] = term if s == 0 else sums[r][c] + term
        diag = iota((32, 128), 0) + part * 32 == iota((32, 128), 1)
        for r in range(2):
            sums[r][r] = sums[r][r] + jnp.where(diag, loop_weight, 0.0)
            for c in range(4):
                adj_f[r * 128 + part * 32 : r * 128 + part * 32 + 32, c * 128 : c * 128 + 128] = sums[r][c]
    adj[...] = adj_f[...].astype(BF16)
    for r in range(2):
        for c in range(4):
            adj_t[c * 128 : c * 128 + 128, r * 128 : r * 128 + 128] = (
                adj_f[r * 128 : r * 128 + 128, c * 128 : c * 128 + 128].T.astype(BF16)
            )
    inverse = 1.0 / dot(adj[...], jnp.ones((512, 128), BF16))
    inv_deg[:, 0:128] = inverse
    inv_deg[:, 128:256] = inverse

    loads[4].wait()
    gs_two = (out_grad[0].astype(F32) * scale_loss * inv_deg[...]).astype(BF16)
    qa_src[...] = dot(adj_t[256:512], gs_two).astype(BF16).reshape(2, 128, 256)
    send(qa_src.at[0], qa_dst.at[1], 4, left)
    send(qa_src.at[1], qa_dst.at[0], 5, right)
    gz_ref[...] = dot(adj_t[0:256], gs_two)

    source = ((rows >> 1) & (NY - 1)) * 32 + (rows >> 4) * 2 + (rows & 1)
    mid[...] = one_where(cols == source)
    regroup[...] = one_where(half_rows == (half_cols >> 4) * 2 + (half_cols & 1))
    spread[...] = one_where(half_rows == (half_cols & 15))
    loads[5].wait()
    loads[6].wait()
    loads[7].wait()
    w_two_t[...] = w_two[...].T
    w_one_t[...] = w_one[...].T

    arrived(ai_dst, 1, NY - 1)
    ids_mid = dot(ai_dst[...].reshape(NY, 128).astype(BF16), regroup[...])
    ids_mid = jnp.sum(
        jnp.where(rows[0:NY] == ((cols[0:NY] >> 1) & (NY - 1)), ids_mid, 0.0), axis=0, keepdims=True
    )
    id_left = jnp.where((cols[0:NZ] >> 4) == rows[0:NZ], ids_mid, 0.0).astype(BF16)
    bi_src[1:17] = dot_nt(id_left, spread[...]).reshape(NZ, 1, 128)
    arrived(a_dst, 0, NY - 1)
    b_src[1:17] = dot(mid[...], a_dst[...].reshape(256, 128)).astype(BF16).reshape(NZ, 16, 128)
    for ref in (b_src, bi_src):
        ref[0] = ref[NZ]
        ref[NZ + 1] = ref[1]
    up = {"dom": ((my_y + 1) % NY) * NZ}
    down = {"dom": ((my_y + NY - 1) % NY) * NZ + NZ - 1}
    for src, dst, step in ((bi_src, edge_i, 23), (b_src, edge, 22)):
        send(src.at[NZ], dst.at[my_z], step, up)
        send(src.at[1], dst.at[my_z], step, down)
    for _, k, device in others("zc"):
        send(bi_src.at[pl.ds(k + k % 2, 2)], bi_dst.at[my_z], 3, device)
        send(b_src.at[pl.ds(k + k % 2, 2)], b_dst.at[my_z], 2, device)
    bi_dst[my_z] = bi_src[pl.ds(my_z + core, 2)]
    b_dst[my_z] = b_src[pl.ds(my_z + core, 2)]

    wait_for(qa_dst.at[1], recv_sem.at[4])
    wait_for(qa_dst.at[0], recv_sem.at[5])
    gz_two = (gz_ref[...] + qa_dst[...].astype(F32).reshape(256, 256)).astype(BF16)
    gh_ref[...] = dot(gz_two, w_two_t[...]) * inv_deg[...]

    def lane_ids(found):
        found = dot(found.astype(BF16), spread[...])
        return jnp.sum(jnp.where(rows[0:NZ] == (cols[0:NZ] >> 4), found, 0.0), axis=0, keepdims=True)

    low = core == 0
    arrived(bi_dst, 3, NZ - 1)
    first = bi_dst[:, 0].reshape(NZ, 128)
    second = bi_dst[:, 1].reshape(NZ, 128)
    far_ids[...] = jnp.where(low, first, second)
    finish[...] = one_where(rows.astype(F32) == lane_ids(jnp.where(low, second, first)))
    arrived(b_dst, 2, NZ - 1)
    first = b_dst[:, 0].reshape(256, 128)
    second = b_dst[:, 1].reshape(256, 128)
    far_rows[...] = jnp.where(low, first, second)
    ev_own = dot(finish[...], jnp.where(low, second, first)).astype(BF16)
    ev_win[0:256] = ev_own
    send(
        ev_win.at[pl.ds(128 * (1 - core), 128)], ev_win.at[pl.ds(256 + 128 * core, 128)], 6,
        {"dom": me + 1 - 2 * core},
    )

    @pl.when(at_start | at_end)
    def _():
        arrived(edge_i, 23, NZ)
        far_ids[...] = edge_i[...].reshape(NZ, 128)
        arrived(edge, 22, NZ)
        far_rows[...] = edge[...].reshape(256, 128)

    far_place = one_where((half_rows + 128 * (1 - core)).astype(F32) == lane_ids(far_ids[...]))
    ev_win[pl.ds(256 + 128 * core, 128)] = dot(far_place, far_rows[...]).astype(BF16)

    def encoded(rows_in):
        pre_rows = dot(rows_in, w_enc[...])
        return pre_rows, (pre_rows * sigmoid(pre_rows)).astype(BF16)

    pre, h_zero = encoded(ev_own)
    z_own = dot(h_zero, w_one[...]).astype(BF16)
    total = dot(adj[:, 0:256], z_own)
    pre_win[0:256] = pre
    h_win_t[:, 0:256] = h_zero.T
    wait_for(ev_win.at[pl.ds(384 - 128 * core, 128)], recv_sem.at[6])
    pre, h_zero = encoded(ev_win[256:512])
    z_side = dot(h_zero, w_one[...]).astype(BF16)
    agg_one = (total + dot(adj[:, 256:512], z_side)) * inv_deg[...]
    pre_win[256:512] = pre
    h_win_t[:, 256:512] = h_zero.T

    sig = sigmoid(agg_one)
    gs_one = (gh_ref[...] * (sig * (1.0 + agg_one * (1.0 - sig)))).astype(BF16)
    gz_one = dot(adj_t[...], gs_one).astype(BF16)
    one_src[...] = dot(h_win_t[...], gz_one).astype(BF16).reshape(NZ, 16, 256)
    h_one = (agg_one * sig).astype(BF16)
    two_src[...] = dot(h_one.T, gz_two).astype(BF16).reshape(NZ, 16, 256)
    scatter((one_src, one_dst, my_z, 10, "zc"), (two_src, two_dst, my_yc, 11, "yc"))
    gh_zero = dot(gz_one, w_one_t[...]).astype(BF16)
    pre = pre_win[...]
    sig = sigmoid(pre)
    g_enc = (gh_zero.astype(F32) * (sig * (1.0 + pre * (1.0 - sig)))).astype(BF16)
    enc_src[...] = dot(ev_win[...].T, g_enc).astype(BF16).reshape(NY, 16, 256)
    scatter((enc_src, enc_dst, my_xc, 12, "xc"))
    z_two[0:256] = dot(h_one, w_two[...]).astype(BF16)

    def summed(ref):
        return jnp.sum(ref[...].astype(F32), axis=0).astype(BF16)

    arrived(enc_dst, 12, NY - 1)
    enc_y[my_y] = summed(enc_dst)
    spread_out(enc_y, my_y, 13, "y")
    arrived(one_dst, 10, NZ - 1)
    one_mid[my_y] = summed(one_dst)
    spread_out(one_mid, my_y, 14, "y")
    arrived(two_dst, 11, NZ - 1)
    two_mid[my_zc] = summed(two_dst)
    spread_out(two_mid, my_zc, 15, "z")
    send(z_two.at[pl.ds(0, 128)], z_two.at[pl.ds(384, 128)], 8, left)
    send(z_two.at[pl.ds(128, 128)], z_two.at[pl.ds(256, 128)], 9, right)
    arrived(enc_y, 13, NY - 1)
    enc_z[my_zc] = summed(enc_y)
    spread_out(enc_z, my_zc, 16, "z")
    arrived(one_mid, 14, NY - 1)
    one_x[rep] = summed(one_mid)
    spread_out(one_x, rep, 17, "x")
    arrived(two_mid, 15, NY - 1)
    two_x[rep] = summed(two_mid)
    spread_out(two_x, rep, 18, "x")
    wait_for(z_two.at[pl.ds(384, 128)], recv_sem.at[8])
    wait_for(z_two.at[pl.ds(256, 128)], recv_sem.at[9])
    embed[0] = (dot(adj[...], z_two[...]) * inv_deg[...]).astype(BF16)
    arrived(one_x, 17, NX - 1)
    one_all[my_z] = summed(one_x)
    spread_out(one_all, my_z, 19, "zc")
    arrived(two_x, 18, NX - 1)
    two_all[my_yc] = summed(two_x)
    spread_out(two_all, my_yc, 20, "yc")
    arrived(enc_z, 16, NY - 1)
    enc_all[my_xc] = summed(enc_z)
    spread_out(enc_all, my_xc, 21, "xc")
    arrived(enc_all, 21, NY - 1)
    arrived(one_all, 19, NZ - 1)
    arrived(two_all, 20, NZ - 1)

    for step, ref in ((0, a_src), (1, ai_src), (13, enc_y), (14, one_mid), (15, two_mid), (16, enc_z)):
        left_all(ref, step, NY - 1)
    for step, ref in ((2, b_dst), (3, bi_dst), (10, one_src), (11, two_src), (19, one_all), (20, two_all)):
        left_all(ref, step, NZ - 1)
    for step, ref in ((12, enc_src), (21, enc_all)):
        left_all(ref, step, NY - 1)
    for step, ref in ((17, one_x), (18, two_x)):
        left_all(ref, step, NX - 1)
    for step, ref in ((4, qa_src), (5, qa_src)):
        left_all(ref, step, 1)
    left_all(b_src, 22, 2)
    left_all(bi_src, 23, 2)
    for step, ref in ((6, ev_win), (8, z_two), (9, z_two)):
        left_all(ref, step, 128)


def result_kernel(
    embed, enc_all, one_all, two_all, embed_out, grad_enc, grad_one, grad_two, enc, one, two, sem
):
    stores = [pltpu.make_async_copy(embed, embed_out, sem.at[0])]
    stores[0].start()
    for i, (src, wide, out) in enumerate(
        ((enc_all, enc, grad_enc), (one_all, one, grad_one), (two_all, two, grad_two))
    ):
        wide[...] = src[...].astype(F32).reshape(wide.shape)
        stores.append(pltpu.make_async_copy(wide, out, sem.at[i + 1]))
        stores[-1].start()
    for store in stores:
        store.wait()


def body(events, perm, w_enc, w_one, w_two, slot_blocks, live_count, block_counts, out_grad):
    scale_loss = 1.0 / math.sqrt(lax.axis_size("rep") * lax.axis_size("dom") * events.shape[1])
    vmem = pl.BlockSpec(memory_space=pltpu.VMEM)
    smem = pl.BlockSpec(memory_space=pltpu.SMEM)
    hbm = pl.BlockSpec(memory_space=pltpu.HBM)
    slot_rows = jnp.swapaxes(slot_blocks, 1, 2)
    args = [
        pltpu.with_memory_space_constraint(x, pltpu.HBM)
        for x in (events, perm, w_enc, w_one, w_two, slot_rows, block_counts, out_grad)
    ]

    def pieces(*shape, dtype=BF16):
        return pltpu.VMEM(shape, dtype)

    found = pl.pallas_call(
        functools.partial(step_kernel, scale_loss),
        out_shape=(
            jax.ShapeDtypeStruct((1, 256, 256), BF16),
            jax.ShapeDtypeStruct((NY, 16, 256), BF16),
            jax.ShapeDtypeStruct((NZ, 16, 256), BF16),
            jax.ShapeDtypeStruct((NZ, 16, 256), BF16),
        ),
        in_specs=[hbm] * 6 + [smem] + [hbm] * 2,
        out_specs=(vmem, vmem, vmem, vmem),
        scratch_shapes=[
            pieces(1, 256, 128),
            pieces(1, 256, dtype=jnp.int32),
            pieces(128, 256),
            pieces(256, 256),
            pieces(256, 256),
            pieces(1, 10, 128, 128, dtype=jnp.int32),
            pieces(1, 256, 256),
            pltpu.SMEM((1, 2, 10), jnp.int32),
            pieces(256, 512, dtype=F32),
            pieces(256, 512),
            pieces(512, 256),
            pieces(256, 256, dtype=F32),
            pieces(256, 256),
            pieces(128, 256),
            pieces(128, 256),
            pieces(256, 256),
            pieces(256, 256),
            pieces(256, 256),
            pieces(512, 128),
            pieces(512, 256),
            pieces(256, 256, dtype=F32),
            pieces(256, 256, dtype=F32),
            pieces(NY, 32, 128),
            pieces(NY, 32, 128),
            pieces(NY, 1, 128, dtype=F32),
            pieces(NY, 1, 128, dtype=F32),
            pieces(NZ + 2, 16, 128),
            pieces(NZ, 2, 16, 128),
            pieces(NZ + 2, 1, 128, dtype=F32),
            pieces(NZ, 2, 1, 128, dtype=F32),
            pieces(NZ, 16, 128),
            pieces(NZ, 1, 128, dtype=F32),
            pieces(256, 128),
            pieces(NZ, 128, dtype=F32),
            pieces(2, 128, 256),
            pieces(2, 128, 256),
            pieces(NZ, 16, 256),
            pieces(NZ, 16, 256),
            pieces(NY, 16, 256),
            pieces(NX, 16, 256),
            pieces(NZ, 16, 256),
            pieces(NZ, 16, 256),
            pieces(NY, 16, 256),
            pieces(NX, 16, 256),
            pieces(NY, 16, 256),
            pieces(NY, 16, 256),
            pieces(NY, 16, 256),
            pieces(NY, 16, 256),
            pieces(256, 512),
            pieces(512, 256, dtype=F32),
            pltpu.SemaphoreType.DMA((8,)),
            pltpu.SemaphoreType.DMA((24,)),
            pltpu.SemaphoreType.DMA((24,)),
        ],
        compiler_params=pltpu.CompilerParams(
            collective_id=0, has_side_effects=True, vmem_limit_bytes=16 * 1024 * 1024
        ),
    )(*args[:6], live_count, *args[6:])
    return pl.pallas_call(
        result_kernel,
        out_shape=(
            jax.ShapeDtypeStruct((1, 256, 256), BF16),
            jax.ShapeDtypeStruct((128, 256), F32),
            jax.ShapeDtypeStruct((256, 256), F32),
            jax.ShapeDtypeStruct((256, 256), F32),
        ),
        in_specs=[vmem] * 4,
        out_specs=(pl.BlockSpec(memory_space=pl.ANY),) * 4,
        scratch_shapes=[
            pieces(128, 256, dtype=F32),
            pieces(256, 256, dtype=F32),
            pieces(256, 256, dtype=F32),
            pltpu.SemaphoreType.DMA((4,)),
        ],
        compiler_params=pltpu.CompilerParams(vmem_limit_bytes=8 * 1024 * 1024),
    )(*found)


def solution(mesh):
    return jax.shard_map(
        body,
        mesh=mesh,
        in_specs=(
            P("rep", "dom", None),
            P("rep", "dom"),
            P(),
            P(),
            P(),
            P("rep", "dom", None),
            P("rep", "dom"),
            P("rep", "dom", None, None),
            P("rep", "dom", None),
        ),
        out_specs=(P("rep", "dom", None), P(), P(), P()),
        check_vma=False,
    )
```

```python
import functools
import math

import jax
import jax.numpy as jnp
from jax import lax
from jax.experimental import pallas as pl
from jax.experimental.pallas import tpu as pltpu
from jax.sharding import PartitionSpec as P

loop_weight = 4.0
NY = 8
NZ = 16
NX = 4
F32 = jnp.float32
BF16 = jnp.bfloat16


def dot(a, b):
    return jnp.dot(a, b, preferred_element_type=F32)


def dot_nt(a, b):
    return lax.dot_general(a, b, (((1,), (1,)), ((), ())), preferred_element_type=F32)


def sigmoid(value):
    return 1.0 / (1.0 + jnp.exp(-value))


def wait_for(ref, sem):
    pltpu.make_async_copy(ref, ref, sem).wait()


def iota(shape, dim):
    return lax.broadcasted_iota(jnp.int32, shape, dim)


def one_where(mask):
    return jnp.where(mask, 1.0, 0.0).astype(BF16)


def tile(k):
    return 16 * (k // 2), 128 * (k % 2)


def step_kernel(
    scale_loss,
    events_in, perm_in, w_enc_in, w_one_in, w_two_in, slots_in, live, counts_in, out_grad_in,
    embed, enc_all, one_all, two_all,
    events, perm, w_enc, w_one, w_two, counts, out_grad, slots,
    adj_f, adj, adj_t, inv_deg, mid, regroup, spread, finish, w_one_t, w_two_t,
    ev_win, z_two, gz_ref, gh_ref,
    a_src, a_dst, ai_src, ai_dst, b_src, b_dst, bi_src, bi_dst, edge, edge_i, far_rows, far_ids, qa_src, qa_dst,
    two_src, two_dst, two_mid, two_x, one_src, one_dst, one_ay, one_az, one_by, one_bz,
    enc_src, enc_dst, enc_mid, enc_x, h_win_t, ev_win_t, slope,
    load_sem, send_sem, recv_sem,
):
    me = lax.axis_index("dom")
    rep = lax.axis_index("rep")
    ndom = NY * NZ
    my_y = me // NZ
    my_z = me % NZ
    core = me % 2
    my_yc = my_y * 2 + core
    my_xc = rep * 2 + core
    my_zc = my_z // 2
    left = {"dom": (me + ndom - 1) % ndom}
    right = {"dom": (me + 1) % ndom}

    loads = [
        pltpu.make_async_copy(src, dst, load_sem.at[i])
        for i, (src, dst) in enumerate(
            (
                (perm_in, perm), (events_in, events), (slots_in, slots), (counts_in, counts),
                (out_grad_in, out_grad), (w_two_in, w_two), (w_enc_in, w_enc), (w_one_in, w_one),
            )
        )
    ]
    for load in loads[:2]:
        load.start()

    def others(group):
        ring = NX if group[0] == "x" else NY
        here = {"x": rep, "y": my_y, "z": my_zc}[group[0]]
        found = []
        for ahead in sorted(range(ring), key=lambda n: -min(n, ring - n)):
            chip = (here + ahead) % ring
            for flip in range(len(group)):
                if ahead or flip:
                    side = (core + flip) % 2
                    y = chip if group[0] == "y" else my_y
                    z = chip if group[0] == "z" else my_zc
                    x = chip if group[0] == "x" else rep
                    rank = chip * 2 + side if len(group) == 2 else chip
                    found.append((min(ahead, ring - ahead), rank, {"dom": y * NZ + z * 2 + side, "rep": x}))
        return found

    barrier = pltpu.get_barrier_semaphore()

    def hello(device):
        pl.semaphore_signal(barrier, inc=1, device_id=device, device_id_type=pl.DeviceIdType.MESH)

    friends = others("y") + others("zc") + [f for f in others("xc") if f[0]]
    friends.sort(key=lambda f: -f[0])
    for _, _, device in friends:
        hello(device)
    at_start = my_z == 0
    at_end = my_z == NZ - 1
    pl.when(at_start)(lambda: hello(left))
    pl.when(at_end)(lambda: hello(right))
    for load in loads[2:]:
        load.start()

    def send(src, dst, step, device):
        pltpu.make_async_remote_copy(
            src_ref=src, dst_ref=dst, send_sem=send_sem.at[step], recv_sem=recv_sem.at[step],
            device_id=device, device_id_type=pl.DeviceIdType.MESH,
        ).start()

    def scatter(*flows):
        starts = []
        for src, dst, mine, step, group in flows:
            starts += [(away, src.at[k], dst.at[mine], step, dev) for away, k, dev in others(group)]
        for _, src, dst, step, device in sorted(starts, key=lambda start: -start[0]):
            send(src, dst, step, device)
        for src, dst, mine, _, _ in flows:
            dst[mine] = src[mine]

    def spread_out(ref, mine, step, group):
        for _, _, device in others(group):
            send(ref.at[mine], ref.at[mine], step, device)

    def arrived(ref, step, count):
        wait_for(ref.at[pl.ds(0, count)], recv_sem.at[step])

    def left_all(ref, step, count):
        wait_for(ref.at[pl.ds(0, count)], send_sem.at[step])

    rows = iota((256, 256), 0)
    cols = iota((256, 256), 1)
    half_rows = rows[0:128]
    half_cols = cols[0:128]
    loads[0].wait()
    ids = perm[...]
    ids_row = ids.astype(F32)
    ids_col = jnp.sum(jnp.where(rows == cols, ids_row, 0.0), axis=1, keepdims=True)
    place = jnp.sum(jnp.where(ids_col < ids_row, 1.0, 0.0), axis=0, keepdims=True).astype(jnp.int32)
    local_row = (ids & 255).astype(F32)
    id_left = jnp.where((place >> 5) == rows[0:16], local_row, 0.0).astype(BF16)
    id_right = one_where((place & 31) == half_rows)
    ai_src[...] = dot_nt(id_left, id_right)[0:NY].reshape(NY, 1, 128)
    loads[1].wait()
    a_src[...] = dot(one_where(rows == place), events[0]).astype(BF16).reshape(NY, 32, 128)

    extra = jnp.where(at_start | at_end, 1, 0)
    pl.semaphore_wait(barrier, len(friends) + extra)
    scatter((ai_src, ai_dst, my_y, 1, "y"), (a_src, a_dst, my_y, 0, "y"))

    loads[2].wait()
    loads[3].wait()
    weights = []
    for s in range(10):
        row = slots[0, 0, s] - 2 * me
        col = (slots[0, 1, s] - 2 * me + 1 + 2 * ndom) % (2 * ndom)
        used = s < live[0, 0]
        weights.append(
            [
                [jnp.where(used & (row == r) & (col == c), 1.0, 0.0) for c in (1, 2, 0, 3)]
                for r in range(2)
            ]
        )
    for part in range(4):
        here = slice(part * 32, part * 32 + 32)
        sums = [[None] * 4 for _ in range(2)]
        for s in range(10):
            cell = counts[0, s, here, :].astype(F32)
            for r in range(2):
                for c in range(4):
                    term = cell * weights[s][r][c]
                    sums[r][c] = term if s == 0 else sums[r][c] + term
        diag = iota((32, 128), 0) + part * 32 == iota((32, 128), 1)
        for r in range(2):
            sums[r][r] = sums[r][r] + jnp.where(diag, loop_weight, 0.0)
            for c in range(4):
                adj_f[r * 128 + part * 32 : r * 128 + part * 32 + 32, c * 128 : c * 128 + 128] = sums[r][c]
    adj[...] = adj_f[...].astype(BF16)
    for r in range(2):
        for c in range(4):
            adj_t[c * 128 : c * 128 + 128, r * 128 : r * 128 + 128] = (
                adj_f[r * 128 : r * 128 + 128, c * 128 : c * 128 + 128].T.astype(BF16)
            )
    inverse = 1.0 / dot(adj[...], jnp.ones((512, 128), BF16))
    inv_deg[:, 0:128] = inverse
    inv_deg[:, 128:256] = inverse

    loads[4].wait()
    gs_two = (out_grad[0].astype(F32) * scale_loss * inv_deg[...]).astype(BF16)
    qa_src[...] = dot(adj_t[256:512], gs_two).astype(BF16).reshape(2, 128, 256)
    send(qa_src.at[0], qa_dst.at[1], 4, left)
    send(qa_src.at[1], qa_dst.at[0], 5, right)
    gz_ref[...] = dot(adj_t[0:256], gs_two)

    source = ((rows >> 1) & (NY - 1)) * 32 + (rows >> 4) * 2 + (rows & 1)
    mid[...] = one_where(cols == source)
    regroup[...] = one_where(half_rows == (half_cols >> 4) * 2 + (half_cols & 1))
    spread[...] = one_where(half_rows == (half_cols & 15))
    loads[5].wait()
    loads[6].wait()
    loads[7].wait()
    w_two_t[...] = w_two[...].T
    w_one_t[...] = w_one[...].T

    arrived(ai_dst, 1, NY - 1)
    ids_mid = dot(ai_dst[...].reshape(NY, 128).astype(BF16), regroup[...])
    ids_mid = jnp.sum(
        jnp.where(rows[0:NY] == ((cols[0:NY] >> 1) & (NY - 1)), ids_mid, 0.0), axis=0, keepdims=True
    )
    id_left = jnp.where((cols[0:NZ] >> 4) == rows[0:NZ], ids_mid, 0.0).astype(BF16)
    bi_src[1:17] = dot_nt(id_left, spread[...]).reshape(NZ, 1, 128)
    arrived(a_dst, 0, NY - 1)
    b_src[1:17] = dot(mid[...], a_dst[...].reshape(256, 128)).astype(BF16).reshape(NZ, 16, 128)
    for ref in (b_src, bi_src):
        ref[0] = ref[NZ]
        ref[NZ + 1] = ref[1]
    up = {"dom": ((my_y + 1) % NY) * NZ}
    down = {"dom": ((my_y + NY - 1) % NY) * NZ + NZ - 1}
    for src, dst, step in ((bi_src, edge_i, 23), (b_src, edge, 22)):
        send(src.at[NZ], dst.at[my_z], step, up)
        send(src.at[1], dst.at[my_z], step, down)
    for _, k, device in others("zc"):
        send(bi_src.at[pl.ds(k + k % 2, 2)], bi_dst.at[my_z], 3, device)
        send(b_src.at[pl.ds(k + k % 2, 2)], b_dst.at[my_z], 2, device)
    bi_dst[my_z] = bi_src[pl.ds(my_z + core, 2)]
    b_dst[my_z] = b_src[pl.ds(my_z + core, 2)]

    wait_for(qa_dst.at[1], recv_sem.at[4])
    wait_for(qa_dst.at[0], recv_sem.at[5])
    gz_two = (gz_ref[...] + qa_dst[...].astype(F32).reshape(256, 256)).astype(BF16)
    gh_ref[...] = dot(gz_two, w_two_t[...]) * inv_deg[...]

    def lane_ids(found):
        found = dot(found.astype(BF16), spread[...])
        return jnp.sum(jnp.where(rows[0:NZ] == (cols[0:NZ] >> 4), found, 0.0), axis=0, keepdims=True)

    low = core == 0
    arrived(bi_dst, 3, NZ - 1)
    first = bi_dst[:, 0].reshape(NZ, 128)
    second = bi_dst[:, 1].reshape(NZ, 128)
    far_ids[...] = jnp.where(low, first, second)
    finish[...] = one_where(rows.astype(F32) == lane_ids(jnp.where(low, second, first)))
    arrived(b_dst, 2, NZ - 1)
    first = b_dst[:, 0].reshape(256, 128)
    second = b_dst[:, 1].reshape(256, 128)
    far_rows[...] = jnp.where(low, first, second)
    ev_own = dot(finish[...], jnp.where(low, second, first)).astype(BF16)
    ev_win[0:256] = ev_own
    send(
        ev_win.at[pl.ds(128 * (1 - core), 128)], ev_win.at[pl.ds(256 + 128 * core, 128)], 6,
        {"dom": me + 1 - 2 * core},
    )

    @pl.when(at_start | at_end)
    def _():
        arrived(edge_i, 23, NZ)
        far_ids[...] = edge_i[...].reshape(NZ, 128)
        arrived(edge, 22, NZ)
        far_rows[...] = edge[...].reshape(256, 128)

    far_place = one_where((half_rows + 128 * (1 - core)).astype(F32) == lane_ids(far_ids[...]))
    ev_win[pl.ds(256 + 128 * core, 128)] = dot(far_place, far_rows[...]).astype(BF16)

    def encoded(rows_in):
        pre_rows = dot(rows_in, w_enc[...])
        return pre_rows, (pre_rows * sigmoid(pre_rows)).astype(BF16)

    pre, h_zero = encoded(ev_own)
    z_own = dot(h_zero, w_one[...]).astype(BF16)
    total = dot(adj[:, 0:256], z_own)
    sig = sigmoid(pre)
    slope[0:256] = sig * (1.0 + pre * (1.0 - sig))
    h_win_t[:, 0:256] = h_zero.T
    ev_win_t[:, 0:256] = ev_own.T
    wait_for(ev_win.at[pl.ds(384 - 128 * core, 128)], recv_sem.at[6])
    ev_side = ev_win[256:512]
    pre, h_zero = encoded(ev_side)
    z_side = dot(h_zero, w_one[...]).astype(BF16)
    agg_one = (total + dot(adj[:, 256:512], z_side)) * inv_deg[...]
    h_win_t[:, 256:512] = h_zero.T
    ev_win_t[:, 256:512] = ev_side.T
    sig = sigmoid(pre)
    slope[256:512] = sig * (1.0 + pre * (1.0 - sig))

    sig = sigmoid(agg_one)
    h_one = (agg_one * sig).astype(BF16)
    two_src[...] = dot(h_one.T, gz_two).astype(BF16).reshape(NZ, 16, 256)
    scatter((two_src, two_dst, my_yc, 11, "yc"))
    gs_one = (gh_ref[...] * (sig * (1.0 + agg_one * (1.0 - sig)))).astype(BF16)
    gz_one = dot(adj_t[...], gs_one).astype(BF16)
    one_src[...] = dot(h_win_t[...], gz_one).astype(BF16).reshape(NY, 32, 256)
    scatter((one_src, one_dst, my_xc, 10, "xc"))
    gh_zero = dot(gz_one, w_one_t[...]).astype(BF16)
    g_enc = (gh_zero.astype(F32) * slope[...]).astype(BF16)
    grad = dot(ev_win_t[...], g_enc).astype(BF16)
    for k in range(NZ):
        r, c = tile(k)
        enc_src[k] = grad[r : r + 16, c : c + 128]
    scatter((enc_src, enc_dst, my_z, 12, "zc"))
    z_two[0:256] = dot(h_one, w_two[...]).astype(BF16)

    def summed(ref):
        return jnp.sum(ref[...].astype(F32), axis=0).astype(BF16)

    arrived(one_dst, 10, NY - 1)
    total = summed(one_dst)
    one_ay[my_y] = total[0:16]
    one_bz[my_zc] = total[16:32]
    spread_out(one_ay, my_y, 14, "y")
    spread_out(one_bz, my_zc, 24, "z")
    arrived(two_dst, 11, NZ - 1)
    two_mid[my_zc] = summed(two_dst)
    spread_out(two_mid, my_zc, 15, "z")
    arrived(enc_dst, 12, NZ - 1)
    enc_mid[my_y] = summed(enc_dst)
    spread_out(enc_mid, my_y, 13, "y")
    send(z_two.at[pl.ds(0, 128)], z_two.at[pl.ds(384, 128)], 8, left)
    send(z_two.at[pl.ds(128, 128)], z_two.at[pl.ds(256, 128)], 9, right)
    arrived(one_ay, 14, NY - 1)
    one_az[my_zc] = summed(one_ay)
    spread_out(one_az, my_zc, 17, "z")
    arrived(one_bz, 24, NY - 1)
    one_by[my_y] = summed(one_bz)
    spread_out(one_by, my_y, 25, "y")
    arrived(two_mid, 15, NY - 1)
    two_x[rep] = summed(two_mid)
    spread_out(two_x, rep, 18, "x")
    arrived(enc_mid, 13, NY - 1)
    enc_x[rep] = summed(enc_mid)
    spread_out(enc_x, rep, 16, "x")
    wait_for(z_two.at[pl.ds(384, 128)], recv_sem.at[8])
    wait_for(z_two.at[pl.ds(256, 128)], recv_sem.at[9])
    embed[0] = (dot(adj[...], z_two[...]) * inv_deg[...]).astype(BF16)
    arrived(two_x, 18, NX - 1)
    two_all[my_yc] = summed(two_x)
    spread_out(two_all, my_yc, 20, "yc")
    arrived(enc_x, 16, NX - 1)
    enc_all[my_z] = summed(enc_x)
    spread_out(enc_all, my_z, 21, "zc")
    arrived(one_az, 17, NY - 1)
    arrived(one_by, 25, NY - 1)
    one_all[my_xc] = jnp.concatenate([summed(one_az), summed(one_by)], axis=0)
    spread_out(one_all, my_xc, 19, "xc")
    arrived(enc_all, 21, NZ - 1)
    arrived(one_all, 19, NY - 1)
    arrived(two_all, 20, NZ - 1)

    for step, ref in ((0, a_src), (1, ai_src), (13, enc_mid), (14, one_ay), (15, two_mid), (24, one_bz)):
        left_all(ref, step, NY - 1)
    for step, ref in ((10, one_src), (17, one_az), (25, one_by), (19, one_all)):
        left_all(ref, step, NY - 1)
    for step, ref in ((2, b_dst), (3, bi_dst), (12, enc_src), (11, two_src), (21, enc_all), (20, two_all)):
        left_all(ref, step, NZ - 1)
    for step, ref in ((16, enc_x), (18, two_x)):
        left_all(ref, step, NX - 1)
    for step, ref in ((4, qa_src), (5, qa_src)):
        left_all(ref, step, 1)
    left_all(b_src, 22, 2)
    left_all(bi_src, 23, 2)
    for step, ref in ((6, ev_win), (8, z_two), (9, z_two)):
        left_all(ref, step, 128)


def result_kernel(
    embed, enc_all, one_all, two_all, embed_out, grad_enc, grad_one, grad_two, enc, one, two, sem
):
    stores = [pltpu.make_async_copy(embed, embed_out, sem.at[0])]
    stores[0].start()
    for i, (src, wide, out) in enumerate(((one_all, one, grad_one), (two_all, two, grad_two))):
        wide[...] = src[...].astype(F32).reshape(wide.shape)
        stores.append(pltpu.make_async_copy(wide, out, sem.at[i + 1]))
        stores[-1].start()
    for k in range(NZ):
        r, c = tile(k)
        enc[r : r + 16, c : c + 128] = enc_all[k].astype(F32)
    stores.append(pltpu.make_async_copy(enc, grad_enc, sem.at[3]))
    stores[3].start()
    for store in stores:
        store.wait()


def body(events, perm, w_enc, w_one, w_two, slot_blocks, live_count, block_counts, out_grad):
    scale_loss = 1.0 / math.sqrt(lax.axis_size("rep") * lax.axis_size("dom") * events.shape[1])
    vmem = pl.BlockSpec(memory_space=pltpu.VMEM)
    smem = pl.BlockSpec(memory_space=pltpu.SMEM)
    hbm = pl.BlockSpec(memory_space=pltpu.HBM)
    slot_rows = jnp.swapaxes(slot_blocks, 1, 2)
    args = [
        pltpu.with_memory_space_constraint(x, pltpu.HBM)
        for x in (events, perm, w_enc, w_one, w_two, slot_rows, block_counts, out_grad)
    ]

    def pieces(*shape, dtype=BF16):
        return pltpu.VMEM(shape, dtype)

    found = pl.pallas_call(
        functools.partial(step_kernel, scale_loss),
        out_shape=(
            jax.ShapeDtypeStruct((1, 256, 256), BF16),
            jax.ShapeDtypeStruct((NZ, 16, 128), BF16),
            jax.ShapeDtypeStruct((NY, 32, 256), BF16),
            jax.ShapeDtypeStruct((NZ, 16, 256), BF16),
        ),
        in_specs=[hbm] * 6 + [smem] + [hbm] * 2,
        out_specs=(vmem, vmem, vmem, vmem),
        scratch_shapes=[
            pieces(1, 256, 128),
            pieces(1, 256, dtype=jnp.int32),
            pieces(128, 256),
            pieces(256, 256),
            pieces(256, 256),
            pieces(1, 10, 128, 128, dtype=jnp.int32),
            pieces(1, 256, 256),
            pltpu.SMEM((1, 2, 10), jnp.int32),
            pieces(256, 512, dtype=F32),
            pieces(256, 512),
            pieces(512, 256),
            pieces(256, 256, dtype=F32),
            pieces(256, 256),
            pieces(128, 256),
            pieces(128, 256),
            pieces(256, 256),
            pieces(256, 256),
            pieces(256, 256),
            pieces(512, 128),
            pieces(512, 256),
            pieces(256, 256, dtype=F32),
            pieces(256, 256, dtype=F32),
            pieces(NY, 32, 128),
            pieces(NY, 32, 128),
            pieces(NY, 1, 128, dtype=F32),
            pieces(NY, 1, 128, dtype=F32),
            pieces(NZ + 2, 16, 128),
            pieces(NZ, 2, 16, 128),
            pieces(NZ + 2, 1, 128, dtype=F32),
            pieces(NZ, 2, 1, 128, dtype=F32),
            pieces(NZ, 16, 128),
            pieces(NZ, 1, 128, dtype=F32),
            pieces(256, 128),
            pieces(NZ, 128, dtype=F32),
            pieces(2, 128, 256),
            pieces(2, 128, 256),
            pieces(NZ, 16, 256),
            pieces(NZ, 16, 256),
            pieces(NY, 16, 256),
            pieces(NX, 16, 256),
            pieces(NY, 32, 256),
            pieces(NY, 32, 256),
            pieces(NY, 16, 256),
            pieces(NY, 16, 256),
            pieces(NY, 16, 256),
            pieces(NY, 16, 256),
            pieces(NZ, 16, 128),
            pieces(NZ, 16, 128),
            pieces(NY, 16, 128),
            pieces(NX, 16, 128),
            pieces(256, 512),
            pieces(128, 512),
            pieces(512, 256, dtype=F32),
            pltpu.SemaphoreType.DMA((8,)),
            pltpu.SemaphoreType.DMA((26,)),
            pltpu.SemaphoreType.DMA((26,)),
        ],
        compiler_params=pltpu.CompilerParams(
            collective_id=0, has_side_effects=True, vmem_limit_bytes=16 * 1024 * 1024
        ),
    )(*args[:6], live_count, *args[6:])
    return pl.pallas_call(
        result_kernel,
        out_shape=(
            jax.ShapeDtypeStruct((1, 256, 256), BF16),
            jax.ShapeDtypeStruct((128, 256), F32),
            jax.ShapeDtypeStruct((256, 256), F32),
            jax.ShapeDtypeStruct((256, 256), F32),
        ),
        in_specs=[vmem] * 4,
        out_specs=(pl.BlockSpec(memory_space=pl.ANY),) * 4,
        scratch_shapes=[
            pieces(128, 256, dtype=F32),
            pieces(256, 256, dtype=F32),
            pieces(256, 256, dtype=F32),
            pltpu.SemaphoreType.DMA((4,)),
        ],
        compiler_params=pltpu.CompilerParams(vmem_limit_bytes=8 * 1024 * 1024),
    )(*found)


def solution(mesh):
    return jax.shard_map(
        body,
        mesh=mesh,
        in_specs=(
            P("rep", "dom", None),
            P("rep", "dom"),
            P(),
            P(),
            P(),
            P("rep", "dom", None),
            P("rep", "dom"),
            P("rep", "dom", None, None),
            P("rep", "dom", None),
        ),
        out_specs=(P("rep", "dom", None), P(), P(), P()),
        check_vma=False,
    )
```
